256 devices in a mesh: group: 2 (over z_hi), dp: 32 (over y, x, core), tensor: 4 (over z_lo).
Axes of the slice: x: 4, y: 4, z: 8 (z_hi: 2, z_lo: 4; z = z_hi * 4 + z_lo), core: 2. Of those that a mesh axis runs over, the one named last changes fastest.
Arguments:
- hidden: bfloat16 [14336, 4096], P('dp', ('group', 'tensor')), may hold values from -42 to 42
- cotangent: bfloat16 [14336, 4096], P('dp', ('group', 'tensor')), may hold values from -6 to 6
- query_weight: bfloat16 [4096, 2048], P(None, ('group', 'tensor')), may hold values from -0.09375 to 0.09375
- out_weight: bfloat16 [2048, 4096], P(('group', 'tensor')), may hold values from -0.125 to 0.125
- condition_weight: bfloat16 [4096, 1792], P(None, ('group', 'tensor')), may hold values from -0.09375 to 0.09375
- key_value_weight: bfloat16 [2, 896, 2048], P(None, None, ('group', 'tensor')), may hold values from -0.1875 to 0.1875
- encoder_query: bfloat16 [896, 896], replicated, may hold values from -0.1875 to 0.1875
- encoder_out: bfloat16 [896, 896], replicated, may hold values from -0.1875 to 0.1875
- database: bfloat16 [512, 128, 896], P('dp', ('group', 'tensor')), may hold values from -36 to 36
- neighbours: int32 [224, 2], P('dp'), may hold values from 0 to 15
- owners: int32 [224, 1], P('dp'), may hold values from 0 to 31; in each aligned block of 7 rows (0 to 6, 7 to 13, ...) no two rows name the same one
Outputs:
- branch_grad: bfloat16 [14336, 4096], P('dp', ('group', 'tensor'))
The draws below stay inside these ranges and needn't reach their ends.
Inputs may be any that keep to these rules, and one draw needn't show every extreme that they name: `owners`: within the 7 segments of one index of dp no owner is named more than 1 times, a bound that some block reaches.
All inputs are finite; a program needn't handle non-finite values.
Results may differ from the reference program's by a relative error of at most 0.025.
Values may be sent and summed in bfloat16 or wider, within the bound.
No kernel may reach another device: no remote copies, remote signals or barrier semaphores. Data moves between devices by JAX's collectives and lax.ppermute only.
A program may use at most 128 MiB of HBM per device.

```python
import math
import jax
import jax.numpy as jnp
import numpy as np
from jax import lax

D = 4096
HEADS = 16
HEAD = 128
DE = 896
EHEADS = 7
EHEAD = 128
SEG = 64
NLEN = 128
NEIGH = 2
SEG_DEV = 7
ENTRIES = 16
CAP = 1
TOKENS = 14336
SEGS = 224
STORE = 512
N_DP = 32


def draw_hidden(key, part):
    key = jax.random.fold_in(key, 11)
    row_key, col_key, base_key = jax.random.split(key, 3)
    row_scale = jnp.exp(jax.random.uniform(row_key, (TOKENS, 1), jnp.float32, math.log(0.5), math.log(5.0)))
    col_scale = jnp.exp(math.log(3.0) * jnp.arange(D, dtype=jnp.float32)[None, :] / D + jax.random.uniform(col_key, (1, D), jnp.float32, 0.0, math.log(3.5)))
    base = jnp.clip(jax.random.normal(base_key, (TOKENS, D), jnp.float32), -4.0, 4.0)
    return (0.2 * base * row_scale * col_scale).astype(jnp.bfloat16)


def draw_database(key, part):
    key = jax.random.fold_in(key, 23)
    row_key, col_key, base_key = jax.random.split(key, 3)
    row_scale = jnp.exp(jax.random.uniform(row_key, (STORE, NLEN, 1), jnp.float32, math.log(0.3), math.log(3.0)))
    col_scale = jnp.exp(jax.random.uniform(col_key, (1, 1, DE), jnp.float32, math.log(0.3), math.log(3.0)))
    base = jnp.clip(jax.random.normal(base_key, (STORE, NLEN, DE), jnp.float32), -4.0, 4.0)
    return (base * row_scale * col_scale).astype(jnp.bfloat16)


def with_ends(values, own_key, least, largest):
    longest = values.shape.index(max(values.shape))
    spots = []
    for shift in (0, 1):
        where = [jax.random.randint(jax.random.fold_in(own_key, axis), (), 0, length) for axis, length in enumerate(values.shape)]
        where[longest] = (where[longest] + shift) % values.shape[longest]
        spots.append(tuple(where))
    return values.at[spots[0]].set(least).at[spots[1]].set(largest)


def shard_levels(own_key, shape, cuts, smallest, top_value):
    def one(position, blocks):
        heights = jax.random.uniform(jax.random.fold_in(jax.random.fold_in(own_key, 6), position), (blocks,), jnp.float32, smallest / len(cuts), top_value / len(cuts))
        return jnp.repeat(jnp.exp(heights), shape[position] // blocks).reshape((-1,) + (1,) * (len(shape) - position - 1))

    gain = one(*cuts[0])
    for cut in cuts[1:]:
        gain = gain * one(*cut)
    return gain


def routed_block(key, own, number, rows, number_of, top, reach, lean):
    ranking = jax.random.permutation(key, number_of)
    crowded, usual = load_shares(number_of, rows * top, reach, lean, True), load_shares(number_of, rows * top, reach, lean, False)
    places = jnp.arange(number_of)

    def named(sizes, turn):
        used = int((sizes > 0).sum())
        fixed = max(1, used // 4)
        shifted = fixed + (places - fixed + turn * (used - fixed)) % max(1, number_of - fixed)
        return jnp.zeros((number_of,), jnp.int32).at[ranking[jnp.where(places < fixed, places, shifted)]].set(jnp.asarray(sizes, jnp.int32))

    sizes = jnp.where(number % 4 == 0, named(crowded, number // 4), named(usual, number - number // 4 - 1))
    mixed = jax.random.permutation(jax.random.fold_in(own, 3), number_of)
    giver, receiver = mixed[0:number_of // 2 * 2:2], mixed[1:number_of // 2 * 2:2]
    margin = jnp.minimum(sizes[giver] - 1, reach - sizes[receiver]) // 2
    margin = jnp.where((giver == ranking[0]) | (receiver == ranking[0]) | (sizes[receiver] == 0), 0, jnp.maximum(margin, 0))
    shifted = jax.random.randint(jax.random.fold_in(own, 4), (number_of // 2,), 0, 1 << 20) % (margin + 1)
    sizes = sizes.at[giver].add(-shifted).at[receiver].add(shifted)
    labels = jnp.searchsorted(jnp.cumsum(sizes), jnp.arange(rows * top), side="right").astype(jnp.int32)
    grid = labels.reshape(top, rows).T
    grid = grid[jax.random.permutation(jax.random.fold_in(own, 1), rows)]
    turn = jax.random.randint(jax.random.fold_in(own, 2), (rows, 1), 0, top)
    return jnp.take_along_axis(grid, (jnp.arange(top)[None, :] + turn) % top, axis=1)


def load_shares(count, total, bound, slope, full):
    portions = [(1 << 20) // math.isqrt(standing ** slope) + 1 for standing in range(1, count + 1)]
    largest = bound if full else min(bound, max(-(-total // count), total * portions[0] // sum(portions)))
    least = 1 if total - largest >= count - 1 else 0
    given, rest = [largest] + [least] * (count - 1), total - largest - least * (count - 1)
    while rest > 0:
        free = [i for i in range(1, count) if given[i] < largest] or [i for i in range(1, count) if given[i] < bound]
        pool, remaining = sum([portions[i] for i in free]), rest
        for i in free:
            addition = min(bound - given[i], max(1, remaining * portions[i] // pool), rest)
            given[i] = given[i] + addition
            rest = rest - addition
    return np.array(given)


def scatter_about(rng, extent, deviation, bound, shards=(), kind=jnp.bfloat16):
    array = jax.random.normal(rng, extent, jnp.float32) * deviation
    if len(shards) > 0:
        array = shard_levels(rng, extent, shards, -0.22, 0.18) * array
    return jnp.clip(array, min=-bound, max=bound).astype(kind)


def setup_inputs(seed: int = 0) -> dict:
    seeds = jax.random.split(jax.random.key(seed), 12)
    hidden = draw_hidden(jax.random.fold_in(seeds[11], 71), 0)
    cotangent = scatter_about(seeds[1], (TOKENS, D), 1.0, 6.0, ((0, 32), (1, 8)))
    query_weight = scatter_about(seeds[2], (D, HEADS * HEAD), D ** -0.5, 0.09375, ((1, 8),))
    out_weight = scatter_about(seeds[3], (HEADS * HEAD, D), (HEADS * HEAD) ** -0.5, 0.125, ((0, 8),))
    condition_weight = scatter_about(seeds[4], (D, 2 * DE), D ** -0.5, 0.09375, ((1, 8),))
    key_value_weight = scatter_about(seeds[5], (2, DE, HEADS * HEAD), DE ** -0.5, 0.1875, ((2, 8),))
    encoder_query = scatter_about(seeds[6], (DE, DE), DE ** -0.5, 0.1875)
    encoder_out = scatter_about(seeds[7], (DE, DE), DE ** -0.5, 0.1875)
    database = draw_database(jax.random.fold_in(seeds[11], 71), 0)
    neighbours = with_ends(jax.random.randint(seeds[9], (SEGS, NEIGH), 0, ENTRIES), jax.random.fold_in(seeds[9], 1), 0, ENTRIES - 1).astype(jnp.int32)
    owners_keys = jax.random.split(jax.random.fold_in(seeds[10], 1), SEGS // SEG_DEV)
    owners_turns = jax.random.permutation(jax.random.fold_in(seeds[10], 3), SEGS // SEG_DEV)
    owners = jax.vmap(lambda own, number: routed_block(jax.random.fold_in(seeds[10], 2), own, number, SEG_DEV, N_DP, 1, CAP, 2))(owners_keys, owners_turns).reshape((SEGS, 1))
    return dict(hidden=hidden, cotangent=cotangent, query_weight=query_weight, out_weight=out_weight, condition_weight=condition_weight, key_value_weight=key_value_weight, encoder_query=encoder_query, encoder_out=encoder_out, database=database, neighbours=neighbours, owners=owners)


epsilon = 1e-05

def encode(fetched, condition, encoder_query, encoder_out):
    rows_float = fetched.astype(jnp.float32)
    inverse = lax.rsqrt(lax.optimization_barrier(jnp.mean(rows_float * rows_float, axis=-1, keepdims=True)) + epsilon)
    enc_normed = (rows_float * inverse).astype(jnp.bfloat16)
    leading = fetched.shape[:-1]
    enc_queries = jnp.dot(enc_normed.reshape(-1, DE), encoder_query, preferred_element_type=jnp.float32).astype(jnp.bfloat16)
    enc_queries = enc_queries.reshape(leading + (EHEADS, EHEAD))
    seg_total = condition.shape[0]
    cond_keys = condition[:, :, :DE].reshape(seg_total, SEG, EHEADS, EHEAD)
    cond_values = condition[:, :, DE:].reshape(seg_total, SEG, EHEADS, EHEAD)
    scores = jnp.einsum('snreh,speh->snrep', enc_queries.astype(jnp.float32), cond_keys.astype(jnp.float32)) * EHEAD ** (-0.5)
    exponent = jnp.exp(scores)
    enc_weights = (exponent / lax.optimization_barrier(jnp.sum(exponent, axis=-1, keepdims=True))).astype(jnp.bfloat16)
    mixed = jnp.einsum('snrep,speh->snreh', enc_weights.astype(jnp.float32), cond_values.astype(jnp.float32)).astype(jnp.bfloat16)
    mixed = mixed.reshape(-1, DE)
    update = jnp.dot(mixed, encoder_out, preferred_element_type=jnp.float32).reshape(leading + (DE,))
    return (rows_float + update).astype(jnp.bfloat16)

def reference(hidden, cotangent, query_weight, out_weight, condition_weight, key_value_weight, encoder_query, encoder_out, database, neighbours, owners):
    hidden_float = hidden.astype(jnp.float32)
    inverse_rms = lax.rsqrt(lax.optimization_barrier(jnp.mean(hidden_float * hidden_float, axis=-1, keepdims=True)) + epsilon)
    normed = (hidden_float * inverse_rms).astype(jnp.bfloat16)
    queries = jnp.dot(normed, query_weight, preferred_element_type=jnp.float32).astype(jnp.bfloat16)
    queries = queries.reshape(SEGS, SEG, HEADS, HEAD)
    condition = jnp.dot(normed, condition_weight, preferred_element_type=jnp.float32).astype(jnp.bfloat16)
    condition = condition.reshape(SEGS, SEG, 2 * DE)
    entry_index = (owners[:, :1] * ENTRIES + neighbours).astype(jnp.int32)
    fetched = database[entry_index]
    encoded = encode(fetched, condition, encoder_query, encoder_out).reshape(SEGS * NEIGH * NLEN, DE)
    all_keys = jnp.dot(encoded, key_value_weight[0], preferred_element_type=jnp.float32).astype(jnp.bfloat16)
    all_keys = all_keys.reshape(SEGS, NEIGH * NLEN, HEADS, HEAD)
    all_values = jnp.dot(encoded, key_value_weight[1], preferred_element_type=jnp.float32).astype(jnp.bfloat16)
    all_values = all_values.reshape(SEGS, NEIGH * NLEN, HEADS, HEAD)
    scale = HEAD ** (-0.5)
    scores = jnp.einsum('cqah,ckah->caqk', queries.astype(jnp.float32), all_keys.astype(jnp.float32)) * scale
    exponent = jnp.exp(scores)
    prob_exact = exponent / lax.optimization_barrier(jnp.sum(exponent, axis=-1, keepdims=True))
    prob_bf = prob_exact.astype(jnp.bfloat16)
    attended = jnp.einsum('caqk,ckah->cqah', prob_bf.astype(jnp.float32), all_values.astype(jnp.float32)).astype(jnp.bfloat16)
    grad_attended = jnp.dot(cotangent, out_weight.T, preferred_element_type=jnp.float32).astype(jnp.bfloat16)
    grad_attended = grad_attended.reshape(SEGS, SEG, HEADS, HEAD)
    delta_rows = lax.optimization_barrier(jnp.sum(grad_attended.astype(jnp.float32) * attended.astype(jnp.float32), axis=-1))
    grad_probs = jnp.einsum('cqah,ckah->caqk', grad_attended.astype(jnp.float32), all_values.astype(jnp.float32))
    grad_scores = (prob_exact * (grad_probs - jnp.transpose(delta_rows, (0, 2, 1))[..., None]) * scale).astype(jnp.bfloat16)
    grad_query = jnp.einsum('caqk,ckah->cqah', grad_scores.astype(jnp.float32), all_keys.astype(jnp.float32)).astype(jnp.bfloat16)
    grad_query = grad_query.reshape(TOKENS, HEADS * HEAD)
    normed_grad = jnp.dot(grad_query, query_weight.T, preferred_element_type=jnp.float32)
    statistic = lax.optimization_barrier(jnp.mean(hidden_float * normed_grad, axis=-1, keepdims=True))
    return (inverse_rms * normed_grad - hidden_float * inverse_rms ** 3 * statistic).astype(jnp.bfloat16)
```

```python
import functools

import jax
import jax.numpy as jnp
from jax import lax
from jax.experimental import pallas as pl
from jax.experimental.pallas import tpu as pltpu
from jax.sharding import PartitionSpec as P

D = 4096
HEAD = 128
DE = 896
EHEADS = 7
SEG = 64
NLEN = 128
NEIGH = 2
KEYS = NLEN * NEIGH
NZ = 8
NDP = 32
SEGS = 7
FEAT = D // NZ
TOK = SEGS * SEG
HALF = 8 * HEAD
SCALE = HEAD**-0.5
epsilon = 1e-05
Z = ("group", "tensor")
BF = jnp.bfloat16
F32 = jnp.float32
PARAMS = pltpu.CompilerParams(vmem_limit_bytes=40 * 1024 * 1024)
VMEM = pl.BlockSpec(memory_space=pltpu.VMEM)
SMEM = pl.BlockSpec(memory_space=pltpu.SMEM)
ANY = pl.BlockSpec(memory_space=pl.ANY)
NT = (((1,), (1,)), ((), ()))


def dot(a, b):
    return jnp.dot(a, b, preferred_element_type=F32)


def dot_nt(a, b):
    return lax.dot_general(a, b, NT, preferred_element_type=F32)


def shift(x, by):
    return lax.ppermute(x, Z, [(i, (i + by) % NZ) for i in range(NZ)])


def ring(x):
    rows = x.shape[0] // 2
    chunks = [(x, 0)]
    right = left = x
    for step in range(1, 4):
        right, left = shift(right, 1), shift(left, -1)
        chunks += [(right, -step), (left, step)]
    far = jnp.concatenate([shift(right[:rows], 1), shift(left[rows:], -1)], axis=0)
    chunks.append((far, 4))
    return chunks


def exchange(x, axis):
    return lax.all_to_all(x, axis, split_axis=0, concat_axis=0, tiled=True)


def encoder_queries(fetched_ref, weight_ref, out_ref):
    rows = fetched_ref[...].astype(F32)
    inverse = lax.rsqrt(jnp.mean(rows * rows, axis=-1, keepdims=True) + epsilon)
    out_ref[...] = dot((rows * inverse).astype(BF), weight_ref[...]).astype(BF)


def forward(
    fetched_ref, enc_q_ref, cond_ref, q_ref, enc_out_ref, mixed_weights_ref,
    key_ref, value_ref, prob_ref, attended_ref,
    mixed_ref, encoded_ref, kv_ref, sem,
):
    copies = []
    for j in range(2):
        copies.append(
            pltpu.make_async_copy(
                mixed_weights_ref.at[:, j, pl.ds(0, 112), :], kv_ref.at[j], sem.at[j]
            )
        )
        copies[j].start()
    for h in range(EHEADS):
        columns = slice(h * HEAD, (h + 1) * HEAD)
        cond_key = cond_ref[:, columns]
        cond_value = cond_ref[:, DE + h * HEAD : DE + (h + 1) * HEAD]
        exponent = jnp.exp(dot_nt(enc_q_ref[:, columns], cond_key) * SCALE)
        weights = (exponent / jnp.sum(exponent, axis=-1, keepdims=True)).astype(BF)
        mixed_ref[:, columns] = dot(weights, cond_value).astype(BF)
    encoded_ref[...] = (
        fetched_ref[...].astype(F32) + dot(mixed_ref[...], enc_out_ref[...])
    ).astype(BF)
    for j in range(2):
        copies[j].wait()
    encoded = encoded_ref[...]
    for j in range(2):
        key_ref[j] = dot(encoded, kv_ref[j, 0:8].reshape(DE, HALF)).astype(BF)
        value_ref[j] = dot(encoded, kv_ref[j, 8:16].reshape(DE, HALF)).astype(BF)
        for z in range(NZ):
            columns = slice(z * HEAD, (z + 1) * HEAD)
            query = q_ref[z, :, j * HEAD : (j + 1) * HEAD]
            exponent = jnp.exp(dot_nt(query, key_ref[j, :, columns]) * SCALE)
            probs = exponent / jnp.sum(exponent, axis=-1, keepdims=True)
            prob_ref[j * NZ + z] = probs
            attended_ref[j * NZ + z] = dot(probs.astype(BF), value_ref[j, :, columns]).astype(BF)


def backward(grad_att_ref, q_ref, key_ref, value_ref, prob_ref, attended_ref, out_ref):
    total = jnp.zeros((SEG, HEAD), F32)
    for j in range(2):
        for z in range(NZ):
            columns = slice(z * HEAD, (z + 1) * HEAD)
            head = slice(j * HEAD, (j + 1) * HEAD)
            grad_att = grad_att_ref[z, :, head]
            delta = jnp.sum(
                grad_att.astype(F32) * attended_ref[j * NZ + z].astype(F32),
                axis=-1, keepdims=True,
            )
            grad_probs = dot_nt(grad_att, value_ref[j, :, columns])
            grad_scores = (prob_ref[j * NZ + z] * (grad_probs - delta) * SCALE).astype(BF)
            grad_query = dot(grad_scores, key_ref[j, :, columns]).astype(BF)
            out_ref[:, j * HALF + z * HEAD : j * HALF + (z + 1) * HEAD] = grad_query
            total = total + grad_query.astype(F32) * q_ref[z, :, head].astype(F32)
    stat = jnp.sum(total, axis=-1, keepdims=True) / D
    high = stat.astype(BF)
    low = (stat - high.astype(F32)).astype(BF)
    lane = lax.broadcasted_iota(jnp.int32, (SEG, HEAD), 1)
    out_ref[:, 2 * HALF :] = jnp.where(
        lane == 0, high.astype(F32), jnp.where(lane == 1, low.astype(F32), 0.0)
    ).astype(BF)


def finish(count, first, *refs):
    source_ref, refs = refs[0], refs[1:]
    chunk_refs, refs = refs[:count], refs[count:]
    hidden_ref, inverse_ref, weights_ref = refs[:3]
    refs = refs[3:]
    if not first:
        previous_ref, refs = refs[0], refs[1:]
    out_ref, weight_ref, sem = refs
    copies = []
    for j in range(2):
        copies.append(
            pltpu.make_async_copy(
                weights_ref.at[:, pl.ds(112 + 16 * j, 16), :], weight_ref.at[j], sem.at[j]
            )
        )
        copies[j].start()
    if not first:
        out_ref[...] = previous_ref[...]
    for j in range(2):
        copies[j].wait()
    for k in range(count):
        source = source_ref[k]

        @pl.when(source < SEGS)
        def _(k=k, source=source):
            rows = pl.ds(pl.multiple_of(source * SEG, SEG), SEG)
            grad = sum(
                dot_nt(
                    chunk_refs[k][:, j * HALF : (j + 1) * HALF],
                    weight_ref[j].reshape(FEAT, HALF),
                )
                for j in range(2)
            )
            tail = chunk_refs[k][:, 2 * HALF :].astype(F32)
            stat = tail[:, 0:1] + tail[:, 1:2]
            inverse = inverse_ref[rows, :]
            out_ref[rows, :] = (
                inverse * grad - hidden_ref[rows, :].astype(F32) * (inverse * inverse * stat)
            ).astype(BF)


def finish_call(chunks, sources, hidden, inverse, weights, previous):
    first = previous is None
    operands = [sources, *chunks, hidden, inverse, weights] + ([] if first else [previous])
    return pl.pallas_call(
        functools.partial(finish, len(chunks), first),
        out_shape=jax.ShapeDtypeStruct((TOK, FEAT), BF),
        in_specs=[SMEM] + [VMEM] * (len(chunks) + 2) + [ANY] + ([] if first else [VMEM]),
        out_specs=VMEM,
        scratch_shapes=[
            pltpu.VMEM((2, NDP, 16, HALF), BF),
            pltpu.SemaphoreType.DMA((2,)),
        ],
        compiler_params=PARAMS,
        name="finish",
    )(*operands)


def shards(
    hidden,
    cotangent,
    query_weight,
    out_weight,
    condition_weight,
    key_value_weight,
    encoder_query,
    encoder_out,
    database,
    neighbours,
    owners,
):
    me = lax.axis_index(Z)
    mine = lax.axis_index("dp")

    owner = owners[:, 0]
    selector = owner[None, :] == jnp.arange(NDP, dtype=jnp.int32)[:, None]
    wanted = jnp.sum(selector.astype(jnp.int32)[:, :, None] * neighbours[None, :, :], axis=1)
    asked = exchange(wanted, "dp")
    returned = exchange(database[asked].reshape(NDP, NEIGH * NLEN // NZ, DE), "dp")
    fetched = exchange(returned[jnp.concatenate([owner, owner[:1]])], Z).reshape(KEYS, DE)

    kv_part = lax.dynamic_slice(
        key_value_weight.reshape(2 * DE, 2 * HEAD),
        (mine // 2 * 112, mine % 2 * HEAD),
        (112, HEAD),
    )
    q_part = lax.dynamic_slice(
        query_weight.reshape(NZ, FEAT, 2 * HEAD), (0, mine * 16, 0), (NZ, 16, 2 * HEAD)
    )
    q_part = q_part.reshape(NZ, 16, 2, HEAD).transpose(0, 2, 1, 3).reshape(NZ, 32, HEAD)
    part = jnp.concatenate([jnp.broadcast_to(kv_part, (NZ, 112, HEAD)), q_part], axis=1)
    part = exchange(part, Z).transpose(1, 0, 2).reshape(144, HALF)
    weights = lax.all_gather(part, "dp", axis=0, tiled=False)

    def rows_of(weight, offset):
        return lax.dynamic_slice_in_dim(weight, (me + offset) % NZ * FEAT, FEAT, 0)

    queries = condition = squares = 0.0
    for chunk, offset in ring(hidden):
        queries = queries + dot(chunk, rows_of(query_weight, offset))
        condition = condition + dot(chunk, rows_of(condition_weight, offset))
        squares = squares + jnp.sum(jnp.square(chunk.astype(F32)), axis=-1, keepdims=True)
    inverse = lax.rsqrt(squares / D + epsilon)
    sent = jnp.concatenate([queries * inverse, condition * inverse], axis=1).astype(BF)
    sent = jnp.pad(sent, ((0, SEG), (0, 32))).reshape(NZ, SEG, 512)
    got = exchange(sent, Z)
    cond = got[:, :, 256:480].transpose(1, 0, 2).reshape(SEG, 2 * DE)

    grad_attended = 0.0
    for chunk, offset in ring(cotangent):
        columns = lax.dynamic_slice_in_dim(out_weight, (me + offset) % NZ * FEAT, FEAT, 1)
        grad_attended = grad_attended + dot_nt(chunk, columns)
    grad_attended = jnp.pad(grad_attended.astype(BF), ((0, SEG), (0, 0)))
    got_grad = exchange(grad_attended.reshape(NZ, SEG, 2 * HEAD), Z)

    enc_q = pl.pallas_call(
        encoder_queries,
        out_shape=jax.ShapeDtypeStruct((KEYS, DE), BF),
        in_specs=[VMEM, VMEM],
        out_specs=VMEM,
        compiler_params=PARAMS,
        name="encoder_queries",
    )(fetched, encoder_query)
    keys, values, probs, attended = pl.pallas_call(
        forward,
        out_shape=(
            jax.ShapeDtypeStruct((2, KEYS, HALF), BF),
            jax.ShapeDtypeStruct((2, KEYS, HALF), BF),
            jax.ShapeDtypeStruct((2 * NZ, SEG, KEYS), F32),
            jax.ShapeDtypeStruct((2 * NZ, SEG, HEAD), BF),
        ),
        in_specs=[VMEM] * 5 + [ANY],
        out_specs=(VMEM,) * 4,
        scratch_shapes=[
            pltpu.VMEM((KEYS, DE), BF),
            pltpu.VMEM((KEYS, DE), BF),
            pltpu.VMEM((2, 16, 112, HALF), BF),
            pltpu.SemaphoreType.DMA((2,)),
        ],
        compiler_params=PARAMS,
        name="forward",
    )(fetched, enc_q, cond, got, encoder_out, weights.reshape(16, 2, 144, HALF))
    grad_query = pl.pallas_call(
        backward,
        out_shape=jax.ShapeDtypeStruct((SEG, 2 * HALF + HEAD), BF),
        in_specs=[VMEM] * 6,
        out_specs=VMEM,
        compiler_params=PARAMS,
        name="backward",
    )(got_grad, got, keys, values, probs, attended)

    chunks = ring(grad_query)
    sources = [(me + offset) % NZ for _, offset in chunks]
    early = finish_call(
        [c for c, _ in chunks[:7]], jnp.stack(sources[:7]), hidden, inverse, weights, None
    )
    return finish_call([chunks[7][0]], jnp.stack(sources[7:]), hidden, inverse, weights, early)


def solution(mesh):
    return jax.shard_map(
        shards,
        mesh=mesh,
        in_specs=(
            P("dp", Z),
            P("dp", Z),
            P(None, Z),
            P(Z, None),
            P(None, Z),
            P(None, None, Z),
            P(),
            P(),
            P("dp", Z, None),
            P("dp", None),
            P("dp", None),
        ),
        out_specs=P("dp", Z),
        check_vma=False,
    )
```

```python
import functools

import jax
import jax.numpy as jnp
from jax import lax
from jax.experimental import pallas as pl
from jax.experimental.pallas import tpu as pltpu
from jax.sharding import PartitionSpec as P

D = 4096
HEAD = 128
DE = 896
EHEADS = 7
SEG = 64
NLEN = 128
NEIGH = 2
KEYS = NLEN * NEIGH
NZ = 8
NDP = 32
SEGS = 7
FEAT = D // NZ
TOK = SEGS * SEG
HALF = 8 * HEAD
SCALE = HEAD**-0.5
epsilon = 1e-05
Z = ("group", "tensor")
BF = jnp.bfloat16
F32 = jnp.float32
PARAMS = pltpu.CompilerParams(vmem_limit_bytes=40 * 1024 * 1024)
VMEM = pl.BlockSpec(memory_space=pltpu.VMEM)
SMEM = pl.BlockSpec(memory_space=pltpu.SMEM)
ANY = pl.BlockSpec(memory_space=pl.ANY)
NT = (((1,), (1,)), ((), ()))


def dot(a, b):
    return jnp.dot(a, b, preferred_element_type=F32)


def dot_nt(a, b):
    return lax.dot_general(a, b, NT, preferred_element_type=F32)


def shift(x, by):
    return lax.ppermute(x, Z, [(i, (i + by) % NZ) for i in range(NZ)])


def tie(*arrays):
    return lax.optimization_barrier(arrays)


def ring(x):
    rows = x.shape[0] // 2
    chunks = [(x, 0)]
    right = left = x
    for step in range(1, 4):
        right, left = shift(right, 1), shift(left, -1)
        chunks += [(right, -step), (left, step)]
    far = (shift(right[:rows], 1), shift(left[rows:], -1))
    return chunks, far


def exchange(x, axis):
    return lax.all_to_all(x, axis, split_axis=0, concat_axis=0, tiled=True)


def start(pairs, sem):
    copies = [pltpu.make_async_copy(a, b, sem.at[i]) for i, (a, b) in enumerate(pairs)]
    for copy in copies:
        copy.start()
    return copies


def wait(copies):
    for copy in copies:
        copy.wait()


def like(x):
    return pltpu.VMEM(x.shape, x.dtype)


def encoder_queries(fetched_hbm, weight_hbm, out_ref, fetched_ref, weight_ref, sem):
    copies = start([(fetched_hbm, fetched_ref), (weight_hbm, weight_ref)], sem)
    copies[0].wait()
    rows = fetched_ref[...].astype(F32)
    inverse = lax.rsqrt(jnp.mean(rows * rows, axis=-1, keepdims=True) + epsilon)
    normed = (rows * inverse).astype(BF)
    copies[1].wait()
    out_ref[...] = dot(normed, weight_ref[...]).astype(BF)


def forward(
    fetched_hbm, enc_q_hbm, cond_hbm, q_hbm, enc_out_hbm, weights_hbm,
    key_hbm, value_hbm, prob_hbm, attended_hbm,
    fetched_ref, enc_q_ref, cond_ref, q_ref, enc_out_ref, kv_ref,
    key_ref, value_ref, prob_ref, attended_ref, mixed_ref, in_sem, out_sem,
):
    small = start(
        [
            (enc_q_hbm, enc_q_ref), (cond_hbm, cond_ref), (fetched_hbm, fetched_ref),
            (enc_out_hbm, enc_out_ref), (q_hbm, q_ref),
        ], in_sem,
    )
    large = [
        pltpu.make_async_copy(
            weights_hbm.at[:, j, pl.ds(0, 112), :], kv_ref.at[j], in_sem.at[5 + j]
        )
        for j in range(2)
    ]
    for copy in large:
        copy.start()
    wait(small)
    for h in range(EHEADS):
        columns = slice(h * HEAD, (h + 1) * HEAD)
        cond_key = cond_ref[:, columns]
        cond_value = cond_ref[:, DE + h * HEAD : DE + (h + 1) * HEAD]
        exponent = jnp.exp(dot_nt(enc_q_ref[:, columns], cond_key) * SCALE)
        weights = (exponent / jnp.sum(exponent, axis=-1, keepdims=True)).astype(BF)
        mixed_ref[:, columns] = dot(weights, cond_value).astype(BF)
    encoded = (fetched_ref[...].astype(F32) + dot(mixed_ref[...], enc_out_ref[...])).astype(BF)
    outs = []
    for j in range(2):
        large[j].wait()
        key_ref[j] = dot(encoded, kv_ref[j, 0:8].reshape(DE, HALF)).astype(BF)
        value_ref[j] = dot(encoded, kv_ref[j, 8:16].reshape(DE, HALF)).astype(BF)
        outs += [
            pltpu.make_async_copy(key_ref.at[j], key_hbm.at[j], out_sem.at[4 * j]),
            pltpu.make_async_copy(value_ref.at[j], value_hbm.at[j], out_sem.at[4 * j + 1]),
        ]
        outs[-2].start()
        outs[-1].start()
        for z in range(NZ):
            columns = slice(z * HEAD, (z + 1) * HEAD)
            query = q_ref[z, :, j * HEAD : (j + 1) * HEAD]
            exponent = jnp.exp(dot_nt(query, key_ref[j, :, columns]) * SCALE)
            probs = exponent / jnp.sum(exponent, axis=-1, keepdims=True)
            prob_ref[j, z] = probs
            attended_ref[j, z] = dot(probs.astype(BF), value_ref[j, :, columns]).astype(BF)
        outs += [
            pltpu.make_async_copy(prob_ref.at[j], prob_hbm.at[j], out_sem.at[4 * j + 2]),
            pltpu.make_async_copy(attended_ref.at[j], attended_hbm.at[j], out_sem.at[4 * j + 3]),
        ]
        outs[-2].start()
        outs[-1].start()
    wait(outs)


def backward(
    grad_hbm, q_hbm, key_hbm, value_hbm, prob_hbm, attended_hbm, out_ref,
    grad_ref, q_ref, key_ref, value_ref, prob_ref, attended_ref, sem,
):
    copies = start(
        [
            (grad_hbm, grad_ref), (q_hbm, q_ref), (value_hbm, value_ref),
            (attended_hbm, attended_ref), (prob_hbm, prob_ref), (key_hbm, key_ref),
        ], sem,
    )
    wait(copies)
    total = jnp.zeros((SEG, HEAD), F32)
    for j in range(2):
        for z in range(NZ):
            columns = slice(z * HEAD, (z + 1) * HEAD)
            head = slice(j * HEAD, (j + 1) * HEAD)
            grad_att = grad_ref[z, :, head]
            delta = jnp.sum(
                grad_att.astype(F32) * attended_ref[j, z].astype(F32), axis=-1, keepdims=True
            )
            grad_probs = dot_nt(grad_att, value_ref[j, :, columns])
            grad_scores = (prob_ref[j, z] * (grad_probs - delta) * SCALE).astype(BF)
            grad_query = dot(grad_scores, key_ref[j, :, columns]).astype(BF)
            out_ref[:, j * HALF + z * HEAD : j * HALF + (z + 1) * HEAD] = grad_query
            total = total + grad_query.astype(F32) * q_ref[z, :, head].astype(F32)
    stat = jnp.sum(total, axis=-1, keepdims=True) / D
    high = stat.astype(BF)
    low = (stat - high.astype(F32)).astype(BF)
    lane = lax.broadcasted_iota(jnp.int32, (SEG, HEAD), 1)
    out_ref[:, 2 * HALF :] = jnp.where(
        lane == 0, high.astype(F32), jnp.where(lane == 1, low.astype(F32), 0.0)
    ).astype(BF)


def finish(starts, first, *refs):
    count = len(starts)
    source_ref, refs = refs[0], refs[1:]
    chunks_hbm, refs = refs[:count], refs[count:]
    hidden_hbm, inverse_hbm, weights_hbm = refs[:3]
    refs = refs[3 if first else 4 :]
    out_hbm, refs = refs[0], refs[1:]
    chunk_refs, refs = refs[:count], refs[count:]
    hidden_refs, refs = refs[:count], refs[count:]
    out_refs, refs = refs[:count], refs[count:]
    inverse_ref, weight_ref, sem, out_sem = refs
    places = []
    for k in range(count):
        source = source_ref[k]
        rows = chunk_refs[k].shape[0]
        at = jnp.where(source < SEGS, source, 0) * SEG + starts[k]
        places.append((source < SEGS, pl.ds(pl.multiple_of(at, 32), rows)))
    loads = [(inverse_hbm, inverse_ref)]
    loads += [
        (weights_hbm.at[:, pl.ds(112 + 16 * j, 16), :], weight_ref.at[j]) for j in range(2)
    ]
    for k in range(count):
        loads.append((chunks_hbm[k], chunk_refs[k]))
        loads.append((hidden_hbm.at[places[k][1]], hidden_refs[k]))
    wait(start(loads, sem))
    for k in range(count):
        grad = sum(
            dot_nt(
                chunk_refs[k][:, j * HALF : (j + 1) * HALF],
                weight_ref[j].reshape(FEAT, HALF),
            )
            for j in range(2)
        )
        tail = chunk_refs[k][:, 2 * HALF :].astype(F32)
        stat = tail[:, 0:1] + tail[:, 1:2]
        inverse = inverse_ref[places[k][1], :]
        out_refs[k][...] = (
            inverse * grad - hidden_refs[k][...].astype(F32) * (inverse * inverse * stat)
        ).astype(BF)

        @pl.when(places[k][0])
        def _(k=k):
            copy = pltpu.make_async_copy(
                out_refs[k], out_hbm.at[places[k][1]], out_sem.at[k]
            )
            copy.start()
            copy.wait()


def finish_call(chunks, starts, sources, hidden, inverse, weights, previous):
    first = previous is None
    operands = [sources, *chunks, hidden, inverse, weights] + ([] if first else [previous])
    rows = [c.shape[0] for c in chunks]
    return pl.pallas_call(
        functools.partial(finish, starts, first),
        out_shape=jax.ShapeDtypeStruct((TOK, FEAT), BF),
        in_specs=[SMEM] + [ANY] * (len(operands) - 1),
        out_specs=ANY,
        scratch_shapes=[like(c) for c in chunks]
        + [pltpu.VMEM((r, FEAT), BF) for r in rows] * 2
        + [
            like(inverse),
            pltpu.VMEM((2, NDP, 16, HALF), BF),
            pltpu.SemaphoreType.DMA((3 + 2 * len(chunks),)),
            pltpu.SemaphoreType.DMA((len(chunks),)),
        ],
        input_output_aliases={} if first else {len(operands) - 1: 0},
        compiler_params=PARAMS,
        name="finish",
    )(*operands)


def shards(
    hidden,
    cotangent,
    query_weight,
    out_weight,
    condition_weight,
    key_value_weight,
    encoder_query,
    encoder_out,
    database,
    neighbours,
    owners,
):
    me = lax.axis_index(Z)
    mine = lax.axis_index("dp")

    owner = owners[:, 0]
    selector = owner[None, :] == jnp.arange(NDP, dtype=jnp.int32)[:, None]
    wanted = jnp.sum(selector.astype(jnp.int32)[:, :, None] * neighbours[None, :, :], axis=1)
    asked = exchange(wanted, "dp")

    kv_part = lax.dynamic_slice(
        key_value_weight.reshape(2 * DE, 2 * HEAD),
        (mine // 2 * 112, mine % 2 * HEAD),
        (112, HEAD),
    )
    q_part = lax.dynamic_slice(
        query_weight.reshape(NZ, FEAT, 2 * HEAD), (0, mine * 16, 0), (NZ, 16, 2 * HEAD)
    )
    q_part = q_part.reshape(NZ, 16, 2, HEAD).transpose(0, 2, 1, 3).reshape(NZ, 32, HEAD)
    part = jnp.concatenate([jnp.broadcast_to(kv_part, (NZ, 112, HEAD)), q_part], axis=1)
    part = exchange(part, Z)

    right = left = hidden
    grad_right = grad_left = cotangent
    chunks, grad_chunks = [(hidden, 0)], [(cotangent, 0)]
    half = TOK // 2
    for step in range(1, 5):
        last = step == 4
        new_right = shift(right[:half] if last else right, 1)
        new_left = shift(left[half:] if last else left, -1)
        if step == 1:
            part, asked, new_right, new_left = tie(part, asked, new_right, new_left)
        new_grad_right = shift(grad_right[:half] if last else grad_right, 1)
        new_grad_left = shift(grad_left[half:] if last else grad_left, -1)
        chunks += [(new_right, -step), (new_left, step)]
        grad_chunks += [(new_grad_right, -step), (new_grad_left, step)]
        right, left, grad_right, grad_left = new_right, new_left, new_grad_right, new_grad_left
        if step < 4:
            grad_right, grad_left, _, _ = tie(grad_right, grad_left, right, left)
        if 1 < step < 4:
            right, left, _, _ = tie(right, left, held[0], held[1])
        held = (new_grad_right, new_grad_left)

    returned = exchange(database[asked].reshape(NDP, NEIGH * NLEN // NZ, DE), "dp")
    fetched = exchange(returned[jnp.concatenate([owner, owner[:1]])], Z).reshape(KEYS, DE)
    part = part.transpose(1, 0, 2).reshape(144, HALF)
    weights = lax.all_gather(part, "dp", axis=0, tiled=False)

    def whole(chunks):
        return chunks[:7] + [
            (jnp.concatenate([chunks[7][0], chunks[8][0]], axis=0), 4)
        ]

    def rows_of(weight, offset):
        return lax.dynamic_slice_in_dim(weight, (me + offset) % NZ * FEAT, FEAT, 0)

    queries = condition = squares = 0.0
    for chunk, offset in whole(chunks):
        queries = queries + dot(chunk, rows_of(query_weight, offset))
        condition = condition + dot(chunk, rows_of(condition_weight, offset))
        squares = squares + jnp.sum(jnp.square(chunk.astype(F32)), axis=-1, keepdims=True)
    inverse = lax.rsqrt(squares / D + epsilon)
    sent = jnp.concatenate([queries * inverse, condition * inverse], axis=1).astype(BF)
    sent = jnp.pad(sent, ((0, SEG), (0, 32))).reshape(NZ, SEG, 512)
    got = exchange(sent, Z)
    cond = got[:, :, 256:480].transpose(1, 0, 2).reshape(SEG, 2 * DE)

    grad_attended = 0.0
    for chunk, offset in whole(grad_chunks):
        columns = lax.dynamic_slice_in_dim(out_weight, (me + offset) % NZ * FEAT, FEAT, 1)
        grad_attended = grad_attended + dot_nt(chunk, columns)
    grad_attended = jnp.pad(grad_attended.astype(BF), ((0, SEG), (0, 0)))
    got_grad = exchange(grad_attended.reshape(NZ, SEG, 2 * HEAD), Z)

    enc_q = pl.pallas_call(
        encoder_queries,
        out_shape=jax.ShapeDtypeStruct((KEYS, DE), BF),
        in_specs=[ANY, ANY],
        out_specs=VMEM,
        scratch_shapes=[like(fetched), like(encoder_query), pltpu.SemaphoreType.DMA((2,))],
        compiler_params=PARAMS,
        name="encoder_queries",
    )(fetched, encoder_query)
    results = (
        jax.ShapeDtypeStruct((2, KEYS, HALF), BF),
        jax.ShapeDtypeStruct((2, KEYS, HALF), BF),
        jax.ShapeDtypeStruct((2, NZ, SEG, KEYS), F32),
        jax.ShapeDtypeStruct((2, NZ, SEG, HEAD), BF),
    )
    operands = (fetched, enc_q, cond, got, encoder_out)
    attention = pl.pallas_call(
        forward,
        out_shape=results,
        in_specs=[ANY] * 6,
        out_specs=(ANY,) * 4,
        scratch_shapes=[like(x) for x in operands]
        + [pltpu.VMEM((2, 16, 112, HALF), BF)]
        + [like(x) for x in results]
        + [
            pltpu.VMEM((KEYS, DE), BF),
            pltpu.SemaphoreType.DMA((7,)),
            pltpu.SemaphoreType.DMA((8,)),
        ],
        compiler_params=PARAMS,
        name="forward",
    )(*operands, weights.reshape(16, 2, 144, HALF))
    operands = (got_grad, got, *attention)
    grad_query = pl.pallas_call(
        backward,
        out_shape=jax.ShapeDtypeStruct((SEG, 2 * HALF + HEAD), BF),
        in_specs=[ANY] * 6,
        out_specs=VMEM,
        scratch_shapes=[like(x) for x in operands] + [pltpu.SemaphoreType.DMA((6,))],
        compiler_params=PARAMS,
        name="backward",
    )(*operands)

    chunks, far = ring(grad_query)
    out = None
    for group in (chunks[:1], chunks[1:3], chunks[3:5], chunks[5:7], [(far[0], 4), (far[1], 4)]):
        sources = jnp.stack([(me + offset) % NZ for _, offset in group])
        group = [c for c, _ in group]
        starts = (0, SEG // 2) if group[0].shape[0] < SEG else (0,) * len(group)
        out = finish_call(group, starts, sources, hidden, inverse, weights, out)
    return out


def solution(mesh):
    return jax.shard_map(
        shards,
        mesh=mesh,
        in_specs=(
            P("dp", Z),
            P("dp", Z),
            P(None, Z),
            P(Z, None),
            P(None, Z),
            P(None, None, Z),
            P(),
            P(),
            P("dp", Z, None),
            P("dp", None),
            P("dp", None),
        ),
        out_specs=P("dp", Z),
        check_vma=False,
    )
```

```python
import functools

import jax
import jax.numpy as jnp
from jax import lax
from jax.experimental import pallas as pl
from jax.experimental.pallas import tpu as pltpu
from jax.sharding import PartitionSpec as P

D = 4096
HEAD = 128
DE = 896
EHEADS = 7
SEG = 64
NLEN = 128
NEIGH = 2
KEYS = NLEN * NEIGH
NZ = 8
NDP = 32
SEGS = 7
FEAT = D // NZ
TOK = SEGS * SEG
HALF = 8 * HEAD
SCALE = HEAD**-0.5
epsilon = 1e-05
Z = ("group", "tensor")
BF = jnp.bfloat16
F32 = jnp.float32
PARAMS = pltpu.CompilerParams(vmem_limit_bytes=40 * 1024 * 1024)
VMEM = pl.BlockSpec(memory_space=pltpu.VMEM)
SMEM = pl.BlockSpec(memory_space=pltpu.SMEM)
ANY = pl.BlockSpec(memory_space=pl.ANY)
NT = (((1,), (1,)), ((), ()))


def dot(a, b):
    return jnp.dot(a, b, preferred_element_type=F32)


def dot_nt(a, b):
    return lax.dot_general(a, b, NT, preferred_element_type=F32)


def shift(x, by):
    return lax.ppermute(x, Z, [(i, (i + by) % NZ) for i in range(NZ)])


def tie(*arrays):
    return lax.optimization_barrier(arrays)


def ring(x):
    rows = x.shape[0] // 2
    chunks = [(x, 0)]
    right = left = x
    for step in range(1, 4):
        right, left = shift(right, 1), shift(left, -1)
        chunks += [(right, -step), (left, step)]
    far = (shift(right[:rows], 1), shift(left[rows:], -1))
    return chunks, far


def exchange(x, axis):
    return lax.all_to_all(x, axis, split_axis=0, concat_axis=0, tiled=True)


def start(pairs, sem):
    copies = [pltpu.make_async_copy(a, b, sem.at[i]) for i, (a, b) in enumerate(pairs)]
    for copy in copies:
        copy.start()
    return copies


def wait(copies):
    for copy in copies:
        copy.wait()


def cost(flops, size):
    return pl.CostEstimate(flops=flops, bytes_accessed=size, transcendentals=0)


def like(x):
    return pltpu.VMEM(x.shape, x.dtype)


def encoder_queries(fetched_hbm, weight_hbm, out_ref, fetched_ref, weight_ref, sem):
    copies = start([(fetched_hbm, fetched_ref), (weight_hbm, weight_ref)], sem)
    copies[0].wait()
    rows = fetched_ref[...].astype(F32)
    inverse = lax.rsqrt(jnp.mean(rows * rows, axis=-1, keepdims=True) + epsilon)
    normed = (rows * inverse).astype(BF)
    copies[1].wait()
    out_ref[...] = dot(normed, weight_ref[...]).astype(BF)


def project(count, index_ref, *refs):
    chunks_hbm, refs = refs[:count], refs[count:]
    query_hbm, cond_hbm, out_hbm, acc_ref, squares_ref = refs[:5]
    chunk_ref, query_ref, cond_ref, out_weight_ref, sem = refs[5:]
    copies = []
    for k in range(count):
        at = pl.ds(pl.multiple_of(index_ref[k] * FEAT, FEAT), FEAT)
        copies.append(
            start(
                [
                    (chunks_hbm[k], chunk_ref.at[k]), (query_hbm.at[at], query_ref.at[k]),
                    (cond_hbm.at[at], cond_ref.at[k]), (out_hbm.at[:, at], out_weight_ref.at[k]),
                ], sem.at[k],
            )
        )
    for k in range(count):
        wait(copies[k])
        chunk = chunk_ref[k, :TOK]
        squares = jnp.sum(jnp.square(chunk.astype(F32)), axis=-1, keepdims=True)
        parts = (
            dot(chunk, query_ref[k]),
            dot_nt(chunk_ref[k, TOK:], out_weight_ref[k]),
            dot(chunk, cond_ref[k]),
        )
        for columns, part in zip((slice(0, 256), slice(256, 512), slice(512, 736)), parts):
            acc_ref[:, columns] = part if k == 0 else acc_ref[:, columns] + part
        squares_ref[...] = squares if k == 0 else squares_ref[...] + squares


def project_last(
    index_ref, hidden_hbm, cot_hbm, acc_hbm, squares_hbm, query_hbm, cond_hbm, out_hbm,
    sent_ref, inverse_ref,
    hidden_ref, cot_ref, acc_ref, squares_ref, query_ref, cond_ref, out_weight_ref, sem,
):
    at = pl.ds(pl.multiple_of(index_ref[0] * FEAT, FEAT), FEAT)
    copies = start(
        [
            (hidden_hbm, hidden_ref), (squares_hbm, squares_ref), (acc_hbm, acc_ref),
            (query_hbm.at[at], query_ref), (cond_hbm.at[at], cond_ref),
            (cot_hbm, cot_ref), (out_hbm.at[:, at], out_weight_ref),
        ], sem,
    )
    wait(copies)
    chunk = hidden_ref[...]
    squares = squares_ref[...] + jnp.sum(
        jnp.square(chunk.astype(F32)), axis=-1, keepdims=True
    )
    inverse = lax.rsqrt(squares / D + epsilon)
    inverse_ref[...] = inverse
    queries = (acc_ref[:, :256] + dot(chunk, query_ref[...])) * inverse
    grads = acc_ref[:, 256:512] + dot_nt(cot_ref[...], out_weight_ref[...])
    condition = (acc_ref[:, 512:736] + dot(chunk, cond_ref[...])) * inverse
    for columns, part in (
        (slice(0, 256), queries), (slice(256, 512), grads), (slice(512, 736), condition)
    ):
        sent_ref[:SEGS, :, columns] = part.astype(BF).reshape(SEGS, SEG, -1)
    sent_ref[:, :, 736:] = jnp.zeros((NZ, SEG, 32), BF)
    sent_ref[SEGS, :, :736] = jnp.zeros((SEG, 736), BF)


def attention(
    fetched_hbm, enc_q_hbm, got_hbm, enc_out_hbm, weights_hbm, out_ref,
    fetched_ref, enc_q_ref, got_ref, enc_out_ref, kv_ref, key_ref, value_ref, mixed_ref, sem,
):
    small = start(
        [
            (got_hbm, got_ref), (enc_q_hbm, enc_q_ref),
            (fetched_hbm, fetched_ref), (enc_out_hbm, enc_out_ref),
        ], sem,
    )
    large = [
        pltpu.make_async_copy(
            weights_hbm.at[:, j, pl.ds(0, 112), :], kv_ref.at[j], sem.at[4 + j]
        )
        for j in range(2)
    ]
    for copy in large:
        copy.start()
    wait(small)
    cond_keys, cond_values = (
        jnp.concatenate([got_ref[z, :, 512:736] for z in range(n, n + 4)], axis=1)
        for n in (0, 4)
    )
    for h in range(EHEADS):
        columns = slice(h * HEAD, (h + 1) * HEAD)
        exponent = jnp.exp(dot_nt(enc_q_ref[:, columns], cond_keys[:, columns]) * SCALE)
        weights = (exponent / jnp.sum(exponent, axis=-1, keepdims=True)).astype(BF)
        mixed_ref[:, columns] = dot(weights, cond_values[:, columns]).astype(BF)
    encoded = (fetched_ref[...].astype(F32) + dot(mixed_ref[...], enc_out_ref[...])).astype(BF)
    total = jnp.zeros((SEG, HEAD), F32)
    for j in range(2):
        large[j].wait()
        key_ref[j] = dot(encoded, kv_ref[j, 0:8].reshape(DE, HALF)).astype(BF)
        value_ref[j] = dot(encoded, kv_ref[j, 8:16].reshape(DE, HALF)).astype(BF)
        for z in range(NZ):
            columns = slice(z * HEAD, (z + 1) * HEAD)
            query = got_ref[z, :, j * HEAD : (j + 1) * HEAD]
            grad_att = got_ref[z, :, (2 + j) * HEAD : (3 + j) * HEAD]
            key, value = key_ref[j, :, columns], value_ref[j, :, columns]
            exponent = jnp.exp(dot_nt(query, key) * SCALE)
            probs = exponent / jnp.sum(exponent, axis=-1, keepdims=True)
            attended = dot(probs.astype(BF), value).astype(BF)
            delta = jnp.sum(
                grad_att.astype(F32) * attended.astype(F32), axis=-1, keepdims=True
            )
            grad_probs = dot_nt(grad_att, value)
            grad_scores = (probs * (grad_probs - delta) * SCALE).astype(BF)
            grad_query = dot(grad_scores, key).astype(BF)
            out_ref[:, j * HALF + z * HEAD : j * HALF + (z + 1) * HEAD] = grad_query
            total = total + grad_query.astype(F32) * query.astype(F32)
    stat = jnp.sum(total, axis=-1, keepdims=True) / D
    high = stat.astype(BF)
    low = (stat - high.astype(F32)).astype(BF)
    lane = lax.broadcasted_iota(jnp.int32, (SEG, HEAD), 1)
    out_ref[:, 2 * HALF :] = jnp.where(
        lane == 0, high.astype(F32), jnp.where(lane == 1, low.astype(F32), 0.0)
    ).astype(BF)


def finish(starts, first, *refs):
    count = len(starts)
    source_ref, refs = refs[0], refs[1:]
    chunks_hbm, refs = refs[:count], refs[count:]
    hidden_hbm, inverse_hbm, weights_hbm = refs[:3]
    refs = refs[3 if first else 4 :]
    out_hbm, refs = refs[0], refs[1:]
    chunk_refs, refs = refs[:count], refs[count:]
    hidden_refs, refs = refs[:count], refs[count:]
    out_refs, refs = refs[:count], refs[count:]
    inverse_ref, weight_ref, sem, out_sem = refs
    places = []
    for k in range(count):
        source = source_ref[k]
        rows = chunk_refs[k].shape[0]
        at = jnp.where(source < SEGS, source, 0) * SEG + starts[k]
        places.append((source < SEGS, pl.ds(pl.multiple_of(at, 32), rows)))
    loads = [(inverse_hbm, inverse_ref)]
    loads += [
        (weights_hbm.at[:, pl.ds(112 + 16 * j, 16), :], weight_ref.at[j]) for j in range(2)
    ]
    for k in range(count):
        loads.append((chunks_hbm[k], chunk_refs[k]))
        loads.append((hidden_hbm.at[places[k][1]], hidden_refs[k]))
    wait(start(loads, sem))
    rows = [c.shape[0] for c in chunk_refs]
    chunks = jnp.concatenate([c[...] for c in chunk_refs], axis=0)
    grads = sum(
        dot_nt(chunks[:, j * HALF : (j + 1) * HALF], weight_ref[j].reshape(FEAT, HALF))
        for j in range(2)
    )
    for k in range(count):
        grad = grads[sum(rows[:k]) : sum(rows[: k + 1])]
        tail = chunk_refs[k][:, 2 * HALF :].astype(F32)
        stat = tail[:, 0:1] + tail[:, 1:2]
        inverse = inverse_ref[places[k][1], :]
        out_refs[k][...] = (
            inverse * grad - hidden_refs[k][...].astype(F32) * (inverse * inverse * stat)
        ).astype(BF)

        @pl.when(places[k][0])
        def _(k=k):
            pltpu.make_async_copy(
                out_refs[k], out_hbm.at[places[k][1]], out_sem.at[k]
            ).start()

    for k in range(count):

        @pl.when(places[k][0])
        def _(k=k):
            pltpu.make_async_copy(
                out_refs[k], out_hbm.at[places[k][1]], out_sem.at[k]
            ).wait()


def finish_call(chunks, starts, sources, hidden, inverse, weights, previous):
    first = previous is None
    operands = [sources, *chunks, hidden, inverse, weights] + ([] if first else [previous])
    rows = [c.shape[0] for c in chunks]
    return pl.pallas_call(
        functools.partial(finish, starts, first),
        out_shape=jax.ShapeDtypeStruct((TOK, FEAT), BF),
        in_specs=[SMEM] + [ANY] * (len(operands) - 1),
        out_specs=ANY,
        scratch_shapes=[like(c) for c in chunks]
        + [pltpu.VMEM((r, FEAT), BF) for r in rows] * 2
        + [
            like(inverse),
            pltpu.VMEM((2, NDP, 16, HALF), BF),
            pltpu.SemaphoreType.DMA((3 + 2 * len(chunks),)),
            pltpu.SemaphoreType.DMA((len(chunks),)),
        ],
        input_output_aliases={} if first else {len(operands) - 1: 0},
        compiler_params=PARAMS,
        cost_estimate=cost(2 * sum(rows) * FEAT * 2048, 4_000_000),
        name="finish",
    )(*operands)


def shards(
    hidden,
    cotangent,
    query_weight,
    out_weight,
    condition_weight,
    key_value_weight,
    encoder_query,
    encoder_out,
    database,
    neighbours,
    owners,
):
    me = lax.axis_index(Z)
    mine = lax.axis_index("dp")

    owner = owners[:, 0]
    selector = owner[None, :] == jnp.arange(NDP, dtype=jnp.int32)[:, None]
    wanted = jnp.sum(selector.astype(jnp.int32)[:, :, None] * neighbours[None, :, :], axis=1)
    kv_part = lax.dynamic_slice(
        key_value_weight.reshape(2 * DE, 2 * HEAD),
        (mine // 2 * 112, mine % 2 * HEAD),
        (112, HEAD),
    )
    q_part = lax.dynamic_slice(
        query_weight.reshape(NZ, FEAT, 2 * HEAD), (0, mine * 16, 0), (NZ, 16, 2 * HEAD)
    )
    q_part = q_part.reshape(NZ, 16, 2, HEAD).transpose(0, 2, 1, 3).reshape(NZ, 32, HEAD)
    part = jnp.concatenate([jnp.broadcast_to(kv_part, (NZ, 112, HEAD)), q_part], axis=1)
    both = jnp.concatenate([hidden, cotangent], axis=0)

    wanted, part, both = tie(wanted, part, both)
    asked = exchange(wanted, "dp")
    part = exchange(part, Z).transpose(1, 0, 2).reshape(144, HALF)
    weights = lax.all_gather(part, "dp", axis=0, tiled=True).reshape(16, 2, 144, HALF)
    returned = exchange(database[asked].reshape(NDP, NEIGH * NLEN // NZ, DE), "dp")
    fetched = exchange(returned[jnp.concatenate([owner, owner[:1]])], Z).reshape(KEYS, DE)
    enc_q = pl.pallas_call(
        encoder_queries,
        out_shape=jax.ShapeDtypeStruct((KEYS, DE), BF),
        in_specs=[ANY, ANY],
        out_specs=VMEM,
        scratch_shapes=[like(fetched), like(encoder_query), pltpu.SemaphoreType.DMA((2,))],
        compiler_params=PARAMS,
        cost_estimate=cost(2 * KEYS * DE * DE, 3_000_000),
        name="encoder_queries",
    )(fetched, encoder_query)

    chunks, far = ring(both)
    index = jnp.stack([(me + offset) % NZ for _, offset in chunks])
    chunks = [c for c, _ in chunks]
    count = len(chunks)
    acc, squares = pl.pallas_call(
        functools.partial(project, count),
        out_shape=(
            jax.ShapeDtypeStruct((TOK, 768), F32),
            jax.ShapeDtypeStruct((TOK, 1), F32),
        ),
        in_specs=[SMEM] + [ANY] * (count + 3),
        out_specs=(VMEM, VMEM),
        scratch_shapes=[
            pltpu.VMEM((count, 2 * TOK, FEAT), BF),
            pltpu.VMEM((count, FEAT, 256), BF),
            pltpu.VMEM((count, FEAT, 224), BF),
            pltpu.VMEM((count, 256, FEAT), BF),
            pltpu.SemaphoreType.DMA((count, 4)),
        ],
        compiler_params=PARAMS,
        cost_estimate=cost(2 * count * TOK * FEAT * 736, 16_000_000),
        name="project",
    )(index, *chunks, query_weight, condition_weight, out_weight)
    sent, inverse = pl.pallas_call(
        project_last,
        out_shape=(
            jax.ShapeDtypeStruct((NZ, SEG, 768), BF),
            jax.ShapeDtypeStruct((TOK, 1), F32),
        ),
        in_specs=[SMEM] + [ANY] * 7,
        out_specs=(VMEM, VMEM),
        scratch_shapes=[
            pltpu.VMEM((TOK, FEAT), BF),
            pltpu.VMEM((TOK, FEAT), BF),
            like(acc),
            like(squares),
            pltpu.VMEM((FEAT, 256), BF),
            pltpu.VMEM((FEAT, 224), BF),
            pltpu.VMEM((256, FEAT), BF),
            pltpu.SemaphoreType.DMA((7,)),
        ],
        compiler_params=PARAMS,
        cost_estimate=cost(2 * TOK * FEAT * 736, 4_000_000),
        name="project_last",
    )(
        jnp.stack([(me + 4) % NZ]), far[0], far[1], acc, squares,
        query_weight, condition_weight, out_weight,
    )
    got = exchange(sent, Z)
    operands = (fetched, enc_q, got, encoder_out)
    grad_query = pl.pallas_call(
        attention,
        out_shape=jax.ShapeDtypeStruct((SEG, 2 * HALF + HEAD), BF),
        in_specs=[ANY] * 5,
        out_specs=VMEM,
        scratch_shapes=[like(x) for x in operands]
        + [
            pltpu.VMEM((2, 16, 112, HALF), BF),
            pltpu.VMEM((2, KEYS, HALF), BF),
            pltpu.VMEM((2, KEYS, HALF), BF),
            pltpu.VMEM((KEYS, DE), BF),
            pltpu.SemaphoreType.DMA((6,)),
        ],
        compiler_params=PARAMS,
        cost_estimate=cost(4_000_000_000, 12_000_000),
        name="attention",
    )(*operands, weights)

    chunks, far = ring(grad_query)
    out = None
    for group in (chunks[:5], chunks[5:7], [(far[0], 4), (far[1], 4)]):
        sources = jnp.stack([(me + offset) % NZ for _, offset in group])
        group = [c for c, _ in group]
        starts = (0, SEG // 2) if group[0].shape[0] < SEG else (0,) * len(group)
        out = finish_call(
            group, starts, sources, hidden, inverse, weights.reshape(NDP, 144, HALF), out
        )
    return out


def solution(mesh):
    return jax.shard_map(
        shards,
        mesh=mesh,
        in_specs=(
            P("dp", Z),
            P("dp", Z),
            P(None, Z),
            P(Z, None),
            P(None, Z),
            P(None, None, Z),
            P(),
            P(),
            P("dp", Z, None),
            P("dp", None),
            P("dp", None),
        ),
        out_specs=P("dp", Z),
        check_vma=False,
    )
```

```python
import functools

import jax
import jax.numpy as jnp
from jax import lax
from jax.experimental import pallas as pl
from jax.experimental.pallas import tpu as pltpu
from jax.sharding import PartitionSpec as P

D = 4096
HEAD = 128
DE = 896
EHEADS = 7
SEG = 64
NLEN = 128
NEIGH = 2
KEYS = NLEN * NEIGH
NZ = 8
NDP = 32
SEGS = 7
FEAT = D // NZ
TOK = SEGS * SEG
HALF = 8 * HEAD
SCALE = HEAD**-0.5
epsilon = 1e-05
Z = ("group", "tensor")
BF = jnp.bfloat16
F32 = jnp.float32
MIB = 1024 * 1024
PARAMS = pltpu.CompilerParams(vmem_limit_bytes=20 * MIB)
HBM = pl.BlockSpec(memory_space=pltpu.HBM)
VMEM = pl.BlockSpec(memory_space=pltpu.VMEM)
SMEM = pl.BlockSpec(memory_space=pltpu.SMEM)
ANY = pl.BlockSpec(memory_space=pl.ANY)
NT = (((1,), (1,)), ((), ()))


def dot(a, b):
    return jnp.dot(a, b, preferred_element_type=F32)


def dot_nt(a, b):
    return lax.dot_general(a, b, NT, preferred_element_type=F32)


def shift(x, by):
    return lax.ppermute(x, Z, [(i, (i + by) % NZ) for i in range(NZ)])


def tie(*arrays):
    return lax.optimization_barrier(arrays)


def exchange(x, axis):
    return lax.all_to_all(x, axis, split_axis=0, concat_axis=0, tiled=True)


def start(pairs, sem):
    copies = [pltpu.make_async_copy(a, b, sem.at[i]) for i, (a, b) in enumerate(pairs)]
    for copy in copies:
        copy.start()
    return copies


def wait(copies):
    for copy in copies:
        copy.wait()


def cost(flops, size):
    return pl.CostEstimate(flops=flops, bytes_accessed=size, transcendentals=0)


def like(x):
    return pltpu.VMEM(x.shape, x.dtype)


def encoder_queries(fetched_hbm, weight_hbm, out_ref, fetched_ref, weight_ref, sem):
    copies = start([(fetched_hbm, fetched_ref), (weight_hbm, weight_ref)], sem)
    copies[0].wait()
    rows = fetched_ref[...].astype(F32)
    inverse = lax.rsqrt(jnp.mean(rows * rows, axis=-1, keepdims=True) + epsilon)
    normed = (rows * inverse).astype(BF)
    copies[1].wait()
    out_ref[...] = dot(normed, weight_ref[...]).astype(BF)


def project(count, first, index_ref, *refs):
    hiddens_hbm, cots_hbm, refs = refs[:count], refs[count : 2 * count], refs[2 * count :]
    query_hbm, cond_hbm, out_hbm = refs[:3]
    if not first:
        old_acc_ref, old_squares_ref = refs[3:5]
    acc_ref, squares_ref = refs[3 if first else 5 :][:2]
    hidden_ref, cot_ref, query_ref, cond_ref, out_weight_ref, sem = refs[-6:]
    copies = []
    for k in range(count):
        at = pl.ds(pl.multiple_of(index_ref[k] * FEAT, FEAT), FEAT)
        copies.append(
            start(
                [
                    (hiddens_hbm[k], hidden_ref.at[k]), (query_hbm.at[at], query_ref.at[k]),
                    (cond_hbm.at[:, at], cond_ref.at[k]), (cots_hbm[k], cot_ref.at[k]),
                    (out_hbm.at[:, at], out_weight_ref.at[k]),
                ], sem.at[k],
            )
        )
    for k in range(count):
        wait(copies[k])
        chunk = hidden_ref[k]
        squares = jnp.sum(jnp.square(chunk.astype(F32)), axis=-1, keepdims=True)
        parts = (
            dot(chunk, query_ref[k]),
            dot_nt(cot_ref[k], out_weight_ref[k]),
            dot_nt(chunk, cond_ref[k]),
        )
        source, source_squares = acc_ref, squares_ref
        if k == 0 and not first:
            source, source_squares = old_acc_ref, old_squares_ref
        fresh = first and k == 0
        for columns, part in zip((slice(0, 256), slice(256, 512), slice(512, 736)), parts):
            acc_ref[:, columns] = part if fresh else source[:, columns] + part
        squares_ref[...] = squares if fresh else source_squares[...] + squares


def project_call(hiddens, cots, index, weights, before):
    count, first = len(hiddens), before is None
    before = () if first else before
    results = (
        jax.ShapeDtypeStruct((TOK, 768), F32),
        jax.ShapeDtypeStruct((TOK, 1), F32),
    )
    at = 1 + 2 * count + 3
    return pl.pallas_call(
        functools.partial(project, count, first),
        out_shape=results,
        in_specs=[SMEM] + [ANY] * (2 * count) + [HBM] * 3 + [VMEM] * len(before),
        out_specs=(VMEM, VMEM),
        scratch_shapes=[
            pltpu.VMEM((count, TOK, FEAT), BF),
            pltpu.VMEM((count, TOK, FEAT), BF),
            pltpu.VMEM((count, FEAT, 256), BF),
            pltpu.VMEM((count, 224, FEAT), BF),
            pltpu.VMEM((count, 256, FEAT), BF),
            pltpu.SemaphoreType.DMA((count, 5)),
        ],
        input_output_aliases={} if first else {at: 0, at + 1: 1},
        compiler_params=PARAMS,
        cost_estimate=cost(2 * count * TOK * FEAT * 736, 6_000_000),
        name="project",
    )(jnp.stack(index), *hiddens, *cots, *weights, *before)


def project_last(
    index_ref, hidden_hbm, cot_hbm, acc_ref, squares_ref, query_hbm, cond_hbm, out_hbm,
    sent_ref, inverse_ref,
    hidden_ref, cot_ref, query_ref, cond_ref, out_weight_ref, sem,
):
    at = pl.ds(pl.multiple_of(index_ref[0] * FEAT, FEAT), FEAT)
    copies = start(
        [
            (hidden_hbm, hidden_ref),
            (query_hbm.at[at], query_ref), (cond_hbm.at[:, at], cond_ref),
            (cot_hbm, cot_ref), (out_hbm.at[:, at], out_weight_ref),
        ], sem,
    )
    wait(copies)
    chunk = hidden_ref[...]
    squares = squares_ref[...] + jnp.sum(
        jnp.square(chunk.astype(F32)), axis=-1, keepdims=True
    )
    inverse = lax.rsqrt(squares / D + epsilon)
    inverse_ref[...] = inverse
    queries = (acc_ref[:, :256] + dot(chunk, query_ref[...])) * inverse
    grads = acc_ref[:, 256:512] + dot_nt(cot_ref[...], out_weight_ref[...])
    condition = (acc_ref[:, 512:736] + dot_nt(chunk, cond_ref[...])) * inverse
    for columns, part in (
        (slice(0, 256), queries), (slice(256, 512), grads), (slice(512, 736), condition)
    ):
        sent_ref[:SEGS, :, columns] = part.astype(BF).reshape(SEGS, SEG, -1)
    sent_ref[:, :, 736:] = jnp.zeros((NZ, SEG, 32), BF)
    sent_ref[SEGS, :, :736] = jnp.zeros((SEG, 736), BF)


def attention(
    fetched_hbm, enc_q_hbm, got_hbm, enc_out_hbm, weights_hbm, out_ref,
    fetched_ref, enc_q_ref, got_ref, enc_out_ref, kv_ref, key_ref, value_ref, mixed_ref, sem,
):
    small = start(
        [
            (got_hbm, got_ref), (enc_q_hbm, enc_q_ref),
            (fetched_hbm, fetched_ref), (enc_out_hbm, enc_out_ref),
        ], sem,
    )
    large = [
        pltpu.make_async_copy(
            weights_hbm.at[:, j], kv_ref.at[j], sem.at[4 + j]
        )
        for j in range(2)
    ]
    for copy in large:
        copy.start()
    wait(small)
    cond_keys, cond_values = (
        jnp.concatenate([got_ref[z, :, 512:736] for z in range(n, n + 4)], axis=1)
        for n in (0, 4)
    )
    for h in range(EHEADS):
        columns = slice(h * HEAD, (h + 1) * HEAD)
        exponent = jnp.exp(dot_nt(enc_q_ref[:, columns], cond_keys[:, columns]) * SCALE)
        weights = (exponent / jnp.sum(exponent, axis=-1, keepdims=True)).astype(BF)
        mixed_ref[:, columns] = dot(weights, cond_values[:, columns]).astype(BF)
    encoded = (fetched_ref[...].astype(F32) + dot(mixed_ref[...], enc_out_ref[...])).astype(BF)
    total = jnp.zeros((SEG, HEAD), F32)
    for j in range(2):
        large[j].wait()
        key_ref[j] = dot(encoded, kv_ref[j, 0:8].reshape(DE, HALF)).astype(BF)
        value_ref[j] = dot(encoded, kv_ref[j, 8:16].reshape(DE, HALF)).astype(BF)
        for z in range(NZ):
            columns = slice(z * HEAD, (z + 1) * HEAD)
            query = got_ref[z, :, j * HEAD : (j + 1) * HEAD]
            grad_att = got_ref[z, :, (2 + j) * HEAD : (3 + j) * HEAD]
            key, value = key_ref[j, :, columns], value_ref[j, :, columns]
            exponent = jnp.exp(dot_nt(query, key) * SCALE)
            probs = exponent / jnp.sum(exponent, axis=-1, keepdims=True)
            attended = dot(probs.astype(BF), value).astype(BF)
            delta = jnp.sum(
                grad_att.astype(F32) * attended.astype(F32), axis=-1, keepdims=True
            )
            grad_probs = dot_nt(grad_att, value)
            grad_scores = (probs * (grad_probs - delta) * SCALE).astype(BF)
            grad_query = dot(grad_scores, key).astype(BF)
            out_ref[:, j * HALF + z * HEAD : j * HALF + (z + 1) * HEAD] = grad_query
            total = total + grad_query.astype(F32) * query.astype(F32)
    stat = jnp.sum(total, axis=-1, keepdims=True) / D
    high = stat.astype(BF)
    low = (stat - high.astype(F32)).astype(BF)
    lane = lax.broadcasted_iota(jnp.int32, (SEG, HEAD), 1)
    out_ref[:, 2 * HALF :] = jnp.where(
        lane == 0, high.astype(F32), jnp.where(lane == 1, low.astype(F32), 0.0)
    ).astype(BF)


def finish(starts, first, *refs):
    count = len(starts)
    source_ref, refs = refs[0], refs[1:]
    chunks_hbm, refs = refs[:count], refs[count:]
    hidden_hbm, inverse_hbm, weights_hbm = refs[:3]
    refs = refs[3 if first else 4 :]
    out_hbm, refs = refs[0], refs[1:]
    chunk_refs, refs = refs[:count], refs[count:]
    hidden_refs, refs = refs[:count], refs[count:]
    out_refs, refs = refs[:count], refs[count:]
    inverse_ref, weight_ref, sem, out_sem = refs
    places = []
    for k in range(count):
        source = source_ref[k]
        rows = chunk_refs[k].shape[0]
        at = jnp.where(source < SEGS, source, 0) * SEG + starts[k]
        places.append((source < SEGS, pl.ds(pl.multiple_of(at, 32), rows)))
    loads = [(inverse_hbm, inverse_ref)]
    loads += [
        (weights_hbm.at[:, j], weight_ref.at[j]) for j in range(2)
    ]
    for k in range(count):
        loads.append((chunks_hbm[k], chunk_refs[k]))
        loads.append((hidden_hbm.at[places[k][1]], hidden_refs[k]))
    wait(start(loads, sem))
    rows = [c.shape[0] for c in chunk_refs]
    chunks = jnp.concatenate([c[...] for c in chunk_refs], axis=0)
    grads = sum(
        dot_nt(chunks[:, j * HALF : (j + 1) * HALF], weight_ref[j].reshape(FEAT, HALF))
        for j in range(2)
    )
    for k in range(count):
        grad = grads[sum(rows[:k]) : sum(rows[: k + 1])]
        tail = chunk_refs[k][:, 2 * HALF :].astype(F32)
        stat = tail[:, 0:1] + tail[:, 1:2]
        inverse = inverse_ref[places[k][1], :]
        out_refs[k][...] = (
            inverse * grad - hidden_refs[k][...].astype(F32) * (inverse * inverse * stat)
        ).astype(BF)

        @pl.when(places[k][0])
        def _(k=k):
            pltpu.make_async_copy(
                out_refs[k], out_hbm.at[places[k][1]], out_sem.at[k]
            ).start()

    for k in range(count):

        @pl.when(places[k][0])
        def _(k=k):
            pltpu.make_async_copy(
                out_refs[k], out_hbm.at[places[k][1]], out_sem.at[k]
            ).wait()


def finish_call(chunks, starts, sources, hidden, inverse, weights, previous):
    first = previous is None
    operands = [sources, *chunks, hidden, inverse, weights] + ([] if first else [previous])
    rows = [c.shape[0] for c in chunks]
    return pl.pallas_call(
        functools.partial(finish, starts, first),
        out_shape=jax.ShapeDtypeStruct((TOK, FEAT), BF),
        in_specs=[SMEM] + [ANY] * (len(chunks) + 2) + [HBM] * (1 if first else 2),
        out_specs=HBM,
        scratch_shapes=[like(c) for c in chunks]
        + [pltpu.VMEM((r, FEAT), BF) for r in rows] * 2
        + [
            like(inverse),
            pltpu.VMEM((2, NDP, 16, HALF), BF),
            pltpu.SemaphoreType.DMA((3 + 2 * len(chunks),)),
            pltpu.SemaphoreType.DMA((len(chunks),)),
        ],
        input_output_aliases={} if first else {len(operands) - 1: 0},
        compiler_params=PARAMS,
        cost_estimate=cost(2 * sum(rows) * FEAT * 2048, 4_000_000),
        name="finish",
    )(*operands)


def shards(
    hidden,
    cotangent,
    query_weight,
    out_weight,
    condition_weight,
    key_value_weight,
    encoder_query,
    encoder_out,
    database,
    neighbours,
    owners,
):
    me = lax.axis_index(Z)
    mine = lax.axis_index("dp")

    owner = owners[:, 0]
    selector = owner[None, :] == jnp.arange(NDP, dtype=jnp.int32)[:, None]
    wanted = jnp.sum(selector.astype(jnp.int32)[:, :, None] * neighbours[None, :, :], axis=1)
    kv_part = lax.dynamic_slice(
        key_value_weight.reshape(2 * DE, 2 * HEAD),
        (mine // 2 * 112, mine % 2 * HEAD),
        (112, HEAD),
    )
    q_part = lax.dynamic_slice(
        query_weight.reshape(NZ, FEAT, 2 * HEAD), (0, mine * 16, 0), (NZ, 16, 2 * HEAD)
    )
    q_part = q_part.reshape(NZ, 16, 2, HEAD).transpose(0, 2, 1, 3).reshape(NZ, 32, HEAD)
    part = jnp.concatenate([jnp.broadcast_to(kv_part, (NZ, 112, HEAD)), q_part], axis=1)

    projections = (query_weight, condition_weight.T, out_weight)
    right = left = hidden
    grad_right = grad_left = cotangent
    acc = project_call([hidden], [cotangent], [me], projections, None)
    for step in range(1, 4):
        right, left = shift(right, 1), shift(left, -1)
        if step == 1:
            wanted, part, right, left = tie(wanted, part, right, left)
        else:
            right, left, _, _ = tie(right, left, grad_right, grad_left)
        grad_right, grad_left = shift(grad_right, 1), shift(grad_left, -1)
        grad_right, grad_left, right, left, *acc = tie(grad_right, grad_left, right, left, *acc)
        index = [(me - step) % NZ, (me + step) % NZ]
        acc = project_call([right, left], [grad_right, grad_left], index, projections, acc)
    far = (shift(right, 1), shift(grad_left, -1))
    acc, squares = acc

    asked = exchange(wanted, "dp")
    part = exchange(part, Z).transpose(1, 0, 2).reshape(144, HALF)
    kv_weights = lax.all_gather(part[:112], "dp", axis=0, tiled=True).reshape(16, 2, 112, HALF)
    q_rows, _ = tie(part[112:], right)
    q_weights = lax.all_gather(q_rows, "dp", axis=0, tiled=True).reshape(NDP, 2, 16, HALF)
    returned = exchange(database[asked].reshape(NDP, NEIGH * NLEN // NZ, DE), "dp")
    fetched = exchange(returned[jnp.concatenate([owner, owner[:1]])], Z).reshape(KEYS, DE)
    enc_q = pl.pallas_call(
        encoder_queries,
        out_shape=jax.ShapeDtypeStruct((KEYS, DE), BF),
        in_specs=[HBM, HBM],
        out_specs=VMEM,
        scratch_shapes=[like(fetched), like(encoder_query), pltpu.SemaphoreType.DMA((2,))],
        compiler_params=PARAMS,
        cost_estimate=cost(2 * KEYS * DE * DE, 3_000_000),
        name="encoder_queries",
    )(fetched, encoder_query)

    sent, inverse = pl.pallas_call(
        project_last,
        out_shape=(
            jax.ShapeDtypeStruct((NZ, SEG, 768), BF),
            jax.ShapeDtypeStruct((TOK, 1), F32),
        ),
        in_specs=[SMEM] + [ANY] * 2 + [VMEM] * 2 + [HBM] * 3,
        out_specs=(VMEM, VMEM),
        scratch_shapes=[
            pltpu.VMEM((TOK, FEAT), BF),
            pltpu.VMEM((TOK, FEAT), BF),
            pltpu.VMEM((FEAT, 256), BF),
            pltpu.VMEM((224, FEAT), BF),
            pltpu.VMEM((256, FEAT), BF),
            pltpu.SemaphoreType.DMA((5,)),
        ],
        compiler_params=PARAMS,
        cost_estimate=cost(2 * TOK * FEAT * 736, 4_000_000),
        name="project_last",
    )(
        jnp.stack([(me + 4) % NZ]), far[0], far[1], acc, squares, *projections
    )
    got = exchange(sent, Z)
    operands = (fetched, enc_q, got, encoder_out)
    grad_query = pl.pallas_call(
        attention,
        out_shape=jax.ShapeDtypeStruct((SEG, 2 * HALF + HEAD), BF),
        in_specs=[HBM, ANY, HBM, HBM, HBM],
        out_specs=VMEM,
        scratch_shapes=[like(x) for x in operands]
        + [
            like(kv_weights.transpose(1, 0, 2, 3)),
            pltpu.VMEM((2, KEYS, HALF), BF),
            pltpu.VMEM((2, KEYS, HALF), BF),
            pltpu.VMEM((KEYS, DE), BF),
            pltpu.SemaphoreType.DMA((6,)),
        ],
        compiler_params=PARAMS,
        cost_estimate=cost(4_000_000_000, 12_000_000),
        name="attention",
    )(*operands, kv_weights)

    def finished(group, offsets, out):
        sources = jnp.stack([(me + offset) % NZ for offset in offsets])
        starts = (0, SEG // 2) if group[0].shape[0] < SEG else (0,) * len(group)
        return finish_call(group, starts, sources, hidden, inverse, q_weights, out)

    right = left = grad_query
    group, offsets, out = [grad_query], [0], None
    for step in range(1, 4):
        right, left = shift(right, 1), shift(left, -1)
        out = finished(group, offsets, out)
        group, offsets = [right, left], [-step, step]
        right, left, out = tie(right, left, out)
    far = [shift(right[: SEG // 2], 1), shift(left[SEG // 2 :], -1)]
    out = finished(group, offsets, out)
    return finished(far, (4, 4), out)


def solution(mesh):
    return jax.shard_map(
        shards,
        mesh=mesh,
        in_specs=(
            P("dp", Z),
            P("dp", Z),
            P(None, Z),
            P(Z, None),
            P(None, Z),
            P(None, None, Z),
            P(),
            P(),
            P("dp", Z, None),
            P("dp", None),
            P("dp", None),
        ),
        out_specs=P("dp", Z),
        check_vma=False,
    )
```

```python
import functools

import jax
import jax.numpy as jnp
from jax import lax
from jax.experimental import pallas as pl
from jax.experimental.pallas import tpu as pltpu
from jax.sharding import PartitionSpec as P

D = 4096
HEAD = 128
DE = 896
EHEADS = 7
SEG = 64
NLEN = 128
NEIGH = 2
KEYS = NLEN * NEIGH
NZ = 8
NDP = 32
SEGS = 7
FEAT = D // NZ
TOK = SEGS * SEG
HALF = 8 * HEAD
SCALE = HEAD**-0.5
epsilon = 1e-05
Z = ("group", "tensor")
BF = jnp.bfloat16
F32 = jnp.float32
MIB = 1024 * 1024
KNOB = 20_000_000_000
PARAMS = pltpu.CompilerParams(vmem_limit_bytes=59 * MIB)
ROOM = pltpu.CompilerParams(vmem_limit_bytes=53 * MIB + MIB // 2)
VMEM = pl.BlockSpec(memory_space=pltpu.VMEM)
SMEM = pl.BlockSpec(memory_space=pltpu.SMEM)
ANY = pl.BlockSpec(memory_space=pl.ANY)
NT = (((1,), (1,)), ((), ()))


def dot(a, b):
    return jnp.dot(a, b, preferred_element_type=F32)


def dot_nt(a, b):
    return lax.dot_general(a, b, NT, preferred_element_type=F32)


def shift(x, by):
    return lax.ppermute(x, Z, [(i, (i + by) % NZ) for i in range(NZ)])


def tie(*arrays):
    return lax.optimization_barrier(arrays)


def exchange(x, axis):
    return lax.all_to_all(x, axis, split_axis=0, concat_axis=0, tiled=True)


def start(pairs, sem):
    copies = [pltpu.make_async_copy(a, b, sem.at[i]) for i, (a, b) in enumerate(pairs)]
    for copy in copies:
        copy.start()
    return copies


def wait(copies):
    for copy in copies:
        copy.wait()


def cost(flops, size):
    return pl.CostEstimate(flops=flops, bytes_accessed=size, transcendentals=0)


def like(x):
    return pltpu.VMEM(x.shape, x.dtype)


def encoder_queries(fetched_hbm, weight_hbm, out_hbm, fetched_ref, weight_ref, out_ref, sem):
    copies = start([(fetched_hbm, fetched_ref), (weight_hbm, weight_ref)], sem)
    copies[0].wait()
    rows = fetched_ref[...].astype(F32)
    inverse = lax.rsqrt(jnp.mean(rows * rows, axis=-1, keepdims=True) + epsilon)
    normed = (rows * inverse).astype(BF)
    copies[1].wait()
    out_ref[...] = dot(normed, weight_ref[...]).astype(BF)
    wait(start([(out_ref, out_hbm)], sem.at[pl.ds(2, 1)]))


def project(count, index_ref, *refs):
    hiddens_hbm, cots_hbm, refs = refs[:count], refs[count : 2 * count], refs[2 * count :]
    query_hbm, cond_hbm, out_hbm, acc_hbm, squares_hbm = refs[:5]
    hidden_ref, cot_ref, query_ref, cond_ref, out_weight_ref = refs[5:10]
    acc_ref, squares_ref, sem, out_sem = refs[10:]
    copies = []
    for k in range(count):
        at = pl.ds(pl.multiple_of(index_ref[k] * FEAT, FEAT), FEAT)
        copies.append(
            start(
                [
                    (hiddens_hbm[k], hidden_ref.at[k]), (query_hbm.at[at], query_ref.at[k]),
                    (cond_hbm.at[:, at], cond_ref.at[k]), (cots_hbm[k], cot_ref.at[k]),
                    (out_hbm.at[:, at], out_weight_ref.at[k]),
                ], sem.at[k],
            )
        )
    for k in range(count):
        wait(copies[k])
        chunk = hidden_ref[k]
        squares = jnp.sum(jnp.square(chunk.astype(F32)), axis=-1, keepdims=True)
        parts = (
            dot(chunk, query_ref[k]),
            dot_nt(cot_ref[k], out_weight_ref[k]),
            dot_nt(chunk, cond_ref[k]),
        )
        for columns, part in zip((slice(0, 256), slice(256, 512), slice(512, 736)), parts):
            acc_ref[:, columns] = part if k == 0 else acc_ref[:, columns] + part
        squares_ref[...] = squares if k == 0 else squares_ref[...] + squares
    wait(start([(acc_ref, acc_hbm), (squares_ref, squares_hbm)], out_sem))


def project_last(
    index_ref, hidden_hbm, cot_hbm, acc_hbm, squares_hbm, query_hbm, cond_hbm, out_hbm,
    sent_hbm, inverse_hbm,
    hidden_ref, cot_ref, acc_ref, squares_ref, query_ref, cond_ref, out_weight_ref,
    sent_ref, inverse_ref, sem, out_sem,
):
    at = pl.ds(pl.multiple_of(index_ref[0] * FEAT, FEAT), FEAT)
    copies = start(
        [
            (hidden_hbm, hidden_ref), (squares_hbm, squares_ref), (acc_hbm, acc_ref),
            (query_hbm.at[at], query_ref), (cond_hbm.at[:, at], cond_ref),
            (cot_hbm, cot_ref), (out_hbm.at[:, at], out_weight_ref),
        ], sem,
    )
    wait(copies)
    chunk = hidden_ref[...]
    squares = squares_ref[...] + jnp.sum(
        jnp.square(chunk.astype(F32)), axis=-1, keepdims=True
    )
    inverse = lax.rsqrt(squares / D + epsilon)
    inverse_ref[...] = inverse
    queries = (acc_ref[:, :256] + dot(chunk, query_ref[...])) * inverse
    grads = acc_ref[:, 256:512] + dot_nt(cot_ref[...], out_weight_ref[...])
    condition = (acc_ref[:, 512:736] + dot_nt(chunk, cond_ref[...])) * inverse
    for columns, part in (
        (slice(0, 256), queries), (slice(256, 512), grads), (slice(512, 736), condition)
    ):
        sent_ref[:SEGS, :, columns] = part.astype(BF).reshape(SEGS, SEG, -1)
    sent_ref[:, :, 736:] = jnp.zeros((NZ, SEG, 32), BF)
    sent_ref[SEGS, :, :736] = jnp.zeros((SEG, 736), BF)
    wait(start([(sent_ref, sent_hbm), (inverse_ref, inverse_hbm)], out_sem))


def attention(
    fetched_hbm, enc_q_hbm, got_hbm, enc_out_hbm, weights_hbm, out_ref,
    fetched_ref, enc_q_ref, got_ref, enc_out_ref, kv_ref, key_ref, value_ref, mixed_ref, sem,
):
    small = start(
        [
            (got_hbm, got_ref), (enc_q_hbm, enc_q_ref),
            (fetched_hbm, fetched_ref), (enc_out_hbm, enc_out_ref),
        ], sem,
    )
    large = [
        pltpu.make_async_copy(
            weights_hbm.at[:, j, pl.ds(0, 112), :], kv_ref.at[j], sem.at[4 + j]
        )
        for j in range(2)
    ]
    for copy in large:
        copy.start()
    wait(small)
    cond_keys, cond_values = (
        jnp.concatenate([got_ref[z, :, 512:736] for z in range(n, n + 4)], axis=1)
        for n in (0, 4)
    )
    for h in range(EHEADS):
        columns = slice(h * HEAD, (h + 1) * HEAD)
        exponent = jnp.exp(dot_nt(enc_q_ref[:, columns], cond_keys[:, columns]) * SCALE)
        weights = (exponent / jnp.sum(exponent, axis=-1, keepdims=True)).astype(BF)
        mixed_ref[:, columns] = dot(weights, cond_values[:, columns]).astype(BF)
    encoded = (fetched_ref[...].astype(F32) + dot(mixed_ref[...], enc_out_ref[...])).astype(BF)
    total = jnp.zeros((SEG, HEAD), F32)
    for j in range(2):
        large[j].wait()
        key_ref[j] = dot(encoded, kv_ref[j, 0:8].reshape(DE, HALF)).astype(BF)
        value_ref[j] = dot(encoded, kv_ref[j, 8:16].reshape(DE, HALF)).astype(BF)
        for z in range(NZ):
            columns = slice(z * HEAD, (z + 1) * HEAD)
            query = got_ref[z, :, j * HEAD : (j + 1) * HEAD]
            grad_att = got_ref[z, :, (2 + j) * HEAD : (3 + j) * HEAD]
            key, value = key_ref[j, :, columns], value_ref[j, :, columns]
            exponent = jnp.exp(dot_nt(query, key) * SCALE)
            probs = exponent / jnp.sum(exponent, axis=-1, keepdims=True)
            attended = dot(probs.astype(BF), value).astype(BF)
            delta = jnp.sum(
                grad_att.astype(F32) * attended.astype(F32), axis=-1, keepdims=True
            )
            grad_probs = dot_nt(grad_att, value)
            grad_scores = (probs * (grad_probs - delta) * SCALE).astype(BF)
            grad_query = dot(grad_scores, key).astype(BF)
            out_ref[:, j * HALF + z * HEAD : j * HALF + (z + 1) * HEAD] = grad_query
            total = total + grad_query.astype(F32) * query.astype(F32)
    stat = jnp.sum(total, axis=-1, keepdims=True) / D
    high = stat.astype(BF)
    low = (stat - high.astype(F32)).astype(BF)
    lane = lax.broadcasted_iota(jnp.int32, (SEG, HEAD), 1)
    out_ref[:, 2 * HALF :] = jnp.where(
        lane == 0, high.astype(F32), jnp.where(lane == 1, low.astype(F32), 0.0)
    ).astype(BF)


def finish(starts, first, *refs):
    count = len(starts)
    source_ref, refs = refs[0], refs[1:]
    chunks_hbm, refs = refs[:count], refs[count:]
    hidden_hbm, inverse_hbm, weights_hbm = refs[:3]
    refs = refs[3 if first else 4 :]
    out_hbm, refs = refs[0], refs[1:]
    chunk_refs, refs = refs[:count], refs[count:]
    hidden_refs, refs = refs[:count], refs[count:]
    out_refs, refs = refs[:count], refs[count:]
    inverse_ref, weight_ref, sem, out_sem = refs
    places = []
    for k in range(count):
        source = source_ref[k]
        rows = chunk_refs[k].shape[0]
        at = jnp.where(source < SEGS, source, 0) * SEG + starts[k]
        places.append((source < SEGS, pl.ds(pl.multiple_of(at, 32), rows)))
    loads = [(inverse_hbm, inverse_ref)]
    loads += [
        (weights_hbm.at[:, pl.ds(112 + 16 * j, 16), :], weight_ref.at[j]) for j in range(2)
    ]
    for k in range(count):
        loads.append((chunks_hbm[k], chunk_refs[k]))
        loads.append((hidden_hbm.at[places[k][1]], hidden_refs[k]))
    wait(start(loads, sem))
    rows = [c.shape[0] for c in chunk_refs]
    chunks = jnp.concatenate([c[...] for c in chunk_refs], axis=0)
    grads = sum(
        dot_nt(chunks[:, j * HALF : (j + 1) * HALF], weight_ref[j].reshape(FEAT, HALF))
        for j in range(2)
    )
    for k in range(count):
        grad = grads[sum(rows[:k]) : sum(rows[: k + 1])]
        tail = chunk_refs[k][:, 2 * HALF :].astype(F32)
        stat = tail[:, 0:1] + tail[:, 1:2]
        inverse = inverse_ref[places[k][1], :]
        out_refs[k][...] = (
            inverse * grad - hidden_refs[k][...].astype(F32) * (inverse * inverse * stat)
        ).astype(BF)

        @pl.when(places[k][0])
        def _(k=k):
            pltpu.make_async_copy(
                out_refs[k], out_hbm.at[places[k][1]], out_sem.at[k]
            ).start()

    for k in range(count):

        @pl.when(places[k][0])
        def _(k=k):
            pltpu.make_async_copy(
                out_refs[k], out_hbm.at[places[k][1]], out_sem.at[k]
            ).wait()


def finish_call(chunks, starts, sources, hidden, inverse, weights, previous):
    first = previous is None
    operands = [sources, *chunks, hidden, inverse, weights] + ([] if first else [previous])
    rows = [c.shape[0] for c in chunks]
    return pl.pallas_call(
        functools.partial(finish, starts, first),
        out_shape=jax.ShapeDtypeStruct((TOK, FEAT), BF),
        in_specs=[SMEM] + [ANY] * (len(operands) - 1),
        out_specs=ANY,
        scratch_shapes=[like(c) for c in chunks]
        + [pltpu.VMEM((r, FEAT), BF) for r in rows] * 2
        + [
            like(inverse),
            pltpu.VMEM((2, NDP, 16, HALF), BF),
            pltpu.SemaphoreType.DMA((3 + 2 * len(chunks),)),
            pltpu.SemaphoreType.DMA((len(chunks),)),
        ],
        input_output_aliases={} if first else {len(operands) - 1: 0},
        compiler_params=ROOM,
        cost_estimate=cost(2 * sum(rows) * FEAT * 2048, 4_000_000),
        name="finish",
    )(*operands)


def shards(
    hidden,
    cotangent,
    query_weight,
    out_weight,
    condition_weight,
    key_value_weight,
    encoder_query,
    encoder_out,
    database,
    neighbours,
    owners,
):
    me = lax.axis_index(Z)
    mine = lax.axis_index("dp")

    owner = owners[:, 0]
    selector = owner[None, :] == jnp.arange(NDP, dtype=jnp.int32)[:, None]
    wanted = jnp.sum(selector.astype(jnp.int32)[:, :, None] * neighbours[None, :, :], axis=1)
    kv_part = lax.dynamic_slice(
        key_value_weight.reshape(2 * DE, 2 * HEAD),
        (mine // 2 * 112, mine % 2 * HEAD),
        (112, HEAD),
    )
    q_part = lax.dynamic_slice(
        query_weight.reshape(NZ, FEAT, 2 * HEAD), (0, mine * 16, 0), (NZ, 16, 2 * HEAD)
    )
    q_part = q_part.reshape(NZ, 16, 2, HEAD).transpose(0, 2, 1, 3).reshape(NZ, 32, HEAD)
    part = jnp.concatenate([jnp.broadcast_to(kv_part, (NZ, 112, HEAD)), q_part], axis=1)

    projections = (query_weight, condition_weight.T, out_weight)
    right = left = hidden
    grad_right = grad_left = cotangent
    index, chunks, grad_chunks = [me], [hidden], [cotangent]
    for step in range(1, 4):
        right, left = shift(right, 1), shift(left, -1)
        grad_right, grad_left = shift(grad_right, 1), shift(grad_left, -1)
        index += [(me - step) % NZ, (me + step) % NZ]
        chunks += [right, left]
        grad_chunks += [grad_right, grad_left]
    far = (shift(right, 1), shift(grad_left, -1))
    count = len(chunks)
    acc, squares = pl.pallas_call(
        functools.partial(project, count),
        out_shape=(
            jax.ShapeDtypeStruct((TOK, 768), F32),
            jax.ShapeDtypeStruct((TOK, 1), F32),
        ),
        in_specs=[SMEM] + [ANY] * (2 * count + 3),
        out_specs=(ANY, ANY),
        scratch_shapes=[
            pltpu.VMEM((count, TOK, FEAT), BF),
            pltpu.VMEM((count, TOK, FEAT), BF),
            pltpu.VMEM((count, FEAT, 256), BF),
            pltpu.VMEM((count, 224, FEAT), BF),
            pltpu.VMEM((count, 256, FEAT), BF),
            pltpu.VMEM((TOK, 768), F32),
            pltpu.VMEM((TOK, 1), F32),
            pltpu.SemaphoreType.DMA((count, 5)),
            pltpu.SemaphoreType.DMA((2,)),
        ],
        compiler_params=ROOM,
        cost_estimate=cost(2 * count * TOK * FEAT * 736, 16_000_000),
        name="project",
    )(jnp.stack(index), *chunks, *grad_chunks, *projections)

    asked = exchange(wanted, "dp")
    part = exchange(part, Z).transpose(1, 0, 2).reshape(144, HALF)
    weights = lax.all_gather(part, "dp", axis=0, tiled=True).reshape(16, 2, 144, HALF)
    returned = exchange(database[asked].reshape(NDP, NEIGH * NLEN // NZ, DE), "dp")
    fetched = exchange(returned[jnp.concatenate([owner, owner[:1]])], Z).reshape(KEYS, DE)
    enc_q = pl.pallas_call(
        encoder_queries,
        out_shape=jax.ShapeDtypeStruct((KEYS, DE), BF),
        in_specs=[ANY, ANY],
        out_specs=ANY,
        scratch_shapes=[
            like(fetched), like(encoder_query), like(fetched), pltpu.SemaphoreType.DMA((3,))
        ],
        compiler_params=PARAMS,
        cost_estimate=cost(2 * KEYS * DE * DE, 3_000_000),
        name="encoder_queries",
    )(fetched, encoder_query)

    sent, inverse = pl.pallas_call(
        project_last,
        out_shape=(
            jax.ShapeDtypeStruct((NZ, SEG, 768), BF),
            jax.ShapeDtypeStruct((TOK, 1), F32),
        ),
        in_specs=[SMEM] + [ANY] * 7,
        out_specs=(ANY, ANY),
        scratch_shapes=[
            pltpu.VMEM((TOK, FEAT), BF),
            pltpu.VMEM((TOK, FEAT), BF),
            like(acc),
            like(squares),
            pltpu.VMEM((FEAT, 256), BF),
            pltpu.VMEM((224, FEAT), BF),
            pltpu.VMEM((256, FEAT), BF),
            pltpu.VMEM((NZ, SEG, 768), BF),
            like(squares),
            pltpu.SemaphoreType.DMA((7,)),
            pltpu.SemaphoreType.DMA((2,)),
        ],
        compiler_params=PARAMS,
        cost_estimate=cost(KNOB, 4_000_000),
        name="project_last",
    )(
        jnp.stack([(me + 4) % NZ]), far[0], far[1], acc, squares, *projections
    )
    got = exchange(sent, Z)
    operands = (fetched, enc_q, got, encoder_out)
    grad_query = pl.pallas_call(
        attention,
        out_shape=jax.ShapeDtypeStruct((SEG, 2 * HALF + HEAD), BF),
        in_specs=[ANY] * 5,
        out_specs=VMEM,
        scratch_shapes=[like(x) for x in operands]
        + [
            pltpu.VMEM((2, 16, 112, HALF), BF),
            pltpu.VMEM((2, KEYS, HALF), BF),
            pltpu.VMEM((2, KEYS, HALF), BF),
            pltpu.VMEM((KEYS, DE), BF),
            pltpu.SemaphoreType.DMA((6,)),
        ],
        compiler_params=PARAMS,
        cost_estimate=cost(4_000_000_000, 12_000_000),
        name="attention",
    )(*operands, weights)

    def finished(group, offsets, out):
        sources = jnp.stack([(me + offset) % NZ for offset in offsets])
        starts = (0, SEG // 2) if group[0].shape[0] < SEG else (0,) * len(group)
        return finish_call(group, starts, sources, hidden, inverse, weights.reshape(NDP, 144, HALF), out)

    right = left = grad_query
    group, offsets, out = [grad_query], [0], None
    for step in range(1, 4):
        right, left = shift(right, 1), shift(left, -1)
        out = finished(group, offsets, out)
        group, offsets = [right, left], [-step, step]
        right, left, out = tie(right, left, out)
    far = [shift(right[: SEG // 2], 1), shift(left[SEG // 2 :], -1)]
    out = finished(group, offsets, out)
    return finished(far, (4, 4), out)


def solution(mesh):
    return jax.shard_map(
        shards,
        mesh=mesh,
        in_specs=(
            P("dp", Z),
            P("dp", Z),
            P(None, Z),
            P(Z, None),
            P(None, Z),
            P(None, None, Z),
            P(),
            P(),
            P("dp", Z, None),
            P("dp", None),
            P("dp", None),
        ),
        out_specs=P("dp", Z),
        check_vma=False,
    )
```

```python
import functools

import jax
import jax.numpy as jnp
from jax import lax
from jax.experimental import pallas as pl
from jax.experimental.pallas import tpu as pltpu
from jax.sharding import PartitionSpec as P

D = 4096
HEAD = 128
DE = 896
EHEADS = 7
SEG = 64
NLEN = 128
NEIGH = 2
KEYS = NLEN * NEIGH
NZ = 8
NDP = 32
SEGS = 7
FEAT = D // NZ
TOK = SEGS * SEG
HALF = 8 * HEAD
SCALE = HEAD**-0.5
epsilon = 1e-05
Z = ("group", "tensor")
BF = jnp.bfloat16
F32 = jnp.float32
MIB = 1024 * 1024
KNOB = 20_000_000_000
PARAMS = pltpu.CompilerParams(vmem_limit_bytes=59 * MIB)
SMALL = pltpu.CompilerParams(vmem_limit_bytes=24 * MIB)
ROOM = pltpu.CompilerParams(vmem_limit_bytes=53 * MIB + MIB // 2)
VMEM = pl.BlockSpec(memory_space=pltpu.VMEM)
SMEM = pl.BlockSpec(memory_space=pltpu.SMEM)
ANY = pl.BlockSpec(memory_space=pl.ANY)
NT = (((1,), (1,)), ((), ()))


def dot(a, b):
    return jnp.dot(a, b, preferred_element_type=F32)


def dot_nt(a, b):
    return lax.dot_general(a, b, NT, preferred_element_type=F32)


def shift(x, by):
    return lax.ppermute(x, Z, [(i, (i + by) % NZ) for i in range(NZ)])


def tie(*arrays):
    return lax.optimization_barrier(arrays)


def exchange(x, axis):
    return lax.all_to_all(x, axis, split_axis=0, concat_axis=0, tiled=True)


def start(pairs, sem):
    copies = [pltpu.make_async_copy(a, b, sem.at[i]) for i, (a, b) in enumerate(pairs)]
    for copy in copies:
        copy.start()
    return copies


def wait(copies):
    for copy in copies:
        copy.wait()


def cost(flops, size):
    return pl.CostEstimate(flops=flops, bytes_accessed=size, transcendentals=0)


def like(x):
    return pltpu.VMEM(x.shape, x.dtype)


def encoder_queries(fetched_hbm, weight_hbm, out_hbm, fetched_ref, weight_ref, out_ref, sem):
    copies = start([(fetched_hbm, fetched_ref), (weight_hbm, weight_ref)], sem)
    copies[0].wait()
    rows = fetched_ref[...].astype(F32)
    inverse = lax.rsqrt(jnp.mean(rows * rows, axis=-1, keepdims=True) + epsilon)
    normed = (rows * inverse).astype(BF)
    copies[1].wait()
    out_ref[...] = dot(normed, weight_ref[...]).astype(BF)
    wait(start([(out_ref, out_hbm)], sem.at[pl.ds(2, 1)]))


def project(count, index_ref, *refs):
    hiddens_hbm, cots_hbm, refs = refs[:count], refs[count : 2 * count], refs[2 * count :]
    query_hbm, cond_hbm, out_hbm, acc_hbm, squares_hbm = refs[:5]
    hidden_ref, cot_ref, query_ref, cond_ref, out_weight_ref = refs[5:10]
    acc_ref, squares_ref, sem, out_sem = refs[10:]
    copies = []
    for k in range(count):
        at = pl.ds(pl.multiple_of(index_ref[k] * FEAT, FEAT), FEAT)
        copies.append(
            start(
                [
                    (hiddens_hbm[k], hidden_ref.at[k]), (query_hbm.at[at], query_ref.at[k]),
                    (cond_hbm.at[:, at], cond_ref.at[k]), (cots_hbm[k], cot_ref.at[k]),
                    (out_hbm.at[:, at], out_weight_ref.at[k]),
                ], sem.at[k],
            )
        )
    for k in range(count):
        wait(copies[k])
        chunk = hidden_ref[k]
        squares = jnp.sum(jnp.square(chunk.astype(F32)), axis=-1, keepdims=True)
        parts = (
            dot(chunk, query_ref[k]),
            dot_nt(cot_ref[k], out_weight_ref[k]),
            dot_nt(chunk, cond_ref[k]),
        )
        for columns, part in zip((slice(0, 256), slice(256, 512), slice(512, 736)), parts):
            acc_ref[:, columns] = part if k == 0 else acc_ref[:, columns] + part
        squares_ref[...] = squares if k == 0 else squares_ref[...] + squares
    wait(start([(acc_ref, acc_hbm), (squares_ref, squares_hbm)], out_sem))


def project_last(count, index_ref, *refs):
    hiddens_hbm, cots_hbm, refs = refs[:count], refs[count : 2 * count], refs[2 * count :]
    acc_hbm, squares_hbm, query_hbm, cond_hbm, out_hbm, sent_hbm, inverse_hbm = refs[:7]
    hidden_ref, cot_ref, acc_ref, squares_ref, query_ref, cond_ref, out_weight_ref = refs[7:14]
    sent_ref, inverse_ref, sem, acc_sem, out_sem = refs[14:]
    before = start([(acc_hbm, acc_ref), (squares_hbm, squares_ref)], acc_sem)
    copies = []
    for k in range(count):
        at = pl.ds(pl.multiple_of(index_ref[k] * FEAT, FEAT), FEAT)
        copies.append(
            start(
                [
                    (hiddens_hbm[k], hidden_ref.at[k]), (query_hbm.at[at], query_ref.at[k]),
                    (cond_hbm.at[:, at], cond_ref.at[k]), (cots_hbm[k], cot_ref.at[k]),
                    (out_hbm.at[:, at], out_weight_ref.at[k]),
                ], sem.at[k],
            )
        )
    wait(before)
    for k in range(count):
        wait(copies[k])
        chunk = hidden_ref[k]
        squares_ref[...] += jnp.sum(jnp.square(chunk.astype(F32)), axis=-1, keepdims=True)
        if k < count - 1:
            acc_ref[:, 0:256] += dot(chunk, query_ref[k])
            acc_ref[:, 256:512] += dot_nt(cot_ref[k], out_weight_ref[k])
            acc_ref[:, 512:736] += dot_nt(chunk, cond_ref[k])
    inverse = lax.rsqrt(squares_ref[...] / D + epsilon)
    inverse_ref[...] = inverse
    outs = start([(inverse_ref, inverse_hbm)], out_sem.at[pl.ds(0, 1)])
    k = count - 1
    queries = (acc_ref[:, :256] + dot(chunk, query_ref[k])) * inverse
    sent_ref[:SEGS, :, 0:256] = queries.astype(BF).reshape(SEGS, SEG, -1)
    grads = acc_ref[:, 256:512] + dot_nt(cot_ref[k], out_weight_ref[k])
    sent_ref[:SEGS, :, 256:512] = grads.astype(BF).reshape(SEGS, SEG, -1)
    condition = (acc_ref[:, 512:736] + dot_nt(chunk, cond_ref[k])) * inverse
    sent_ref[:SEGS, :, 512:736] = condition.astype(BF).reshape(SEGS, SEG, -1)
    sent_ref[:, :, 736:] = jnp.zeros((NZ, SEG, 32), BF)
    sent_ref[SEGS, :, :736] = jnp.zeros((SEG, 736), BF)
    wait(start([(sent_ref, sent_hbm)], out_sem.at[pl.ds(1, 1)]) + outs)


def attention(
    fetched_hbm, enc_q_hbm, got_hbm, enc_out_hbm, weights_hbm, out_ref,
    fetched_ref, enc_q_ref, got_ref, enc_out_ref, kv_ref, key_ref, value_ref, mixed_ref, sem,
):
    small = start(
        [
            (got_hbm, got_ref), (enc_q_hbm, enc_q_ref),
            (fetched_hbm, fetched_ref), (enc_out_hbm, enc_out_ref),
        ], sem,
    )
    large = [
        pltpu.make_async_copy(
            weights_hbm.at[:, j, pl.ds(0, 112), :], kv_ref.at[j], sem.at[4 + j]
        )
        for j in range(2)
    ]
    for copy in large:
        copy.start()
    wait(small)
    cond_keys, cond_values = (
        jnp.concatenate([got_ref[z, :, 512:736] for z in range(n, n + 4)], axis=1)
        for n in (0, 4)
    )
    for h in range(EHEADS):
        columns = slice(h * HEAD, (h + 1) * HEAD)
        exponent = jnp.exp(dot_nt(enc_q_ref[:, columns], cond_keys[:, columns]) * SCALE)
        weights = (exponent / jnp.sum(exponent, axis=-1, keepdims=True)).astype(BF)
        mixed_ref[:, columns] = dot(weights, cond_values[:, columns]).astype(BF)
    encoded = (fetched_ref[...].astype(F32) + dot(mixed_ref[...], enc_out_ref[...])).astype(BF)
    total = jnp.zeros((SEG, HEAD), F32)
    for j in range(2):
        large[j].wait()
        key_ref[j] = dot(encoded, kv_ref[j, 0:8].reshape(DE, HALF)).astype(BF)
        value_ref[j] = dot(encoded, kv_ref[j, 8:16].reshape(DE, HALF)).astype(BF)
        for z in range(NZ):
            columns = slice(z * HEAD, (z + 1) * HEAD)
            query = got_ref[z, :, j * HEAD : (j + 1) * HEAD]
            grad_att = got_ref[z, :, (2 + j) * HEAD : (3 + j) * HEAD]
            key, value = key_ref[j, :, columns], value_ref[j, :, columns]
            exponent = jnp.exp(dot_nt(query, key) * SCALE)
            probs = exponent / jnp.sum(exponent, axis=-1, keepdims=True)
            attended = dot(probs.astype(BF), value).astype(BF)
            delta = jnp.sum(
                grad_att.astype(F32) * attended.astype(F32), axis=-1, keepdims=True
            )
            grad_probs = dot_nt(grad_att, value)
            grad_scores = (probs * (grad_probs - delta) * SCALE).astype(BF)
            grad_query = dot(grad_scores, key).astype(BF)
            out_ref[:, j * HALF + z * HEAD : j * HALF + (z + 1) * HEAD] = grad_query
            total = total + grad_query.astype(F32) * query.astype(F32)
    stat = jnp.sum(total, axis=-1, keepdims=True) / D
    high = stat.astype(BF)
    low = (stat - high.astype(F32)).astype(BF)
    lane = lax.broadcasted_iota(jnp.int32, (SEG, HEAD), 1)
    out_ref[:, 2 * HALF :] = jnp.where(
        lane == 0, high.astype(F32), jnp.where(lane == 1, low.astype(F32), 0.0)
    ).astype(BF)


def finish_rows(chunk_refs, hidden_ref, inverse_ref, weight_ref, source_ref, starts, out_refs, out_hbm, sem):
    rows = [c.shape[0] for c in chunk_refs]
    chunks = jnp.concatenate([c[...] for c in chunk_refs], axis=0)
    grads = sum(
        dot_nt(chunks[:, j * HALF : (j + 1) * HALF], weight_ref[j].reshape(FEAT, HALF))
        for j in range(2)
    )
    inside, copies = [], []
    for k, chunk_ref in enumerate(chunk_refs):
        source = source_ref[k]
        at = jnp.where(source < SEGS, source, 0) * SEG + starts[k]
        place = pl.ds(pl.multiple_of(at, 32), rows[k])
        grad = grads[sum(rows[:k]) : sum(rows[: k + 1])]
        tail = chunk_ref[:, 2 * HALF :].astype(F32)
        stat = tail[:, 0:1] + tail[:, 1:2]
        inverse = inverse_ref[place, :]
        out_refs[k][...] = (
            inverse * grad - hidden_ref[place, :].astype(F32) * (inverse * inverse * stat)
        ).astype(BF)
        inside.append(source < SEGS)
        copies.append(pltpu.make_async_copy(out_refs[k], out_hbm.at[place], sem.at[k]))
        pl.when(inside[k])(copies[k].start)
    for k, copy in enumerate(copies):
        pl.when(inside[k])(copy.wait)


def finish_first(
    source_ref, chunk_ref, hidden_hbm, inverse_hbm, weights_hbm,
    out_hbm, hidden_ref, inverse_ref, weight_ref, result_ref, sem, out_sem,
):
    loads = [(inverse_hbm, inverse_ref), (hidden_hbm, hidden_ref)]
    loads += [
        (weights_hbm.at[:, pl.ds(112 + 16 * j, 16), :], weight_ref.at[j]) for j in range(2)
    ]
    wait(start(loads, sem))
    finish_rows(
        [chunk_ref], hidden_ref, inverse_ref, weight_ref, source_ref, (0,), [result_ref],
        out_hbm, out_sem,
    )


def finish(starts, source_ref, *refs):
    count = len(starts)
    chunk_refs, refs = refs[:count], refs[count:]
    hidden_ref, inverse_ref, weight_ref, _, out_hbm = refs[:5]
    result_refs, sem = refs[5 : 5 + count], refs[5 + count]
    finish_rows(
        chunk_refs, hidden_ref, inverse_ref, weight_ref, source_ref, starts, result_refs,
        out_hbm, sem,
    )


def finish_call(chunks, starts, sources, held, previous):
    rows = [c.shape[0] for c in chunks]
    operands = [sources, *chunks, *held, previous]
    return pl.pallas_call(
        functools.partial(finish, starts),
        out_shape=jax.ShapeDtypeStruct((TOK, FEAT), BF),
        in_specs=[SMEM] + [VMEM] * (len(chunks) + 3) + [ANY],
        out_specs=ANY,
        scratch_shapes=[pltpu.VMEM((r, FEAT), BF) for r in rows]
        + [pltpu.SemaphoreType.DMA((len(chunks),))],
        input_output_aliases={len(operands) - 1: 0},
        compiler_params=SMALL,
        cost_estimate=cost(2 * sum(rows) * FEAT * 2048, 4_000_000),
        name="finish",
    )(*operands)


def shards(
    hidden,
    cotangent,
    query_weight,
    out_weight,
    condition_weight,
    key_value_weight,
    encoder_query,
    encoder_out,
    database,
    neighbours,
    owners,
):
    me = lax.axis_index(Z)
    mine = lax.axis_index("dp")

    owner = owners[:, 0]
    selector = owner[None, :] == jnp.arange(NDP, dtype=jnp.int32)[:, None]
    wanted = jnp.sum(selector.astype(jnp.int32)[:, :, None] * neighbours[None, :, :], axis=1)
    kv_part = lax.dynamic_slice(
        key_value_weight.reshape(2 * DE, 2 * HEAD),
        (mine // 2 * 112, mine % 2 * HEAD),
        (112, HEAD),
    )
    q_part = lax.dynamic_slice(
        query_weight.reshape(NZ, FEAT, 2 * HEAD), (0, mine * 16, 0), (NZ, 16, 2 * HEAD)
    )
    q_part = q_part.reshape(NZ, 16, 2, HEAD).transpose(0, 2, 1, 3).reshape(NZ, 32, HEAD)
    part = jnp.concatenate([jnp.broadcast_to(kv_part, (NZ, 112, HEAD)), q_part], axis=1)

    asked = exchange(wanted, "dp")
    part = exchange(part, Z)

    projections = (query_weight, condition_weight.T, out_weight)
    right = left = hidden
    grad_right = grad_left = cotangent
    index, chunks, grad_chunks = [me], [hidden], [cotangent]
    for step in range(1, 4):
        right, left = shift(right, 1), shift(left, -1)
        grad_right, grad_left = shift(grad_right, 1), shift(grad_left, -1)
        if step == 1:
            part, right, left, grad_right, grad_left, asked = tie(
                part, right, left, grad_right, grad_left, asked
            )
        index += [(me - step) % NZ, (me + step) % NZ]
        chunks += [right, left]
        grad_chunks += [grad_right, grad_left]
    part = part.transpose(1, 0, 2).reshape(144, HALF)
    weights = lax.all_gather(part, "dp", axis=0, tiled=True).reshape(16, 2, 144, HALF)
    returned = exchange(database[asked].reshape(NDP, NEIGH * NLEN // NZ, DE), "dp")
    chosen = returned[jnp.concatenate([owner, owner[:1]])]
    early = 5
    acc, squares = pl.pallas_call(
        functools.partial(project, early),
        out_shape=(
            jax.ShapeDtypeStruct((TOK, 768), F32),
            jax.ShapeDtypeStruct((TOK, 1), F32),
        ),
        in_specs=[SMEM] + [ANY] * (2 * early + 3),
        out_specs=(ANY, ANY),
        scratch_shapes=[
            pltpu.VMEM((early, TOK, FEAT), BF),
            pltpu.VMEM((early, TOK, FEAT), BF),
            pltpu.VMEM((early, FEAT, 256), BF),
            pltpu.VMEM((early, 224, FEAT), BF),
            pltpu.VMEM((early, 256, FEAT), BF),
            pltpu.VMEM((TOK, 768), F32),
            pltpu.VMEM((TOK, 1), F32),
            pltpu.SemaphoreType.DMA((early, 5)),
            pltpu.SemaphoreType.DMA((2,)),
        ],
        compiler_params=ROOM,
        cost_estimate=cost(2 * early * TOK * FEAT * 736, 16_000_000),
        name="project",
    )(jnp.stack(index[:early]), *chunks[:early], *grad_chunks[:early], *projections)

    right, acc, chosen = tie(right, acc, chosen)
    chunks[5] = right
    fetched = exchange(chosen, Z).reshape(KEYS, DE)
    far = (shift(right, 1), shift(grad_left, -1))
    enc_q = pl.pallas_call(
        encoder_queries,
        out_shape=jax.ShapeDtypeStruct((KEYS, DE), BF),
        in_specs=[ANY, ANY],
        out_specs=ANY,
        scratch_shapes=[
            like(fetched), like(encoder_query), like(fetched), pltpu.SemaphoreType.DMA((3,))
        ],
        compiler_params=PARAMS,
        cost_estimate=cost(2 * KEYS * DE * DE, 3_000_000),
        name="encoder_queries",
    )(fetched, encoder_query)
    hiddens, cots = (*chunks[5:], far[0]), (*grad_chunks[5:], far[1])
    index = index[5:] + [(me + 4) % NZ]
    sent, inverse = pl.pallas_call(
        functools.partial(project_last, len(hiddens)),
        out_shape=(
            jax.ShapeDtypeStruct((NZ, SEG, 768), BF),
            jax.ShapeDtypeStruct((TOK, 1), F32),
        ),
        in_specs=[SMEM] + [ANY] * (2 * len(hiddens) + 5),
        out_specs=(ANY, ANY),
        scratch_shapes=[
            pltpu.VMEM((len(hiddens), TOK, FEAT), BF),
            pltpu.VMEM((len(hiddens), TOK, FEAT), BF),
            like(acc),
            like(squares),
            pltpu.VMEM((len(hiddens), FEAT, 256), BF),
            pltpu.VMEM((len(hiddens), 224, FEAT), BF),
            pltpu.VMEM((len(hiddens), 256, FEAT), BF),
            pltpu.VMEM((NZ, SEG, 768), BF),
            like(squares),
            pltpu.SemaphoreType.DMA((len(hiddens), 5)),
            pltpu.SemaphoreType.DMA((2,)),
            pltpu.SemaphoreType.DMA((2,)),
        ],
        compiler_params=ROOM,
        cost_estimate=cost(KNOB, 4_000_000),
        name="project_last",
    )(jnp.stack(index), *hiddens, *cots, acc, squares, *projections)
    got = exchange(sent, Z)
    operands = (fetched, enc_q, got, encoder_out)
    grad_query = pl.pallas_call(
        attention,
        out_shape=jax.ShapeDtypeStruct((SEG, 2 * HALF + HEAD), BF),
        in_specs=[ANY] * 5,
        out_specs=VMEM,
        scratch_shapes=[like(x) for x in operands]
        + [
            pltpu.VMEM((2, 16, 112, HALF), BF),
            pltpu.VMEM((2, KEYS, HALF), BF),
            pltpu.VMEM((2, KEYS, HALF), BF),
            pltpu.VMEM((KEYS, DE), BF),
            pltpu.SemaphoreType.DMA((6,)),
        ],
        compiler_params=PARAMS,
        cost_estimate=cost(4_000_000_000, 12_000_000),
        name="attention",
    )(*operands, weights)

    results = (
        jax.ShapeDtypeStruct((TOK, FEAT), BF),
        jax.ShapeDtypeStruct((TOK, FEAT), BF),
        jax.ShapeDtypeStruct((TOK, 1), F32),
        jax.ShapeDtypeStruct((2, NDP, 16, HALF), BF),
    )
    out, *held = pl.pallas_call(
        finish_first,
        out_shape=results,
        in_specs=[SMEM, VMEM, ANY, ANY, ANY],
        out_specs=(ANY, VMEM, VMEM, VMEM),
        scratch_shapes=[
            pltpu.VMEM((SEG, FEAT), BF),
            pltpu.SemaphoreType.DMA((4,)),
            pltpu.SemaphoreType.DMA((1,)),
        ],
        compiler_params=ROOM,
        cost_estimate=cost(2 * SEG * FEAT * 2048, 4_000_000),
        name="finish_first",
    )(jnp.stack([me]), grad_query, hidden, inverse, weights.reshape(NDP, 144, HALF))

    right = left = grad_query
    for step in range(1, 4):
        right, left = shift(right, 1), shift(left, -1)
        if step > 1:
            out = finish_call(*group, held, out)
        right, left, out = tie(right, left, out)
        group = [right, left], (0, 0), jnp.stack([(me - step) % NZ, (me + step) % NZ])
    far = [shift(right[: SEG // 2], 1), shift(left[SEG // 2 :], -1)]
    out = finish_call(*group, held, out)
    return finish_call(far, (0, SEG // 2), jnp.stack([(me + 4) % NZ] * 2), held, out)


def solution(mesh):
    return jax.shard_map(
        shards,
        mesh=mesh,
        in_specs=(
            P("dp", Z),
            P("dp", Z),
            P(None, Z),
            P(Z, None),
            P(None, Z),
            P(None, None, Z),
            P(),
            P(),
            P("dp", Z, None),
            P("dp", None),
            P("dp", None),
        ),
        out_specs=P("dp", Z),
        check_vma=False,
    )
```

```python
import functools

import jax
import jax.numpy as jnp
from jax import lax
from jax.experimental import pallas as pl
from jax.experimental.pallas import tpu as pltpu
from jax.sharding import PartitionSpec as P

D = 4096
HEAD = 128
DE = 896
EHEADS = 7
SEG = 64
NLEN = 128
NEIGH = 2
KEYS = NLEN * NEIGH
NZ = 8
NDP = 32
SEGS = 7
FEAT = D // NZ
TOK = SEGS * SEG
HALF = 8 * HEAD
SCALE = HEAD**-0.5
epsilon = 1e-05
Z = ("group", "tensor")
BF = jnp.bfloat16
F32 = jnp.float32
MIB = 1024 * 1024
KNOB = 20_000_000_000
PARAMS = pltpu.CompilerParams(vmem_limit_bytes=59 * MIB)
SMALL = pltpu.CompilerParams(vmem_limit_bytes=24 * MIB)
ROOM = pltpu.CompilerParams(vmem_limit_bytes=53 * MIB + MIB // 2)
VMEM = pl.BlockSpec(memory_space=pltpu.VMEM)
SMEM = pl.BlockSpec(memory_space=pltpu.SMEM)
ANY = pl.BlockSpec(memory_space=pl.ANY)
NT = (((1,), (1,)), ((), ()))


def dot(a, b):
    return jnp.dot(a, b, preferred_element_type=F32)


def dot_nt(a, b):
    return lax.dot_general(a, b, NT, preferred_element_type=F32)


def shift(x, by):
    return lax.ppermute(x, Z, [(i, (i + by) % NZ) for i in range(NZ)])


def tie(*arrays):
    return lax.optimization_barrier(arrays)


def exchange(x, axis):
    return lax.all_to_all(x, axis, split_axis=0, concat_axis=0, tiled=True)


def start(pairs, sem):
    copies = [pltpu.make_async_copy(a, b, sem.at[i]) for i, (a, b) in enumerate(pairs)]
    for copy in copies:
        copy.start()
    return copies


def wait(copies):
    for copy in copies:
        copy.wait()


def cost(flops, size):
    return pl.CostEstimate(flops=flops, bytes_accessed=size, transcendentals=0)


def like(x):
    return pltpu.VMEM(x.shape, x.dtype)


def encoder_queries(fetched_hbm, weight_hbm, out_hbm, fetched_ref, weight_ref, out_ref, sem):
    copies = start([(fetched_hbm, fetched_ref), (weight_hbm, weight_ref)], sem)
    copies[0].wait()
    rows = fetched_ref[...].astype(F32)
    inverse = lax.rsqrt(jnp.mean(rows * rows, axis=-1, keepdims=True) + epsilon)
    normed = (rows * inverse).astype(BF)
    copies[1].wait()
    out_ref[...] = dot(normed, weight_ref[...]).astype(BF)
    wait(start([(out_ref, out_hbm)], sem.at[pl.ds(2, 1)]))


def project(count, index_ref, *refs):
    hiddens_hbm, cots_hbm, refs = refs[:count], refs[count : 2 * count], refs[2 * count :]
    query_hbm, cond_hbm, out_hbm, acc_hbm, squares_hbm = refs[:5]
    hidden_ref, cot_ref, query_ref, cond_ref, out_weight_ref = refs[5:10]
    acc_ref, squares_ref, sem, out_sem = refs[10:]
    copies = []
    for k in range(count):
        at = pl.ds(pl.multiple_of(index_ref[k] * FEAT, FEAT), FEAT)
        copies.append(
            start(
                [
                    (hiddens_hbm[k], hidden_ref.at[k]), (query_hbm.at[at], query_ref.at[k]),
                    (cond_hbm.at[:, at], cond_ref.at[k]), (cots_hbm[k], cot_ref.at[k]),
                    (out_hbm.at[:, at], out_weight_ref.at[k]),
                ], sem.at[k],
            )
        )
    for k in range(count):
        wait(copies[k])
        chunk = hidden_ref[k]
        squares = jnp.sum(jnp.square(chunk.astype(F32)), axis=-1, keepdims=True)
        parts = (
            dot(chunk, query_ref[k]),
            dot_nt(cot_ref[k], out_weight_ref[k]),
            dot_nt(chunk, cond_ref[k]),
        )
        for columns, part in zip((slice(0, 256), slice(256, 512), slice(512, 736)), parts):
            acc_ref[:, columns] = part if k == 0 else acc_ref[:, columns] + part
        squares_ref[...] = squares if k == 0 else squares_ref[...] + squares
    wait(start([(acc_ref, acc_hbm), (squares_ref, squares_hbm)], out_sem))


def project_last(count, index_ref, *refs):
    hiddens_hbm, cots_hbm, refs = refs[:count], refs[count : 2 * count], refs[2 * count :]
    acc_hbm, squares_hbm, query_hbm, cond_hbm, out_hbm, sent_hbm, inverse_hbm = refs[:7]
    hidden_ref, cot_ref, acc_ref, squares_ref, query_ref, cond_ref, out_weight_ref = refs[7:14]
    sent_ref, inverse_ref, sem, acc_sem, out_sem = refs[14:]
    before = start([(acc_hbm, acc_ref), (squares_hbm, squares_ref)], acc_sem)
    copies = []
    for k in range(count):
        at = pl.ds(pl.multiple_of(index_ref[k] * FEAT, FEAT), FEAT)
        copies.append(
            start(
                [
                    (hiddens_hbm[k], hidden_ref.at[k]), (query_hbm.at[at], query_ref.at[k]),
                    (cond_hbm.at[:, at], cond_ref.at[k]), (cots_hbm[k], cot_ref.at[k]),
                    (out_hbm.at[:, at], out_weight_ref.at[k]),
                ], sem.at[k],
            )
        )
    wait(before)
    for k in range(count):
        wait(copies[k])
        chunk = hidden_ref[k]
        squares_ref[...] += jnp.sum(jnp.square(chunk.astype(F32)), axis=-1, keepdims=True)
        if k < count - 1:
            acc_ref[:, 0:256] += dot(chunk, query_ref[k])
            acc_ref[:, 256:512] += dot_nt(cot_ref[k], out_weight_ref[k])
            acc_ref[:, 512:736] += dot_nt(chunk, cond_ref[k])
    inverse = lax.rsqrt(squares_ref[...] / D + epsilon)
    inverse_ref[...] = inverse
    outs = start([(inverse_ref, inverse_hbm)], out_sem.at[pl.ds(0, 1)])
    k = count - 1
    queries = (acc_ref[:, :256] + dot(chunk, query_ref[k])) * inverse
    sent_ref[:SEGS, :, 0:256] = queries.astype(BF).reshape(SEGS, SEG, -1)
    grads = acc_ref[:, 256:512] + dot_nt(cot_ref[k], out_weight_ref[k])
    sent_ref[:SEGS, :, 256:512] = grads.astype(BF).reshape(SEGS, SEG, -1)
    condition = (acc_ref[:, 512:736] + dot_nt(chunk, cond_ref[k])) * inverse
    sent_ref[:SEGS, :, 512:736] = condition.astype(BF).reshape(SEGS, SEG, -1)
    sent_ref[:, :, 736:] = jnp.zeros((NZ, SEG, 32), BF)
    sent_ref[SEGS, :, :736] = jnp.zeros((SEG, 736), BF)
    wait(start([(sent_ref, sent_hbm)], out_sem.at[pl.ds(1, 1)]) + outs)


def attention(
    fetched_hbm, enc_q_hbm, got_hbm, enc_out_hbm, weights_hbm, out_ref,
    fetched_ref, enc_q_ref, got_ref, enc_out_ref, kv_ref, key_ref, value_ref, mixed_ref, sem,
):
    small = start(
        [
            (got_hbm, got_ref), (enc_q_hbm, enc_q_ref),
            (fetched_hbm, fetched_ref), (enc_out_hbm, enc_out_ref),
        ], sem,
    )
    large = [
        pltpu.make_async_copy(
            weights_hbm.at[:, j, pl.ds(0, 112), :], kv_ref.at[j], sem.at[4 + j]
        )
        for j in range(2)
    ]
    for copy in large:
        copy.start()
    wait(small)
    cond_keys, cond_values = (
        jnp.concatenate([got_ref[z, :, 512:736] for z in range(n, n + 4)], axis=1)
        for n in (0, 4)
    )
    for h in range(EHEADS):
        columns = slice(h * HEAD, (h + 1) * HEAD)
        exponent = jnp.exp(dot_nt(enc_q_ref[:, columns], cond_keys[:, columns]) * SCALE)
        weights = (exponent / jnp.sum(exponent, axis=-1, keepdims=True)).astype(BF)
        mixed_ref[:, columns] = dot(weights, cond_values[:, columns]).astype(BF)
    encoded = (fetched_ref[...].astype(F32) + dot(mixed_ref[...], enc_out_ref[...])).astype(BF)
    total = jnp.zeros((SEG, HEAD), F32)
    for j in range(2):
        large[j].wait()
        key_ref[j] = dot(encoded, kv_ref[j, 0:8].reshape(DE, HALF)).astype(BF)
        value_ref[j] = dot(encoded, kv_ref[j, 8:16].reshape(DE, HALF)).astype(BF)
        for z in range(NZ):
            columns = slice(z * HEAD, (z + 1) * HEAD)
            query = got_ref[z, :, j * HEAD : (j + 1) * HEAD]
            grad_att = got_ref[z, :, (2 + j) * HEAD : (3 + j) * HEAD]
            key, value = key_ref[j, :, columns], value_ref[j, :, columns]
            exponent = jnp.exp(dot_nt(query, key) * SCALE)
            probs = exponent / jnp.sum(exponent, axis=-1, keepdims=True)
            attended = dot(probs.astype(BF), value).astype(BF)
            delta = jnp.sum(
                grad_att.astype(F32) * attended.astype(F32), axis=-1, keepdims=True
            )
            grad_probs = dot_nt(grad_att, value)
            grad_scores = (probs * (grad_probs - delta) * SCALE).astype(BF)
            grad_query = dot(grad_scores, key).astype(BF)
            out_ref[:, j * HALF + z * HEAD : j * HALF + (z + 1) * HEAD] = grad_query
            total = total + grad_query.astype(F32) * query.astype(F32)
    stat = jnp.sum(total, axis=-1, keepdims=True) / D
    high = stat.astype(BF)
    low = (stat - high.astype(F32)).astype(BF)
    lane = lax.broadcasted_iota(jnp.int32, (SEG, HEAD), 1)
    out_ref[:, 2 * HALF :] = jnp.where(
        lane == 0, high.astype(F32), jnp.where(lane == 1, low.astype(F32), 0.0)
    ).astype(BF)


def finish_rows(chunk_refs, hidden_ref, inverse_ref, weight_ref, source_ref, starts, out_refs, out_hbm, sem):
    rows = [c.shape[0] for c in chunk_refs]
    chunks = jnp.concatenate([c[...] for c in chunk_refs], axis=0)
    grads = sum(
        dot_nt(chunks[:, j * HALF : (j + 1) * HALF], weight_ref[j].reshape(FEAT, HALF))
        for j in range(2)
    )
    inside, copies = [], []
    for k, chunk_ref in enumerate(chunk_refs):
        source = source_ref[k]
        at = jnp.where(source < SEGS, source, 0) * SEG + starts[k]
        place = pl.ds(pl.multiple_of(at, 32), rows[k])
        grad = grads[sum(rows[:k]) : sum(rows[: k + 1])]
        tail = chunk_ref[:, 2 * HALF :].astype(F32)
        stat = tail[:, 0:1] + tail[:, 1:2]
        inverse = inverse_ref[place, :]
        out_refs[k][...] = (
            inverse * grad - hidden_ref[place, :].astype(F32) * (inverse * inverse * stat)
        ).astype(BF)
        inside.append(source < SEGS)
        copies.append(pltpu.make_async_copy(out_refs[k], out_hbm.at[place], sem.at[k]))
        pl.when(inside[k])(copies[k].start)
    for k, copy in enumerate(copies):
        pl.when(inside[k])(copy.wait)


def finish_first(
    source_ref, chunk_ref, hidden_hbm, inverse_hbm, weights_hbm,
    out_hbm, hidden_ref, inverse_ref, weight_ref, result_ref, sem, out_sem,
):
    loads = [(inverse_hbm, inverse_ref), (hidden_hbm, hidden_ref)]
    loads += [
        (weights_hbm.at[:, pl.ds(112 + 16 * j, 16), :], weight_ref.at[j]) for j in range(2)
    ]
    wait(start(loads, sem))
    finish_rows(
        [chunk_ref], hidden_ref, inverse_ref, weight_ref, source_ref, (0,), [result_ref],
        out_hbm, out_sem,
    )


def finish(starts, source_ref, *refs):
    count = len(starts)
    chunk_refs, refs = refs[:count], refs[count:]
    hidden_ref, inverse_ref, weight_ref, _, out_hbm = refs[:5]
    result_refs, sem = refs[5 : 5 + count], refs[5 + count]
    finish_rows(
        chunk_refs, hidden_ref, inverse_ref, weight_ref, source_ref, starts, result_refs,
        out_hbm, sem,
    )


def finish_call(chunks, starts, sources, held, previous):
    rows = [c.shape[0] for c in chunks]
    operands = [sources, *chunks, *held, previous]
    return pl.pallas_call(
        functools.partial(finish, starts),
        out_shape=jax.ShapeDtypeStruct((TOK, FEAT), BF),
        in_specs=[SMEM] + [VMEM] * (len(chunks) + 3) + [ANY],
        out_specs=ANY,
        scratch_shapes=[pltpu.VMEM((r, FEAT), BF) for r in rows]
        + [pltpu.SemaphoreType.DMA((len(chunks),))],
        input_output_aliases={len(operands) - 1: 0},
        compiler_params=SMALL,
        cost_estimate=cost(2 * sum(rows) * FEAT * 2048, 4_000_000),
        name="finish",
    )(*operands)


def shards(
    hidden,
    cotangent,
    query_weight,
    out_weight,
    condition_weight,
    key_value_weight,
    encoder_query,
    encoder_out,
    database,
    neighbours,
    owners,
):
    me = lax.axis_index(Z)
    mine = lax.axis_index("dp")

    owner = owners[:, 0]
    selector = owner[None, :] == jnp.arange(NDP, dtype=jnp.int32)[:, None]
    wanted = jnp.sum(selector.astype(jnp.int32)[:, :, None] * neighbours[None, :, :], axis=1)
    kv_part = lax.dynamic_slice(
        key_value_weight.reshape(2 * DE, 2 * HEAD),
        (mine // 2 * 112, mine % 2 * HEAD),
        (112, HEAD),
    )
    q_part = lax.dynamic_slice(
        query_weight.reshape(NZ, FEAT, 2 * HEAD), (0, mine * 16, 0), (NZ, 16, 2 * HEAD)
    )
    q_part = q_part.reshape(NZ, 16, 2, HEAD).transpose(0, 2, 1, 3).reshape(NZ, 32, HEAD)
    part = jnp.concatenate([jnp.broadcast_to(kv_part, (NZ, 112, HEAD)), q_part], axis=1)

    asked = exchange(wanted, "dp")
    part = exchange(part, Z)

    projections = (query_weight, condition_weight.T, out_weight)
    right = left = hidden
    grad_right = grad_left = cotangent
    index, chunks, grad_chunks = [me], [hidden], [cotangent]
    for step in range(1, 4):
        right, left = shift(right, 1), shift(left, -1)
        grad_right, grad_left = shift(grad_right, 1), shift(grad_left, -1)
        if step == 1:
            right, left, asked = tie(
                right, left, asked
            )
        index += [(me - step) % NZ, (me + step) % NZ]
        chunks += [right, left]
        grad_chunks += [grad_right, grad_left]
    part = part.transpose(1, 0, 2).reshape(144, HALF)
    weights = lax.all_gather(part, "dp", axis=0, tiled=True).reshape(16, 2, 144, HALF)
    returned = exchange(database[asked].reshape(NDP, NEIGH * NLEN // NZ, DE), "dp")
    chosen = returned[jnp.concatenate([owner, owner[:1]])]
    early = 5
    acc, squares = pl.pallas_call(
        functools.partial(project, early),
        out_shape=(
            jax.ShapeDtypeStruct((TOK, 768), F32),
            jax.ShapeDtypeStruct((TOK, 1), F32),
        ),
        in_specs=[SMEM] + [ANY] * (2 * early + 3),
        out_specs=(ANY, ANY),
        scratch_shapes=[
            pltpu.VMEM((early, TOK, FEAT), BF),
            pltpu.VMEM((early, TOK, FEAT), BF),
            pltpu.VMEM((early, FEAT, 256), BF),
            pltpu.VMEM((early, 224, FEAT), BF),
            pltpu.VMEM((early, 256, FEAT), BF),
            pltpu.VMEM((TOK, 768), F32),
            pltpu.VMEM((TOK, 1), F32),
            pltpu.SemaphoreType.DMA((early, 5)),
            pltpu.SemaphoreType.DMA((2,)),
        ],
        compiler_params=ROOM,
        cost_estimate=cost(2 * early * TOK * FEAT * 736, 16_000_000),
        name="project",
    )(jnp.stack(index[:early]), *chunks[:early], *grad_chunks[:early], *projections)

    right, acc = tie(right, acc)
    chunks[5] = right
    fetched = exchange(chosen, Z).reshape(KEYS, DE)
    far = (shift(right, 1), shift(grad_left, -1))
    enc_q = pl.pallas_call(
        encoder_queries,
        out_shape=jax.ShapeDtypeStruct((KEYS, DE), BF),
        in_specs=[ANY, ANY],
        out_specs=ANY,
        scratch_shapes=[
            like(fetched), like(encoder_query), like(fetched), pltpu.SemaphoreType.DMA((3,))
        ],
        compiler_params=PARAMS,
        cost_estimate=cost(2 * KEYS * DE * DE, 3_000_000),
        name="encoder_queries",
    )(fetched, encoder_query)
    hiddens, cots = (*chunks[5:], far[0]), (*grad_chunks[5:], far[1])
    index = index[5:] + [(me + 4) % NZ]
    sent, inverse = pl.pallas_call(
        functools.partial(project_last, len(hiddens)),
        out_shape=(
            jax.ShapeDtypeStruct((NZ, SEG, 768), BF),
            jax.ShapeDtypeStruct((TOK, 1), F32),
        ),
        in_specs=[SMEM] + [ANY] * (2 * len(hiddens) + 5),
        out_specs=(ANY, ANY),
        scratch_shapes=[
            pltpu.VMEM((len(hiddens), TOK, FEAT), BF),
            pltpu.VMEM((len(hiddens), TOK, FEAT), BF),
            like(acc),
            like(squares),
            pltpu.VMEM((len(hiddens), FEAT, 256), BF),
            pltpu.VMEM((len(hiddens), 224, FEAT), BF),
            pltpu.VMEM((len(hiddens), 256, FEAT), BF),
            pltpu.VMEM((NZ, SEG, 768), BF),
            like(squares),
            pltpu.SemaphoreType.DMA((len(hiddens), 5)),
            pltpu.SemaphoreType.DMA((2,)),
            pltpu.SemaphoreType.DMA((2,)),
        ],
        compiler_params=ROOM,
        cost_estimate=cost(KNOB, 4_000_000),
        name="project_last",
    )(jnp.stack(index), *hiddens, *cots, acc, squares, *projections)
    got = exchange(sent, Z)
    operands = (fetched, enc_q, got, encoder_out)
    grad_query = pl.pallas_call(
        attention,
        out_shape=jax.ShapeDtypeStruct((SEG, 2 * HALF + HEAD), BF),
        in_specs=[ANY] * 5,
        out_specs=VMEM,
        scratch_shapes=[like(x) for x in operands]
        + [
            pltpu.VMEM((2, 16, 112, HALF), BF),
            pltpu.VMEM((2, KEYS, HALF), BF),
            pltpu.VMEM((2, KEYS, HALF), BF),
            pltpu.VMEM((KEYS, DE), BF),
            pltpu.SemaphoreType.DMA((6,)),
        ],
        compiler_params=PARAMS,
        cost_estimate=cost(4_000_000_000, 12_000_000),
        name="attention",
    )(*operands, weights)

    results = (
        jax.ShapeDtypeStruct((TOK, FEAT), BF),
        jax.ShapeDtypeStruct((TOK, FEAT), BF),
        jax.ShapeDtypeStruct((TOK, 1), F32),
        jax.ShapeDtypeStruct((2, NDP, 16, HALF), BF),
    )
    out, *held = pl.pallas_call(
        finish_first,
        out_shape=results,
        in_specs=[SMEM, VMEM, ANY, ANY, ANY],
        out_specs=(ANY, VMEM, VMEM, VMEM),
        scratch_shapes=[
            pltpu.VMEM((SEG, FEAT), BF),
            pltpu.SemaphoreType.DMA((4,)),
            pltpu.SemaphoreType.DMA((1,)),
        ],
        compiler_params=ROOM,
        cost_estimate=cost(2 * SEG * FEAT * 2048, 4_000_000),
        name="finish_first",
    )(jnp.stack([me]), grad_query, hidden, inverse, weights.reshape(NDP, 144, HALF))

    right = left = grad_query
    for step in range(1, 4):
        right, left = shift(right, 1), shift(left, -1)
        if step > 1:
            out = finish_call(*group, held, out)
        right, left, out = tie(right, left, out)
        group = [right, left], (0, 0), jnp.stack([(me - step) % NZ, (me + step) % NZ])
    far = [shift(right[: SEG // 2], 1), shift(left[SEG // 2 :], -1)]
    out = finish_call(*group, held, out)
    return finish_call(far, (0, SEG // 2), jnp.stack([(me + 4) % NZ] * 2), held, out)


def solution(mesh):
    return jax.shard_map(
        shards,
        mesh=mesh,
        in_specs=(
            P("dp", Z),
            P("dp", Z),
            P(None, Z),
            P(Z, None),
            P(None, Z),
            P(None, None, Z),
            P(),
            P(),
            P("dp", Z, None),
            P("dp", None),
            P("dp", None),
        ),
        out_specs=P("dp", Z),
        check_vma=False,
    )
```

```python
import functools

import jax
import jax.numpy as jnp
from jax import lax
from jax.experimental import pallas as pl
from jax.experimental.pallas import tpu as pltpu
from jax.sharding import PartitionSpec as P

D = 4096
HEAD = 128
DE = 896
EHEADS = 7
SEG = 64
NLEN = 128
NEIGH = 2
KEYS = NLEN * NEIGH
NZ = 8
NDP = 32
SEGS = 7
FEAT = D // NZ
TOK = SEGS * SEG
HALF = 8 * HEAD
SCALE = HEAD**-0.5
epsilon = 1e-05
Z = ("group", "tensor")
BF = jnp.bfloat16
F32 = jnp.float32
MIB = 1024 * 1024
KNOB = 20_000_000_000
PARAMS = pltpu.CompilerParams(vmem_limit_bytes=59 * MIB)
SMALL = pltpu.CompilerParams(vmem_limit_bytes=24 * MIB)
ROOM = pltpu.CompilerParams(vmem_limit_bytes=53 * MIB + MIB // 2)
VMEM = pl.BlockSpec(memory_space=pltpu.VMEM)
SMEM = pl.BlockSpec(memory_space=pltpu.SMEM)
ANY = pl.BlockSpec(memory_space=pl.ANY)
NT = (((1,), (1,)), ((), ()))


def dot(a, b):
    return jnp.dot(a, b, preferred_element_type=F32)


def dot_nt(a, b):
    return lax.dot_general(a, b, NT, preferred_element_type=F32)


def shift(x, by):
    return lax.ppermute(x, Z, [(i, (i + by) % NZ) for i in range(NZ)])


def tie(*arrays):
    return lax.optimization_barrier(arrays)


def exchange(x, axis):
    return lax.all_to_all(x, axis, split_axis=0, concat_axis=0, tiled=True)


def start(pairs, sem):
    copies = [pltpu.make_async_copy(a, b, sem.at[i]) for i, (a, b) in enumerate(pairs)]
    for copy in copies:
        copy.start()
    return copies


def wait(copies):
    for copy in copies:
        copy.wait()


def cost(flops, size):
    return pl.CostEstimate(flops=flops, bytes_accessed=size, transcendentals=0)


def like(x):
    return pltpu.VMEM(x.shape, x.dtype)


def encoder_queries(fetched_hbm, weight_hbm, out_hbm, fetched_ref, weight_ref, out_ref, sem):
    copies = start([(fetched_hbm, fetched_ref), (weight_hbm, weight_ref)], sem)
    copies[0].wait()
    rows = fetched_ref[...].astype(F32)
    inverse = lax.rsqrt(jnp.mean(rows * rows, axis=-1, keepdims=True) + epsilon)
    normed = (rows * inverse).astype(BF)
    copies[1].wait()
    out_ref[...] = dot(normed, weight_ref[...]).astype(BF)
    wait(start([(out_ref, out_hbm)], sem.at[pl.ds(2, 1)]))


def project(count, index_ref, *refs):
    hiddens_hbm, cots_hbm, refs = refs[:count], refs[count : 2 * count], refs[2 * count :]
    query_hbm, cond_hbm, out_hbm, acc_hbm, squares_hbm = refs[:5]
    hidden_ref, cot_ref, query_ref, cond_ref, out_weight_ref = refs[5:10]
    acc_ref, squares_ref, sem, out_sem = refs[10:]
    copies = []
    for k in range(count):
        at = pl.ds(pl.multiple_of(index_ref[k] * FEAT, FEAT), FEAT)
        copies.append(
            start(
                [
                    (hiddens_hbm[k], hidden_ref.at[k]), (query_hbm.at[at], query_ref.at[k]),
                    (cond_hbm.at[:, at], cond_ref.at[k]), (cots_hbm[k], cot_ref.at[k]),
                    (out_hbm.at[:, at], out_weight_ref.at[k]),
                ], sem.at[k],
            )
        )
    for k in range(count):
        wait(copies[k])
        chunk = hidden_ref[k]
        squares = jnp.sum(jnp.square(chunk.astype(F32)), axis=-1, keepdims=True)
        parts = (
            dot(chunk, query_ref[k]),
            dot_nt(cot_ref[k], out_weight_ref[k]),
            dot_nt(chunk, cond_ref[k]),
        )
        for columns, part in zip((slice(0, 256), slice(256, 512), slice(512, 736)), parts):
            acc_ref[:, columns] = part if k == 0 else acc_ref[:, columns] + part
        squares_ref[...] = squares if k == 0 else squares_ref[...] + squares
    wait(start([(acc_ref, acc_hbm), (squares_ref, squares_hbm)], out_sem))


def project_last(count, index_ref, *refs):
    hiddens_hbm, cots_hbm, refs = refs[:count], refs[count : 2 * count], refs[2 * count :]
    acc_hbm, squares_hbm, query_hbm, cond_hbm, out_hbm, sent_hbm, inverse_hbm = refs[:7]
    hidden_ref, cot_ref, acc_ref, squares_ref, query_ref, cond_ref, out_weight_ref = refs[7:14]
    sent_ref, inverse_ref, sem, acc_sem, out_sem = refs[14:]
    before = start([(acc_hbm, acc_ref), (squares_hbm, squares_ref)], acc_sem)
    copies = []
    for k in range(count):
        at = pl.ds(pl.multiple_of(index_ref[k] * FEAT, FEAT), FEAT)
        copies.append(
            start(
                [
                    (hiddens_hbm[k], hidden_ref.at[k]), (query_hbm.at[at], query_ref.at[k]),
                    (cond_hbm.at[:, at], cond_ref.at[k]), (cots_hbm[k], cot_ref.at[k]),
                    (out_hbm.at[:, at], out_weight_ref.at[k]),
                ], sem.at[k],
            )
        )
    wait(before)
    for k in range(count):
        wait(copies[k])
        chunk = hidden_ref[k]
        squares_ref[...] += jnp.sum(jnp.square(chunk.astype(F32)), axis=-1, keepdims=True)
        if k < count - 1:
            acc_ref[:, 0:256] += dot(chunk, query_ref[k])
            acc_ref[:, 256:512] += dot_nt(cot_ref[k], out_weight_ref[k])
            acc_ref[:, 512:736] += dot_nt(chunk, cond_ref[k])
    inverse = lax.rsqrt(squares_ref[...] / D + epsilon)
    inverse_ref[...] = inverse
    outs = start([(inverse_ref, inverse_hbm)], out_sem.at[pl.ds(0, 1)])
    k = count - 1
    queries = (acc_ref[:, :256] + dot(chunk, query_ref[k])) * inverse
    sent_ref[:SEGS, :, 0:256] = queries.astype(BF).reshape(SEGS, SEG, -1)
    grads = acc_ref[:, 256:512] + dot_nt(cot_ref[k], out_weight_ref[k])
    sent_ref[:SEGS, :, 256:512] = grads.astype(BF).reshape(SEGS, SEG, -1)
    condition = (acc_ref[:, 512:736] + dot_nt(chunk, cond_ref[k])) * inverse
    sent_ref[:SEGS, :, 512:736] = condition.astype(BF).reshape(SEGS, SEG, -1)
    sent_ref[:, :, 736:] = jnp.zeros((NZ, SEG, 32), BF)
    sent_ref[SEGS, :, :736] = jnp.zeros((SEG, 736), BF)
    wait(start([(sent_ref, sent_hbm)], out_sem.at[pl.ds(1, 1)]) + outs)


def attention(
    fetched_hbm, enc_q_hbm, got_hbm, enc_out_hbm, weights_hbm, out_ref,
    fetched_ref, enc_q_ref, got_ref, enc_out_ref, kv_ref, key_ref, value_ref, mixed_ref, sem,
):
    small = start(
        [
            (got_hbm, got_ref), (enc_q_hbm, enc_q_ref),
            (fetched_hbm, fetched_ref), (enc_out_hbm, enc_out_ref),
        ], sem,
    )
    large = [
        pltpu.make_async_copy(
            weights_hbm.at[:, j, pl.ds(0, 112), :], kv_ref.at[j], sem.at[4 + j]
        )
        for j in range(2)
    ]
    for copy in large:
        copy.start()
    wait(small)
    cond_keys, cond_values = (
        jnp.concatenate([got_ref[z, :, 512:736] for z in range(n, n + 4)], axis=1)
        for n in (0, 4)
    )
    parts = [slice(h * HEAD, (h + 1) * HEAD) for h in range(EHEADS)]
    exponents = [
        jnp.exp(dot_nt(enc_q_ref[:, columns], cond_keys[:, columns]) * SCALE) for columns in parts
    ]
    weights = [(e / jnp.sum(e, axis=-1, keepdims=True)).astype(BF) for e in exponents]
    for columns, weight in zip(parts, weights):
        mixed_ref[:, columns] = dot(weight, cond_values[:, columns]).astype(BF)
    encoded = (fetched_ref[...].astype(F32) + dot(mixed_ref[...], enc_out_ref[...])).astype(BF)
    total = jnp.zeros((SEG, HEAD), F32)
    for j in range(2):
        large[j].wait()
        key_ref[j] = dot(encoded, kv_ref[j, 0:8].reshape(DE, HALF)).astype(BF)
        value_ref[j] = dot(encoded, kv_ref[j, 8:16].reshape(DE, HALF)).astype(BF)
        for group in (range(0, 4), range(4, 8)):
            queries = [got_ref[z, :, j * HEAD : (j + 1) * HEAD] for z in group]
            grads = [got_ref[z, :, (2 + j) * HEAD : (3 + j) * HEAD] for z in group]
            keys = [key_ref[j, :, z * HEAD : (z + 1) * HEAD] for z in group]
            values = [value_ref[j, :, z * HEAD : (z + 1) * HEAD] for z in group]
            exponents = [jnp.exp(dot_nt(q, k) * SCALE) for q, k in zip(queries, keys)]
            grad_probs = [dot_nt(g, v) for g, v in zip(grads, values)]
            probs = [e / jnp.sum(e, axis=-1, keepdims=True) for e in exponents]
            attended = [dot(p.astype(BF), v).astype(BF) for p, v in zip(probs, values)]
            deltas = [
                jnp.sum(g.astype(F32) * x.astype(F32), axis=-1, keepdims=True)
                for g, x in zip(grads, attended)
            ]
            grad_scores = [
                (p * (g - d) * SCALE).astype(BF) for p, g, d in zip(probs, grad_probs, deltas)
            ]
            for z, score, key, query in zip(group, grad_scores, keys, queries):
                grad_query = dot(score, key).astype(BF)
                out_ref[:, j * HALF + z * HEAD : j * HALF + (z + 1) * HEAD] = grad_query
                total = total + grad_query.astype(F32) * query.astype(F32)
    stat = jnp.sum(total, axis=-1, keepdims=True) / D
    high = stat.astype(BF)
    low = (stat - high.astype(F32)).astype(BF)
    lane = lax.broadcasted_iota(jnp.int32, (SEG, HEAD), 1)
    out_ref[:, 2 * HALF :] = jnp.where(
        lane == 0, high.astype(F32), jnp.where(lane == 1, low.astype(F32), 0.0)
    ).astype(BF)


def finish_rows(chunk_refs, hidden_ref, inverse_ref, weight_ref, source_ref, starts, out_refs, out_hbm, sem):
    rows = [c.shape[0] for c in chunk_refs]
    chunks = jnp.concatenate([c[...] for c in chunk_refs], axis=0)
    grads = sum(
        dot_nt(chunks[:, j * HALF : (j + 1) * HALF], weight_ref[j].reshape(FEAT, HALF))
        for j in range(2)
    )
    inside, copies = [], []
    for k, chunk_ref in enumerate(chunk_refs):
        source = source_ref[k]
        at = jnp.where(source < SEGS, source, 0) * SEG + starts[k]
        place = pl.ds(pl.multiple_of(at, 32), rows[k])
        grad = grads[sum(rows[:k]) : sum(rows[: k + 1])]
        tail = chunk_ref[:, 2 * HALF :].astype(F32)
        stat = tail[:, 0:1] + tail[:, 1:2]
        inverse = inverse_ref[place, :]
        out_refs[k][...] = (
            inverse * grad - hidden_ref[place, :].astype(F32) * (inverse * inverse * stat)
        ).astype(BF)
        inside.append(source < SEGS)
        copies.append(pltpu.make_async_copy(out_refs[k], out_hbm.at[place], sem.at[k]))
        pl.when(inside[k])(copies[k].start)
    for k, copy in enumerate(copies):
        pl.when(inside[k])(copy.wait)


def finish_first(
    source_ref, chunk_ref, hidden_hbm, inverse_hbm, weights_hbm,
    out_hbm, hidden_ref, inverse_ref, weight_ref, result_ref, sem, out_sem,
):
    loads = [(inverse_hbm, inverse_ref), (hidden_hbm, hidden_ref)]
    loads += [
        (weights_hbm.at[:, pl.ds(112 + 16 * j, 16), :], weight_ref.at[j]) for j in range(2)
    ]
    wait(start(loads, sem))
    finish_rows(
        [chunk_ref], hidden_ref, inverse_ref, weight_ref, source_ref, (0,), [result_ref],
        out_hbm, out_sem,
    )


def finish(starts, source_ref, *refs):
    count = len(starts)
    chunk_refs, refs = refs[:count], refs[count:]
    hidden_ref, inverse_ref, weight_ref, _, out_hbm = refs[:5]
    result_refs, sem = refs[5 : 5 + count], refs[5 + count]
    finish_rows(
        chunk_refs, hidden_ref, inverse_ref, weight_ref, source_ref, starts, result_refs,
        out_hbm, sem,
    )


def finish_call(chunks, starts, sources, held, previous):
    rows = [c.shape[0] for c in chunks]
    operands = [sources, *chunks, *held, previous]
    return pl.pallas_call(
        functools.partial(finish, starts),
        out_shape=jax.ShapeDtypeStruct((TOK, FEAT), BF),
        in_specs=[SMEM] + [VMEM] * (len(chunks) + 3) + [ANY],
        out_specs=ANY,
        scratch_shapes=[pltpu.VMEM((r, FEAT), BF) for r in rows]
        + [pltpu.SemaphoreType.DMA((len(chunks),))],
        input_output_aliases={len(operands) - 1: 0},
        compiler_params=SMALL,
        cost_estimate=cost(2 * sum(rows) * FEAT * 2048, 4_000_000),
        name="finish",
    )(*operands)


def shards(
    hidden,
    cotangent,
    query_weight,
    out_weight,
    condition_weight,
    key_value_weight,
    encoder_query,
    encoder_out,
    database,
    neighbours,
    owners,
):
    me = lax.axis_index(Z)
    mine = lax.axis_index("dp")

    owner = owners[:, 0]
    selector = owner[None, :] == jnp.arange(NDP, dtype=jnp.int32)[:, None]
    wanted = jnp.sum(selector.astype(jnp.int32)[:, :, None] * neighbours[None, :, :], axis=1)
    kv_part = lax.dynamic_slice(
        key_value_weight.reshape(2 * DE, 2 * HEAD),
        (mine // 2 * 112, mine % 2 * HEAD),
        (112, HEAD),
    )
    q_part = lax.dynamic_slice(
        query_weight.reshape(NZ, FEAT, 2 * HEAD), (0, mine * 16, 0), (NZ, 16, 2 * HEAD)
    )
    q_part = q_part.reshape(NZ, 16, 2, HEAD).transpose(0, 2, 1, 3).reshape(NZ, 32, HEAD)
    part = jnp.concatenate([jnp.broadcast_to(kv_part, (NZ, 112, HEAD)), q_part], axis=1)

    asked = exchange(wanted, "dp")
    part = exchange(part, Z)

    projections = (query_weight, condition_weight.T, out_weight)
    right = left = hidden
    grad_right = grad_left = cotangent
    index, chunks, grad_chunks = [me], [hidden], [cotangent]
    for step in range(1, 4):
        right, left = shift(right, 1), shift(left, -1)
        if step == 1:
            part, right, left = tie(part, right, left)
        grad_right, grad_left = shift(grad_right, 1), shift(grad_left, -1)
        if step == 2:
            asked, right, left = tie(asked, right, left)
        index += [(me - step) % NZ, (me + step) % NZ]
        chunks += [right, left]
        grad_chunks += [grad_right, grad_left]
    part = part.transpose(1, 0, 2).reshape(144, HALF)
    weights = lax.all_gather(part, "dp", axis=0, tiled=True).reshape(16, 2, 144, HALF)
    returned = exchange(database[asked].reshape(NDP, NEIGH * NLEN // NZ, DE), "dp")
    chosen = returned[jnp.concatenate([owner, owner[:1]])]
    early = 5
    acc, squares = pl.pallas_call(
        functools.partial(project, early),
        out_shape=(
            jax.ShapeDtypeStruct((TOK, 768), F32),
            jax.ShapeDtypeStruct((TOK, 1), F32),
        ),
        in_specs=[SMEM] + [ANY] * (2 * early + 3),
        out_specs=(ANY, ANY),
        scratch_shapes=[
            pltpu.VMEM((early, TOK, FEAT), BF),
            pltpu.VMEM((early, TOK, FEAT), BF),
            pltpu.VMEM((early, FEAT, 256), BF),
            pltpu.VMEM((early, 224, FEAT), BF),
            pltpu.VMEM((early, 256, FEAT), BF),
            pltpu.VMEM((TOK, 768), F32),
            pltpu.VMEM((TOK, 1), F32),
            pltpu.SemaphoreType.DMA((early, 5)),
            pltpu.SemaphoreType.DMA((2,)),
        ],
        compiler_params=ROOM,
        cost_estimate=cost(2 * early * TOK * FEAT * 736, 16_000_000),
        name="project",
    )(jnp.stack(index[:early]), *chunks[:early], *grad_chunks[:early], *projections)

    right, acc = tie(right, acc)
    chunks[5] = right
    fetched = exchange(chosen, Z).reshape(KEYS, DE)
    far = (shift(right, 1), shift(grad_left, -1))
    enc_q = pl.pallas_call(
        encoder_queries,
        out_shape=jax.ShapeDtypeStruct((KEYS, DE), BF),
        in_specs=[ANY, ANY],
        out_specs=ANY,
        scratch_shapes=[
            like(fetched), like(encoder_query), like(fetched), pltpu.SemaphoreType.DMA((3,))
        ],
        compiler_params=PARAMS,
        cost_estimate=cost(2 * KEYS * DE * DE, 3_000_000),
        name="encoder_queries",
    )(fetched, encoder_query)
    hiddens, cots = (*chunks[5:], far[0]), (*grad_chunks[5:], far[1])
    index = index[5:] + [(me + 4) % NZ]
    sent, inverse = pl.pallas_call(
        functools.partial(project_last, len(hiddens)),
        out_shape=(
            jax.ShapeDtypeStruct((NZ, SEG, 768), BF),
            jax.ShapeDtypeStruct((TOK, 1), F32),
        ),
        in_specs=[SMEM] + [ANY] * (2 * len(hiddens) + 5),
        out_specs=(ANY, ANY),
        scratch_shapes=[
            pltpu.VMEM((len(hiddens), TOK, FEAT), BF),
            pltpu.VMEM((len(hiddens), TOK, FEAT), BF),
            like(acc),
            like(squares),
            pltpu.VMEM((len(hiddens), FEAT, 256), BF),
            pltpu.VMEM((len(hiddens), 224, FEAT), BF),
            pltpu.VMEM((len(hiddens), 256, FEAT), BF),
            pltpu.VMEM((NZ, SEG, 768), BF),
            like(squares),
            pltpu.SemaphoreType.DMA((len(hiddens), 5)),
            pltpu.SemaphoreType.DMA((2,)),
            pltpu.SemaphoreType.DMA((2,)),
        ],
        compiler_params=ROOM,
        cost_estimate=cost(KNOB, 4_000_000),
        name="project_last",
    )(jnp.stack(index), *hiddens, *cots, acc, squares, *projections)
    got = exchange(sent, Z)
    operands = (fetched, enc_q, got, encoder_out)
    grad_query = pl.pallas_call(
        attention,
        out_shape=jax.ShapeDtypeStruct((SEG, 2 * HALF + HEAD), BF),
        in_specs=[ANY] * 5,
        out_specs=VMEM,
        scratch_shapes=[like(x) for x in operands]
        + [
            pltpu.VMEM((2, 16, 112, HALF), BF),
            pltpu.VMEM((2, KEYS, HALF), BF),
            pltpu.VMEM((2, KEYS, HALF), BF),
            pltpu.VMEM((KEYS, DE), BF),
            pltpu.SemaphoreType.DMA((6,)),
        ],
        compiler_params=PARAMS,
        cost_estimate=cost(4_000_000_000, 12_000_000),
        name="attention",
    )(*operands, weights)

    results = (
        jax.ShapeDtypeStruct((TOK, FEAT), BF),
        jax.ShapeDtypeStruct((TOK, FEAT), BF),
        jax.ShapeDtypeStruct((TOK, 1), F32),
        jax.ShapeDtypeStruct((2, NDP, 16, HALF), BF),
    )
    out, *held = pl.pallas_call(
        finish_first,
        out_shape=results,
        in_specs=[SMEM, VMEM, ANY, ANY, ANY],
        out_specs=(ANY, VMEM, VMEM, VMEM),
        scratch_shapes=[
            pltpu.VMEM((SEG, FEAT), BF),
            pltpu.SemaphoreType.DMA((4,)),
            pltpu.SemaphoreType.DMA((1,)),
        ],
        compiler_params=ROOM,
        cost_estimate=cost(2 * SEG * FEAT * 2048, 4_000_000),
        name="finish_first",
    )(jnp.stack([me]), grad_query, hidden, inverse, weights.reshape(NDP, 144, HALF))

    right = left = grad_query
    for step in range(1, 4):
        right, left = shift(right, 1), shift(left, -1)
        if step > 1:
            out = finish_call(*group, held, out)
        right, left, out = tie(right, left, out)
        group = [right, left], (0, 0), jnp.stack([(me - step) % NZ, (me + step) % NZ])
    far = [shift(right[: SEG // 2], 1), shift(left[SEG // 2 :], -1)]
    out = finish_call(*group, held, out)
    return finish_call(far, (0, SEG // 2), jnp.stack([(me + 4) % NZ] * 2), held, out)


def solution(mesh):
    return jax.shard_map(
        shards,
        mesh=mesh,
        in_specs=(
            P("dp", Z),
            P("dp", Z),
            P(None, Z),
            P(Z, None),
            P(None, Z),
            P(None, None, Z),
            P(),
            P(),
            P("dp", Z, None),
            P("dp", None),
            P("dp", None),
        ),
        out_specs=P("dp", Z),
        check_vma=False,
    )
```

```python
import functools

import jax
import jax.numpy as jnp
from jax import lax
from jax.experimental import pallas as pl
from jax.experimental.pallas import tpu as pltpu
from jax.sharding import PartitionSpec as P

D = 4096
HEAD = 128
DE = 896
EHEADS = 7
SEG = 64
NLEN = 128
NEIGH = 2
KEYS = NLEN * NEIGH
NZ = 8
NDP = 32
SEGS = 7
FEAT = D // NZ
TOK = SEGS * SEG
HALF = 8 * HEAD
SCALE = HEAD**-0.5
epsilon = 1e-05
Z = ("group", "tensor")
BF = jnp.bfloat16
F32 = jnp.float32
MIB = 1024 * 1024
KNOB = 20_000_000_000
PARAMS = pltpu.CompilerParams(vmem_limit_bytes=59 * MIB)
SMALL = pltpu.CompilerParams(vmem_limit_bytes=24 * MIB)
ROOM = pltpu.CompilerParams(vmem_limit_bytes=53 * MIB + MIB // 2)
VMEM = pl.BlockSpec(memory_space=pltpu.VMEM)
SMEM = pl.BlockSpec(memory_space=pltpu.SMEM)
ANY = pl.BlockSpec(memory_space=pl.ANY)
NT = (((1,), (1,)), ((), ()))


def dot(a, b):
    return jnp.dot(a, b, preferred_element_type=F32)


def dot_nt(a, b):
    return lax.dot_general(a, b, NT, preferred_element_type=F32)


def shift(x, by):
    return lax.ppermute(x, Z, [(i, (i + by) % NZ) for i in range(NZ)])


def tie(*arrays):
    return lax.optimization_barrier(arrays)


def exchange(x, axis):
    return lax.all_to_all(x, axis, split_axis=0, concat_axis=0, tiled=True)


def start(pairs, sem):
    copies = [pltpu.make_async_copy(a, b, sem.at[i]) for i, (a, b) in enumerate(pairs)]
    for copy in copies:
        copy.start()
    return copies


def wait(copies):
    for copy in copies:
        copy.wait()


def cost(flops, size):
    return pl.CostEstimate(flops=flops, bytes_accessed=size, transcendentals=0)


def like(x):
    return pltpu.VMEM(x.shape, x.dtype)


def encoder_queries(fetched_hbm, weight_hbm, out_hbm, fetched_ref, weight_ref, out_ref, sem):
    copies = start([(fetched_hbm, fetched_ref), (weight_hbm, weight_ref)], sem)
    copies[0].wait()
    rows = fetched_ref[...].astype(F32)
    inverse = lax.rsqrt(jnp.mean(rows * rows, axis=-1, keepdims=True) + epsilon)
    normed = (rows * inverse).astype(BF)
    copies[1].wait()
    out_ref[...] = dot(normed, weight_ref[...]).astype(BF)
    wait(start([(out_ref, out_hbm)], sem.at[pl.ds(2, 1)]))


def project(count, index_ref, *refs):
    hiddens_hbm, cots_hbm, refs = refs[:count], refs[count : 2 * count], refs[2 * count :]
    query_hbm, cond_hbm, out_hbm, acc_hbm, squares_hbm = refs[:5]
    hidden_ref, cot_ref, query_ref, cond_ref, out_weight_ref = refs[5:10]
    acc_ref, squares_ref, sem, out_sem = refs[10:]
    copies = []
    for k in range(count):
        at = pl.ds(pl.multiple_of(index_ref[k] * FEAT, FEAT), FEAT)
        copies.append(
            start(
                [
                    (hiddens_hbm[k], hidden_ref.at[k]), (query_hbm.at[at], query_ref.at[k]),
                    (cond_hbm.at[:, at], cond_ref.at[k]), (cots_hbm[k], cot_ref.at[k]),
                    (out_hbm.at[:, at], out_weight_ref.at[k]),
                ], sem.at[k],
            )
        )
    for k in range(count):
        wait(copies[k])
        chunk = hidden_ref[k]
        squares = jnp.sum(jnp.square(chunk.astype(F32)), axis=-1, keepdims=True)
        parts = (
            dot(chunk, query_ref[k]),
            dot_nt(cot_ref[k], out_weight_ref[k]),
            dot_nt(chunk, cond_ref[k]),
        )
        for columns, part in zip((slice(0, 256), slice(256, 512), slice(512, 736)), parts):
            acc_ref[:, columns] = part if k == 0 else acc_ref[:, columns] + part
        squares_ref[...] = squares if k == 0 else squares_ref[...] + squares
    wait(start([(acc_ref, acc_hbm), (squares_ref, squares_hbm)], out_sem))


def project_last(count, index_ref, *refs):
    hiddens_hbm, cots_hbm, refs = refs[:count], refs[count : 2 * count], refs[2 * count :]
    acc_hbm, squares_hbm, query_hbm, cond_hbm, out_hbm, sent_hbm, inverse_hbm = refs[:7]
    hidden_ref, cot_ref, acc_ref, squares_ref, query_ref, cond_ref, out_weight_ref = refs[7:14]
    sent_ref, inverse_ref, sem, acc_sem, out_sem = refs[14:]
    before = start([(acc_hbm, acc_ref), (squares_hbm, squares_ref)], acc_sem)
    copies = []
    for k in range(count):
        at = pl.ds(pl.multiple_of(index_ref[k] * FEAT, FEAT), FEAT)
        copies.append(
            start(
                [
                    (hiddens_hbm[k], hidden_ref.at[k]), (query_hbm.at[at], query_ref.at[k]),
                    (cond_hbm.at[:, at], cond_ref.at[k]), (cots_hbm[k], cot_ref.at[k]),
                    (out_hbm.at[:, at], out_weight_ref.at[k]),
                ], sem.at[k],
            )
        )
    wait(before)
    for k in range(count):
        wait(copies[k])
        chunk = hidden_ref[k]
        squares_ref[...] += jnp.sum(jnp.square(chunk.astype(F32)), axis=-1, keepdims=True)
        if k < count - 1:
            acc_ref[:, 0:256] += dot(chunk, query_ref[k])
            acc_ref[:, 256:512] += dot_nt(cot_ref[k], out_weight_ref[k])
            acc_ref[:, 512:736] += dot_nt(chunk, cond_ref[k])
    inverse = lax.rsqrt(squares_ref[...] / D + epsilon)
    inverse_ref[...] = inverse
    outs = start([(inverse_ref, inverse_hbm)], out_sem.at[pl.ds(0, 1)])
    k = count - 1
    queries = (acc_ref[:, :256] + dot(chunk, query_ref[k])) * inverse
    sent_ref[:SEGS, :, 0:256] = queries.astype(BF).reshape(SEGS, SEG, -1)
    grads = acc_ref[:, 256:512] + dot_nt(cot_ref[k], out_weight_ref[k])
    sent_ref[:SEGS, :, 256:512] = grads.astype(BF).reshape(SEGS, SEG, -1)
    condition = (acc_ref[:, 512:736] + dot_nt(chunk, cond_ref[k])) * inverse
    sent_ref[:SEGS, :, 512:736] = condition.astype(BF).reshape(SEGS, SEG, -1)
    sent_ref[:, :, 736:] = jnp.zeros((NZ, SEG, 32), BF)
    sent_ref[SEGS, :, :736] = jnp.zeros((SEG, 736), BF)
    wait(start([(sent_ref, sent_hbm)], out_sem.at[pl.ds(1, 1)]) + outs)


def attention(
    fetched_hbm, enc_q_hbm, got_hbm, enc_out_hbm, weights_hbm, out_ref,
    fetched_ref, enc_q_ref, got_ref, enc_out_ref, kv_ref, key_ref, value_ref, mixed_ref, sem,
):
    small = start(
        [
            (got_hbm, got_ref), (enc_q_hbm, enc_q_ref),
            (fetched_hbm, fetched_ref), (enc_out_hbm, enc_out_ref),
        ], sem,
    )
    large = [
        pltpu.make_async_copy(
            weights_hbm.at[:, j, pl.ds(0, 112), :], kv_ref.at[j], sem.at[4 + j]
        )
        for j in range(2)
    ]
    for copy in large:
        copy.start()
    wait(small)
    cond_keys, cond_values = (
        jnp.concatenate([got_ref[z, :, 512:736] for z in range(n, n + 4)], axis=1)
        for n in (0, 4)
    )
    parts = [slice(h * HEAD, (h + 1) * HEAD) for h in range(EHEADS)]
    exponents = [
        jnp.exp(dot_nt(enc_q_ref[:, columns], cond_keys[:, columns]) * SCALE) for columns in parts
    ]
    weights = [(e / jnp.sum(e, axis=-1, keepdims=True)).astype(BF) for e in exponents]
    for columns, weight in zip(parts, weights):
        mixed_ref[:, columns] = dot(weight, cond_values[:, columns]).astype(BF)
    encoded = (fetched_ref[...].astype(F32) + dot(mixed_ref[...], enc_out_ref[...])).astype(BF)
    total = jnp.zeros((SEG, HEAD), F32)
    for j in range(2):
        large[j].wait()
        key_ref[j] = dot(encoded, kv_ref[j, 0:8].reshape(DE, HALF)).astype(BF)
        value_ref[j] = dot(encoded, kv_ref[j, 8:16].reshape(DE, HALF)).astype(BF)
        for group in (range(0, 4), range(4, 8)):
            queries = [got_ref[z, :, j * HEAD : (j + 1) * HEAD] for z in group]
            grads = [got_ref[z, :, (2 + j) * HEAD : (3 + j) * HEAD] for z in group]
            keys = [key_ref[j, :, z * HEAD : (z + 1) * HEAD] for z in group]
            values = [value_ref[j, :, z * HEAD : (z + 1) * HEAD] for z in group]
            exponents = [jnp.exp(dot_nt(q, k) * SCALE) for q, k in zip(queries, keys)]
            grad_probs = [dot_nt(g, v) for g, v in zip(grads, values)]
            probs = [e / jnp.sum(e, axis=-1, keepdims=True) for e in exponents]
            attended = [dot(p.astype(BF), v).astype(BF) for p, v in zip(probs, values)]
            deltas = [
                jnp.sum(g.astype(F32) * x.astype(F32), axis=-1, keepdims=True)
                for g, x in zip(grads, attended)
            ]
            grad_scores = [
                (p * (g - d) * SCALE).astype(BF) for p, g, d in zip(probs, grad_probs, deltas)
            ]
            for z, score, key, query in zip(group, grad_scores, keys, queries):
                grad_query = dot(score, key).astype(BF)
                out_ref[:, j * HALF + z * HEAD : j * HALF + (z + 1) * HEAD] = grad_query
                total = total + grad_query.astype(F32) * query.astype(F32)
    stat = jnp.sum(total, axis=-1, keepdims=True) / D
    high = stat.astype(BF)
    low = (stat - high.astype(F32)).astype(BF)
    lane = lax.broadcasted_iota(jnp.int32, (SEG, HEAD), 1)
    out_ref[:, 2 * HALF :] = jnp.where(
        lane == 0, high.astype(F32), jnp.where(lane == 1, low.astype(F32), 0.0)
    ).astype(BF)


def finish_rows(chunk_refs, hidden_ref, inverse_ref, weight_ref, source_ref, starts, out_refs, out_hbm, sem):
    rows = [c.shape[0] for c in chunk_refs]
    chunks = jnp.concatenate([c[...] for c in chunk_refs], axis=0)
    grads = sum(
        dot_nt(chunks[:, j * HALF : (j + 1) * HALF], weight_ref[j].reshape(FEAT, HALF))
        for j in range(2)
    )
    inside, copies = [], []
    for k, chunk_ref in enumerate(chunk_refs):
        source = source_ref[k]
        at = jnp.where(source < SEGS, source, 0) * SEG + starts[k]
        place = pl.ds(pl.multiple_of(at, 32), rows[k])
        grad = grads[sum(rows[:k]) : sum(rows[: k + 1])]
        tail = chunk_ref[:, 2 * HALF :].astype(F32)
        stat = tail[:, 0:1] + tail[:, 1:2]
        inverse = inverse_ref[place, :]
        out_refs[k][...] = (
            inverse * grad - hidden_ref[place, :].astype(F32) * (inverse * inverse * stat)
        ).astype(BF)
        inside.append(source < SEGS)
        copies.append(pltpu.make_async_copy(out_refs[k], out_hbm.at[place], sem.at[k]))
        pl.when(inside[k])(copies[k].start)
    for k, copy in enumerate(copies):
        pl.when(inside[k])(copy.wait)


def finish_first(
    source_ref, chunk_ref, hidden_hbm, inverse_hbm, weights_hbm,
    out_hbm, hidden_ref, inverse_ref, weight_ref, result_ref, sem, out_sem,
):
    loads = [(inverse_hbm, inverse_ref), (hidden_hbm, hidden_ref)]
    loads += [
        (weights_hbm.at[:, pl.ds(112 + 16 * j, 16), :], weight_ref.at[j]) for j in range(2)
    ]
    wait(start(loads, sem))
    finish_rows(
        [chunk_ref], hidden_ref, inverse_ref, weight_ref, source_ref, (0,), [result_ref],
        out_hbm, out_sem,
    )


def finish(starts, source_ref, *refs):
    count = len(starts)
    chunk_refs, refs = refs[:count], refs[count:]
    hidden_ref, inverse_ref, weight_ref, _, out_hbm = refs[:5]
    result_refs, sem = refs[5 : 5 + count], refs[5 + count]
    finish_rows(
        chunk_refs, hidden_ref, inverse_ref, weight_ref, source_ref, starts, result_refs,
        out_hbm, sem,
    )


def finish_call(chunks, starts, sources, held, previous):
    rows = [c.shape[0] for c in chunks]
    operands = [sources, *chunks, *held, previous]
    return pl.pallas_call(
        functools.partial(finish, starts),
        out_shape=jax.ShapeDtypeStruct((TOK, FEAT), BF),
        in_specs=[SMEM] + [VMEM] * (len(chunks) + 3) + [ANY],
        out_specs=ANY,
        scratch_shapes=[pltpu.VMEM((r, FEAT), BF) for r in rows]
        + [pltpu.SemaphoreType.DMA((len(chunks),))],
        input_output_aliases={len(operands) - 1: 0},
        compiler_params=SMALL,
        cost_estimate=cost(2 * sum(rows) * FEAT * 2048, 4_000_000),
        name="finish",
    )(*operands)


def shards(
    hidden,
    cotangent,
    query_weight,
    out_weight,
    condition_weight,
    key_value_weight,
    encoder_query,
    encoder_out,
    database,
    neighbours,
    owners,
):
    me = lax.axis_index(Z)
    mine = lax.axis_index("dp")

    owner = owners[:, 0]
    selector = owner[None, :] == jnp.arange(NDP, dtype=jnp.int32)[:, None]
    wanted = jnp.sum(selector.astype(jnp.int32)[:, :, None] * neighbours[None, :, :], axis=1)
    kv_part = lax.dynamic_slice(
        key_value_weight.reshape(2 * DE, 2 * HEAD),
        (mine // 2 * 112, mine % 2 * HEAD),
        (112, HEAD),
    )
    q_part = lax.dynamic_slice(
        query_weight.reshape(NZ, FEAT, 2 * HEAD), (0, mine * 16, 0), (NZ, 16, 2 * HEAD)
    )
    q_part = q_part.reshape(NZ, 16, 2, HEAD).transpose(0, 2, 1, 3).reshape(NZ, 32, HEAD)
    part = jnp.concatenate([jnp.broadcast_to(kv_part, (NZ, 112, HEAD)), q_part], axis=1)

    asked = exchange(wanted, "dp")
    part = exchange(part, Z)

    projections = (query_weight, condition_weight.T, out_weight)
    right = left = hidden
    grad_right = grad_left = cotangent
    index, chunks, grad_chunks = [me], [hidden], [cotangent]
    for step in range(1, 4):
        if step == 1:
            right, left = shift(right, 1), shift(left, -1)
            part, right, left = tie(part, right, left)
            chunks += [right, left]
        if step < 3:
            right, left = shift(right, 1), shift(left, -1)
        grad_right, grad_left = shift(grad_right, 1), shift(grad_left, -1)
        if step == 1:
            asked, right, left, grad_right, grad_left = tie(
                asked, right, left, grad_right, grad_left
            )
        if step < 3:
            chunks += [right, left]
        grad_chunks += [grad_right, grad_left]
        index += [(me - step) % NZ, (me + step) % NZ]
    part = part.transpose(1, 0, 2).reshape(144, HALF)
    weights = lax.all_gather(part, "dp", axis=0, tiled=True).reshape(16, 2, 144, HALF)
    returned = exchange(database[asked].reshape(NDP, NEIGH * NLEN // NZ, DE), "dp")
    chosen = returned[jnp.concatenate([owner, owner[:1]])]
    early = 5
    acc, squares = pl.pallas_call(
        functools.partial(project, early),
        out_shape=(
            jax.ShapeDtypeStruct((TOK, 768), F32),
            jax.ShapeDtypeStruct((TOK, 1), F32),
        ),
        in_specs=[SMEM] + [ANY] * (2 * early + 3),
        out_specs=(ANY, ANY),
        scratch_shapes=[
            pltpu.VMEM((early, TOK, FEAT), BF),
            pltpu.VMEM((early, TOK, FEAT), BF),
            pltpu.VMEM((early, FEAT, 256), BF),
            pltpu.VMEM((early, 224, FEAT), BF),
            pltpu.VMEM((early, 256, FEAT), BF),
            pltpu.VMEM((TOK, 768), F32),
            pltpu.VMEM((TOK, 1), F32),
            pltpu.SemaphoreType.DMA((early, 5)),
            pltpu.SemaphoreType.DMA((2,)),
        ],
        compiler_params=ROOM,
        cost_estimate=cost(2 * early * TOK * FEAT * 736, 16_000_000),
        name="project",
    )(jnp.stack(index[:early]), *chunks[:early], *grad_chunks[:early], *projections)

    right, acc = tie(right, acc)
    chunks[5] = right
    fetched = exchange(chosen, Z).reshape(KEYS, DE)
    far = (shift(right, 1), shift(grad_left, -1))
    enc_q = pl.pallas_call(
        encoder_queries,
        out_shape=jax.ShapeDtypeStruct((KEYS, DE), BF),
        in_specs=[ANY, ANY],
        out_specs=ANY,
        scratch_shapes=[
            like(fetched), like(encoder_query), like(fetched), pltpu.SemaphoreType.DMA((3,))
        ],
        compiler_params=PARAMS,
        cost_estimate=cost(2 * KEYS * DE * DE, 3_000_000),
        name="encoder_queries",
    )(fetched, encoder_query)
    hiddens, cots = (*chunks[5:], far[0]), (*grad_chunks[5:], far[1])
    index = index[5:] + [(me + 4) % NZ]
    sent, inverse = pl.pallas_call(
        functools.partial(project_last, len(hiddens)),
        out_shape=(
            jax.ShapeDtypeStruct((NZ, SEG, 768), BF),
            jax.ShapeDtypeStruct((TOK, 1), F32),
        ),
        in_specs=[SMEM] + [ANY] * (2 * len(hiddens) + 5),
        out_specs=(ANY, ANY),
        scratch_shapes=[
            pltpu.VMEM((len(hiddens), TOK, FEAT), BF),
            pltpu.VMEM((len(hiddens), TOK, FEAT), BF),
            like(acc),
            like(squares),
            pltpu.VMEM((len(hiddens), FEAT, 256), BF),
            pltpu.VMEM((len(hiddens), 224, FEAT), BF),
            pltpu.VMEM((len(hiddens), 256, FEAT), BF),
            pltpu.VMEM((NZ, SEG, 768), BF),
            like(squares),
            pltpu.SemaphoreType.DMA((len(hiddens), 5)),
            pltpu.SemaphoreType.DMA((2,)),
            pltpu.SemaphoreType.DMA((2,)),
        ],
        compiler_params=ROOM,
        cost_estimate=cost(KNOB, 4_000_000),
        name="project_last",
    )(jnp.stack(index), *hiddens, *cots, acc, squares, *projections)
    got = exchange(sent, Z)
    operands = (fetched, enc_q, got, encoder_out)
    grad_query = pl.pallas_call(
        attention,
        out_shape=jax.ShapeDtypeStruct((SEG, 2 * HALF + HEAD), BF),
        in_specs=[ANY] * 5,
        out_specs=VMEM,
        scratch_shapes=[like(x) for x in operands]
        + [
            pltpu.VMEM((2, 16, 112, HALF), BF),
            pltpu.VMEM((2, KEYS, HALF), BF),
            pltpu.VMEM((2, KEYS, HALF), BF),
            pltpu.VMEM((KEYS, DE), BF),
            pltpu.SemaphoreType.DMA((6,)),
        ],
        compiler_params=PARAMS,
        cost_estimate=cost(4_000_000_000, 12_000_000),
        name="attention",
    )(*operands, weights)

    results = (
        jax.ShapeDtypeStruct((TOK, FEAT), BF),
        jax.ShapeDtypeStruct((TOK, FEAT), BF),
        jax.ShapeDtypeStruct((TOK, 1), F32),
        jax.ShapeDtypeStruct((2, NDP, 16, HALF), BF),
    )
    out, *held = pl.pallas_call(
        finish_first,
        out_shape=results,
        in_specs=[SMEM, VMEM, ANY, ANY, ANY],
        out_specs=(ANY, VMEM, VMEM, VMEM),
        scratch_shapes=[
            pltpu.VMEM((SEG, FEAT), BF),
            pltpu.SemaphoreType.DMA((4,)),
            pltpu.SemaphoreType.DMA((1,)),
        ],
        compiler_params=pltpu.CompilerParams(vmem_limit_bytes=50 * MIB),
        cost_estimate=cost(2 * SEG * FEAT * 2048, 4_000_000),
        name="finish_first",
    )(jnp.stack([me]), grad_query, hidden, inverse, weights.reshape(NDP, 144, HALF))

    right = left = grad_query
    for step in range(1, 4):
        right, left = shift(right, 1), shift(left, -1)
        if step > 1:
            out = finish_call(*group, held, out)
        right, left, out = tie(right, left, out)
        group = [right, left], (0, 0), jnp.stack([(me - step) % NZ, (me + step) % NZ])
    far = [shift(right[: SEG // 2], 1), shift(left[SEG // 2 :], -1)]
    out = finish_call(*group, held, out)
    return finish_call(far, (0, SEG // 2), jnp.stack([(me + 4) % NZ] * 2), held, out)


def solution(mesh):
    return jax.shard_map(
        shards,
        mesh=mesh,
        in_specs=(
            P("dp", Z),
            P("dp", Z),
            P(None, Z),
            P(Z, None),
            P(None, Z),
            P(None, None, Z),
            P(),
            P(),
            P("dp", Z, None),
            P("dp", None),
            P("dp", None),
        ),
        out_specs=P("dp", Z),
        check_vma=False,
    )
```

```python
import functools

import jax
import jax.numpy as jnp
from jax import lax
from jax.experimental import pallas as pl
from jax.experimental.pallas import tpu as pltpu
from jax.sharding import PartitionSpec as P

D = 4096
HEAD = 128
DE = 896
EHEADS = 7
SEG = 64
NLEN = 128
NEIGH = 2
KEYS = NLEN * NEIGH
NZ = 8
NDP = 32
SEGS = 7
FEAT = D // NZ
TOK = SEGS * SEG
HALF = 8 * HEAD
SCALE = HEAD**-0.5
epsilon = 1e-05
Z = ("group", "tensor")
BF = jnp.bfloat16
F32 = jnp.float32
MIB = 1024 * 1024
KNOB = 20_000_000_000
PARAMS = pltpu.CompilerParams(vmem_limit_bytes=59 * MIB)
SMALL = pltpu.CompilerParams(vmem_limit_bytes=24 * MIB)
ROOM = pltpu.CompilerParams(vmem_limit_bytes=53 * MIB + MIB // 2)
VMEM = pl.BlockSpec(memory_space=pltpu.VMEM)
SMEM = pl.BlockSpec(memory_space=pltpu.SMEM)
ANY = pl.BlockSpec(memory_space=pl.ANY)
NT = (((1,), (1,)), ((), ()))


def dot(a, b):
    return jnp.dot(a, b, preferred_element_type=F32)


def dot_nt(a, b):
    return lax.dot_general(a, b, NT, preferred_element_type=F32)


def shift(x, by):
    return lax.ppermute(x, Z, [(i, (i + by) % NZ) for i in range(NZ)])


def tie(*arrays):
    return lax.optimization_barrier(arrays)


def exchange(x, axis):
    return lax.all_to_all(x, axis, split_axis=0, concat_axis=0, tiled=True)


def start(pairs, sem):
    copies = [pltpu.make_async_copy(a, b, sem.at[i]) for i, (a, b) in enumerate(pairs)]
    for copy in copies:
        copy.start()
    return copies


def wait(copies):
    for copy in copies:
        copy.wait()


def cost(flops, size):
    return pl.CostEstimate(flops=flops, bytes_accessed=size, transcendentals=0)


def like(x):
    return pltpu.VMEM(x.shape, x.dtype)


def encoder_queries(fetched_hbm, weight_hbm, out_hbm, fetched_ref, weight_ref, out_ref, sem):
    copies = start([(fetched_hbm, fetched_ref), (weight_hbm, weight_ref)], sem)
    copies[0].wait()
    rows = fetched_ref[...].astype(F32)
    inverse = lax.rsqrt(jnp.mean(rows * rows, axis=-1, keepdims=True) + epsilon)
    normed = (rows * inverse).astype(BF)
    copies[1].wait()
    out_ref[...] = dot(normed, weight_ref[...]).astype(BF)
    wait(start([(out_ref, out_hbm)], sem.at[pl.ds(2, 1)]))


def project(count, index_ref, *refs):
    hiddens_hbm, cots_hbm, refs = refs[:count], refs[count : 2 * count], refs[2 * count :]
    query_hbm, cond_hbm, out_hbm, acc_hbm, squares_hbm = refs[:5]
    hidden_ref, cot_ref, query_ref, cond_ref, out_weight_ref = refs[5:10]
    acc_ref, squares_ref, sem, out_sem = refs[10:]
    copies = []
    for k in range(count):
        at = pl.ds(pl.multiple_of(index_ref[k] * FEAT, FEAT), FEAT)
        copies.append(
            start(
                [
                    (hiddens_hbm[k], hidden_ref.at[k]), (query_hbm.at[at], query_ref.at[k]),
                    (cond_hbm.at[:, at], cond_ref.at[k]), (cots_hbm[k], cot_ref.at[k]),
                    (out_hbm.at[:, at], out_weight_ref.at[k]),
                ], sem.at[k],
            )
        )
    for k in range(count):
        wait(copies[k])
        chunk = hidden_ref[k]
        squares = jnp.sum(jnp.square(chunk.astype(F32)), axis=-1, keepdims=True)
        parts = (
            dot(chunk, query_ref[k]),
            dot_nt(cot_ref[k], out_weight_ref[k]),
            dot_nt(chunk, cond_ref[k]),
        )
        for columns, part in zip((slice(0, 256), slice(256, 512), slice(512, 736)), parts):
            acc_ref[:, columns] = part if k == 0 else acc_ref[:, columns] + part
        squares_ref[...] = squares if k == 0 else squares_ref[...] + squares
    wait(start([(acc_ref, acc_hbm), (squares_ref, squares_hbm)], out_sem))


def project_last(count, index_ref, *refs):
    hiddens_hbm, cots_hbm, refs = refs[:count], refs[count : 2 * count], refs[2 * count :]
    acc_hbm, squares_hbm, query_hbm, cond_hbm, out_hbm, sent_hbm, inverse_hbm = refs[:7]
    hidden_ref, cot_ref, acc_ref, squares_ref, query_ref, cond_ref, out_weight_ref = refs[7:14]
    sent_ref, inverse_ref, sem, acc_sem, out_sem = refs[14:]
    before = start([(acc_hbm, acc_ref), (squares_hbm, squares_ref)], acc_sem)
    copies = []
    for k in range(count):
        at = pl.ds(pl.multiple_of(index_ref[k] * FEAT, FEAT), FEAT)
        copies.append(
            start(
                [
                    (hiddens_hbm[k], hidden_ref.at[k]), (query_hbm.at[at], query_ref.at[k]),
                    (cond_hbm.at[:, at], cond_ref.at[k]), (cots_hbm[k], cot_ref.at[k]),
                    (out_hbm.at[:, at], out_weight_ref.at[k]),
                ], sem.at[k],
            )
        )
    wait(before)
    for k in range(count):
        wait(copies[k])
        chunk = hidden_ref[k]
        squares_ref[...] += jnp.sum(jnp.square(chunk.astype(F32)), axis=-1, keepdims=True)
        if k < count - 1:
            acc_ref[:, 0:256] += dot(chunk, query_ref[k])
            acc_ref[:, 256:512] += dot_nt(cot_ref[k], out_weight_ref[k])
            acc_ref[:, 512:736] += dot_nt(chunk, cond_ref[k])
    inverse = lax.rsqrt(squares_ref[...] / D + epsilon)
    inverse_ref[...] = inverse
    outs = start([(inverse_ref, inverse_hbm)], out_sem.at[pl.ds(0, 1)])
    k = count - 1
    queries = (acc_ref[:, :256] + dot(chunk, query_ref[k])) * inverse
    sent_ref[:SEGS, :, 0:256] = queries.astype(BF).reshape(SEGS, SEG, -1)
    grads = acc_ref[:, 256:512] + dot_nt(cot_ref[k], out_weight_ref[k])
    sent_ref[:SEGS, :, 256:512] = grads.astype(BF).reshape(SEGS, SEG, -1)
    condition = (acc_ref[:, 512:736] + dot_nt(chunk, cond_ref[k])) * inverse
    sent_ref[:SEGS, :, 512:736] = condition.astype(BF).reshape(SEGS, SEG, -1)
    sent_ref[:, :, 736:] = jnp.zeros((NZ, SEG, 32), BF)
    sent_ref[SEGS, :, :736] = jnp.zeros((SEG, 736), BF)
    wait(start([(sent_ref, sent_hbm)], out_sem.at[pl.ds(1, 1)]) + outs)


def attention(
    fetched_hbm, enc_q_hbm, got_hbm, enc_out_hbm, weights_hbm, out_ref,
    fetched_ref, enc_q_ref, got_ref, enc_out_ref, kv_ref, key_ref, value_ref, mixed_ref, sem,
):
    small = start(
        [
            (got_hbm, got_ref), (enc_q_hbm, enc_q_ref),
            (fetched_hbm, fetched_ref), (enc_out_hbm, enc_out_ref),
        ], sem,
    )
    large = [
        pltpu.make_async_copy(
            weights_hbm.at[:, j, pl.ds(0, 112), :], kv_ref.at[j], sem.at[4 + j]
        )
        for j in range(2)
    ]
    for copy in large:
        copy.start()
    wait(small)
    cond_keys, cond_values = (
        jnp.concatenate([got_ref[z, :, 512:736] for z in range(n, n + 4)], axis=1)
        for n in (0, 4)
    )
    parts = [slice(h * HEAD, (h + 1) * HEAD) for h in range(EHEADS)]
    exponents = [
        jnp.exp(dot_nt(enc_q_ref[:, columns], cond_keys[:, columns]) * SCALE) for columns in parts
    ]
    weights = [(e / jnp.sum(e, axis=-1, keepdims=True)).astype(BF) for e in exponents]
    for columns, weight in zip(parts, weights):
        mixed_ref[:, columns] = dot(weight, cond_values[:, columns]).astype(BF)
    encoded = (fetched_ref[...].astype(F32) + dot(mixed_ref[...], enc_out_ref[...])).astype(BF)
    total = jnp.zeros((SEG, HEAD), F32)
    for j in range(2):
        large[j].wait()
        key_ref[j] = dot(encoded, kv_ref[j, 0:8].reshape(DE, HALF)).astype(BF)
        value_ref[j] = dot(encoded, kv_ref[j, 8:16].reshape(DE, HALF)).astype(BF)
        for group in (range(0, 4), range(4, 8)):
            queries = [got_ref[z, :, j * HEAD : (j + 1) * HEAD] for z in group]
            grads = [got_ref[z, :, (2 + j) * HEAD : (3 + j) * HEAD] for z in group]
            keys = [key_ref[j, :, z * HEAD : (z + 1) * HEAD] for z in group]
            values = [value_ref[j, :, z * HEAD : (z + 1) * HEAD] for z in group]
            exponents = [jnp.exp(dot_nt(q, k) * SCALE) for q, k in zip(queries, keys)]
            grad_probs = [dot_nt(g, v) for g, v in zip(grads, values)]
            probs = [e / jnp.sum(e, axis=-1, keepdims=True) for e in exponents]
            attended = [dot(p.astype(BF), v).astype(BF) for p, v in zip(probs, values)]
            deltas = [
                jnp.sum(g.astype(F32) * x.astype(F32), axis=-1, keepdims=True)
                for g, x in zip(grads, attended)
            ]
            grad_scores = [
                (p * (g - d) * SCALE).astype(BF) for p, g, d in zip(probs, grad_probs, deltas)
            ]
            for z, score, key, query in zip(group, grad_scores, keys, queries):
                grad_query = dot(score, key).astype(BF)
                out_ref[:, j * HALF + z * HEAD : j * HALF + (z + 1) * HEAD] = grad_query
                total = total + grad_query.astype(F32) * query.astype(F32)
    stat = jnp.sum(total, axis=-1, keepdims=True) / D
    high = stat.astype(BF)
    low = (stat - high.astype(F32)).astype(BF)
    lane = lax.broadcasted_iota(jnp.int32, (SEG, HEAD), 1)
    out_ref[:, 2 * HALF :] = jnp.where(
        lane == 0, high.astype(F32), jnp.where(lane == 1, low.astype(F32), 0.0)
    ).astype(BF)


def finish_rows(chunk_refs, hidden_ref, inverse_ref, weight_ref, source_ref, starts, out_refs, out_hbm, sem):
    rows = [c.shape[0] for c in chunk_refs]
    chunks = jnp.concatenate([c[...] for c in chunk_refs], axis=0)
    grads = sum(
        dot_nt(chunks[:, j * HALF : (j + 1) * HALF], weight_ref[j].reshape(FEAT, HALF))
        for j in range(2)
    )
    inside, copies = [], []
    for k, chunk_ref in enumerate(chunk_refs):
        source = source_ref[k]
        at = jnp.where(source < SEGS, source, 0) * SEG + starts[k]
        place = pl.ds(pl.multiple_of(at, 32), rows[k])
        grad = grads[sum(rows[:k]) : sum(rows[: k + 1])]
        tail = chunk_ref[:, 2 * HALF :].astype(F32)
        stat = tail[:, 0:1] + tail[:, 1:2]
        inverse = inverse_ref[place, :]
        out_refs[k][...] = (
            inverse * grad - hidden_ref[place, :].astype(F32) * (inverse * inverse * stat)
        ).astype(BF)
        inside.append(source < SEGS)
        copies.append(pltpu.make_async_copy(out_refs[k], out_hbm.at[place], sem.at[k]))
        pl.when(inside[k])(copies[k].start)
    for k, copy in enumerate(copies):
        pl.when(inside[k])(copy.wait)


def finish_first(
    source_ref, chunk_ref, hidden_hbm, inverse_hbm, weights_hbm,
    out_hbm, hidden_ref, inverse_ref, weight_ref, result_ref, sem, out_sem,
):
    loads = [(inverse_hbm, inverse_ref), (hidden_hbm, hidden_ref)]
    loads += [
        (weights_hbm.at[:, pl.ds(112 + 16 * j, 16), :], weight_ref.at[j]) for j in range(2)
    ]
    wait(start(loads, sem))
    finish_rows(
        [chunk_ref], hidden_ref, inverse_ref, weight_ref, source_ref, (0,), [result_ref],
        out_hbm, out_sem,
    )


def finish(starts, source_ref, *refs):
    count = len(starts)
    chunk_refs, refs = refs[:count], refs[count:]
    hidden_ref, inverse_ref, weight_ref, _, out_hbm = refs[:5]
    result_refs, sem = refs[5 : 5 + count], refs[5 + count]
    finish_rows(
        chunk_refs, hidden_ref, inverse_ref, weight_ref, source_ref, starts, result_refs,
        out_hbm, sem,
    )


def finish_call(chunks, starts, sources, held, previous):
    rows = [c.shape[0] for c in chunks]
    operands = [sources, *chunks, *held, previous]
    return pl.pallas_call(
        functools.partial(finish, starts),
        out_shape=jax.ShapeDtypeStruct((TOK, FEAT), BF),
        in_specs=[SMEM] + [VMEM] * (len(chunks) + 3) + [ANY],
        out_specs=ANY,
        scratch_shapes=[pltpu.VMEM((r, FEAT), BF) for r in rows]
        + [pltpu.SemaphoreType.DMA((len(chunks),))],
        input_output_aliases={len(operands) - 1: 0},
        compiler_params=SMALL,
        cost_estimate=cost(2 * sum(rows) * FEAT * 2048, 4_000_000),
        name="finish",
    )(*operands)


def shards(
    hidden,
    cotangent,
    query_weight,
    out_weight,
    condition_weight,
    key_value_weight,
    encoder_query,
    encoder_out,
    database,
    neighbours,
    owners,
):
    me = lax.axis_index(Z)
    mine = lax.axis_index("dp")

    owner = owners[:, 0]
    selector = owner[None, :] == jnp.arange(NDP, dtype=jnp.int32)[:, None]
    wanted = jnp.sum(selector.astype(jnp.int32)[:, :, None] * neighbours[None, :, :], axis=1)
    kv_part = lax.dynamic_slice(
        key_value_weight.reshape(2 * DE, 2 * HEAD),
        (mine // 2 * 112, mine % 2 * HEAD),
        (112, HEAD),
    )
    q_part = lax.dynamic_slice(
        query_weight.reshape(NZ, FEAT, 2 * HEAD), (0, mine * 16, 0), (NZ, 16, 2 * HEAD)
    )
    q_part = q_part.reshape(NZ, 16, 2, HEAD).transpose(0, 2, 1, 3).reshape(NZ, 32, HEAD)
    part = jnp.concatenate([jnp.broadcast_to(kv_part, (NZ, 112, HEAD)), q_part], axis=1)

    asked = exchange(wanted, "dp")
    part = exchange(part, Z)

    projections = (query_weight, condition_weight.T, out_weight)
    right, left = shift(hidden, 1), shift(hidden, -1)
    asked, right, left = tie(asked, right, left)
    returned = exchange(database[asked].reshape(NDP, NEIGH * NLEN // NZ, DE), "dp")
    index, chunks, grad_chunks = [me], [hidden, right, left], [cotangent]
    grad_right = grad_left = cotangent
    for step in range(1, 4):
        if step < 3:
            right, left = shift(right, 1), shift(left, -1)
        grad_right, grad_left = shift(grad_right, 1), shift(grad_left, -1)
        if step == 2:
            part, returned, right, left, grad_right, grad_left = tie(
                part, returned, right, left, grad_right, grad_left
            )
        if step < 3:
            chunks += [right, left]
        grad_chunks += [grad_right, grad_left]
        index += [(me - step) % NZ, (me + step) % NZ]
    part = part.transpose(1, 0, 2).reshape(144, HALF)
    weights = lax.all_gather(part, "dp", axis=0, tiled=True).reshape(16, 2, 144, HALF)
    chosen = returned[jnp.concatenate([owner, owner[:1]])]
    early = 5
    acc, squares = pl.pallas_call(
        functools.partial(project, early),
        out_shape=(
            jax.ShapeDtypeStruct((TOK, 768), F32),
            jax.ShapeDtypeStruct((TOK, 1), F32),
        ),
        in_specs=[SMEM] + [ANY] * (2 * early + 3),
        out_specs=(ANY, ANY),
        scratch_shapes=[
            pltpu.VMEM((early, TOK, FEAT), BF),
            pltpu.VMEM((early, TOK, FEAT), BF),
            pltpu.VMEM((early, FEAT, 256), BF),
            pltpu.VMEM((early, 224, FEAT), BF),
            pltpu.VMEM((early, 256, FEAT), BF),
            pltpu.VMEM((TOK, 768), F32),
            pltpu.VMEM((TOK, 1), F32),
            pltpu.SemaphoreType.DMA((early, 5)),
            pltpu.SemaphoreType.DMA((2,)),
        ],
        compiler_params=ROOM,
        cost_estimate=cost(2 * early * TOK * FEAT * 736, 16_000_000),
        name="project",
    )(jnp.stack(index[:early]), *chunks[:early], *grad_chunks[:early], *projections)

    right, acc = tie(right, acc)
    chunks[5] = right
    fetched = exchange(chosen, Z).reshape(KEYS, DE)
    far = (shift(right, 1), shift(grad_left, -1))
    enc_q = pl.pallas_call(
        encoder_queries,
        out_shape=jax.ShapeDtypeStruct((KEYS, DE), BF),
        in_specs=[ANY, ANY],
        out_specs=ANY,
        scratch_shapes=[
            like(fetched), like(encoder_query), like(fetched), pltpu.SemaphoreType.DMA((3,))
        ],
        compiler_params=PARAMS,
        cost_estimate=cost(2 * KEYS * DE * DE, 3_000_000),
        name="encoder_queries",
    )(fetched, encoder_query)
    hiddens, cots = (*chunks[5:], far[0]), (*grad_chunks[5:], far[1])
    index = index[5:] + [(me + 4) % NZ]
    sent, inverse = pl.pallas_call(
        functools.partial(project_last, len(hiddens)),
        out_shape=(
            jax.ShapeDtypeStruct((NZ, SEG, 768), BF),
            jax.ShapeDtypeStruct((TOK, 1), F32),
        ),
        in_specs=[SMEM] + [ANY] * (2 * len(hiddens) + 5),
        out_specs=(ANY, ANY),
        scratch_shapes=[
            pltpu.VMEM((len(hiddens), TOK, FEAT), BF),
            pltpu.VMEM((len(hiddens), TOK, FEAT), BF),
            like(acc),
            like(squares),
            pltpu.VMEM((len(hiddens), FEAT, 256), BF),
            pltpu.VMEM((len(hiddens), 224, FEAT), BF),
            pltpu.VMEM((len(hiddens), 256, FEAT), BF),
            pltpu.VMEM((NZ, SEG, 768), BF),
            like(squares),
            pltpu.SemaphoreType.DMA((len(hiddens), 5)),
            pltpu.SemaphoreType.DMA((2,)),
            pltpu.SemaphoreType.DMA((2,)),
        ],
        compiler_params=ROOM,
        cost_estimate=cost(KNOB, 4_000_000),
        name="project_last",
    )(jnp.stack(index), *hiddens, *cots, acc, squares, *projections)
    got = exchange(sent, Z)
    operands = (fetched, enc_q, got, encoder_out)
    grad_query = pl.pallas_call(
        attention,
        out_shape=jax.ShapeDtypeStruct((SEG, 2 * HALF + HEAD), BF),
        in_specs=[ANY] * 5,
        out_specs=VMEM,
        scratch_shapes=[like(x) for x in operands]
        + [
            pltpu.VMEM((2, 16, 112, HALF), BF),
            pltpu.VMEM((2, KEYS, HALF), BF),
            pltpu.VMEM((2, KEYS, HALF), BF),
            pltpu.VMEM((KEYS, DE), BF),
            pltpu.SemaphoreType.DMA((6,)),
        ],
        compiler_params=PARAMS,
        cost_estimate=cost(4_000_000_000, 12_000_000),
        name="attention",
    )(*operands, weights)

    results = (
        jax.ShapeDtypeStruct((TOK, FEAT), BF),
        jax.ShapeDtypeStruct((TOK, FEAT), BF),
        jax.ShapeDtypeStruct((TOK, 1), F32),
        jax.ShapeDtypeStruct((2, NDP, 16, HALF), BF),
    )
    out, *held = pl.pallas_call(
        finish_first,
        out_shape=results,
        in_specs=[SMEM, VMEM, ANY, ANY, ANY],
        out_specs=(ANY, VMEM, VMEM, VMEM),
        scratch_shapes=[
            pltpu.VMEM((SEG, FEAT), BF),
            pltpu.SemaphoreType.DMA((4,)),
            pltpu.SemaphoreType.DMA((1,)),
        ],
        compiler_params=pltpu.CompilerParams(vmem_limit_bytes=50 * MIB),
        cost_estimate=cost(2 * SEG * FEAT * 2048, 4_000_000),
        name="finish_first",
    )(jnp.stack([me]), grad_query, hidden, inverse, weights.reshape(NDP, 144, HALF))

    right = left = grad_query
    for step in range(1, 4):
        right, left = shift(right, 1), shift(left, -1)
        if step > 1:
            out = finish_call(*group, held, out)
        right, left, out = tie(right, left, out)
        group = [right, left], (0, 0), jnp.stack([(me - step) % NZ, (me + step) % NZ])
    far = [shift(right[: SEG // 2], 1), shift(left[SEG // 2 :], -1)]
    out = finish_call(*group, held, out)
    return finish_call(far, (0, SEG // 2), jnp.stack([(me + 4) % NZ] * 2), held, out)


def solution(mesh):
    return jax.shard_map(
        shards,
        mesh=mesh,
        in_specs=(
            P("dp", Z),
            P("dp", Z),
            P(None, Z),
            P(Z, None),
            P(None, Z),
            P(None, None, Z),
            P(),
            P(),
            P("dp", Z, None),
            P("dp", None),
            P("dp", None),
        ),
        out_specs=P("dp", Z),
        check_vma=False,
    )
```

```python
import functools

import jax
import jax.numpy as jnp
from jax import lax
from jax.experimental import pallas as pl
from jax.experimental.pallas import tpu as pltpu
from jax.sharding import PartitionSpec as P

D = 4096
HEAD = 128
DE = 896
EHEADS = 7
SEG = 64
NLEN = 128
NEIGH = 2
KEYS = NLEN * NEIGH
NZ = 8
NDP = 32
SEGS = 7
FEAT = D // NZ
TOK = SEGS * SEG
HALF = 8 * HEAD
SCALE = HEAD**-0.5
epsilon = 1e-05
Z = ("group", "tensor")
BF = jnp.bfloat16
F32 = jnp.float32
MIB = 1024 * 1024
KNOB = 20_000_000_000
PARAMS = pltpu.CompilerParams(vmem_limit_bytes=59 * MIB)
SMALL = pltpu.CompilerParams(vmem_limit_bytes=24 * MIB)
ROOM = pltpu.CompilerParams(vmem_limit_bytes=53 * MIB + MIB // 2)
VMEM = pl.BlockSpec(memory_space=pltpu.VMEM)
SMEM = pl.BlockSpec(memory_space=pltpu.SMEM)
ANY = pl.BlockSpec(memory_space=pl.ANY)
NT = (((1,), (1,)), ((), ()))


def dot(a, b):
    return jnp.dot(a, b, preferred_element_type=F32)


def dot_nt(a, b):
    return lax.dot_general(a, b, NT, preferred_element_type=F32)


def shift(x, by):
    return lax.ppermute(x, Z, [(i, (i + by) % NZ) for i in range(NZ)])


def tie(*arrays):
    return lax.optimization_barrier(arrays)


def exchange(x, axis):
    return lax.all_to_all(x, axis, split_axis=0, concat_axis=0, tiled=True)


def start(pairs, sem):
    copies = [pltpu.make_async_copy(a, b, sem.at[i]) for i, (a, b) in enumerate(pairs)]
    for copy in copies:
        copy.start()
    return copies


def wait(copies):
    for copy in copies:
        copy.wait()


def cost(flops, size):
    return pl.CostEstimate(flops=flops, bytes_accessed=size, transcendentals=0)


def like(x):
    return pltpu.VMEM(x.shape, x.dtype)


def encoder_queries(fetched_hbm, weight_hbm, out_hbm, fetched_ref, weight_ref, out_ref, sem):
    copies = start([(fetched_hbm, fetched_ref), (weight_hbm, weight_ref)], sem)
    copies[0].wait()
    rows = fetched_ref[...].astype(F32)
    inverse = lax.rsqrt(jnp.mean(rows * rows, axis=-1, keepdims=True) + epsilon)
    normed = (rows * inverse).astype(BF)
    copies[1].wait()
    out_ref[...] = dot(normed, weight_ref[...]).astype(BF)
    wait(start([(out_ref, out_hbm)], sem.at[pl.ds(2, 1)]))


def project(count, index_ref, *refs):
    hiddens_hbm, cots_hbm, refs = refs[:count], refs[count : 2 * count], refs[2 * count :]
    query_hbm, cond_hbm, out_hbm, acc_hbm, squares_hbm = refs[:5]
    hidden_ref, cot_ref, query_ref, cond_ref, out_weight_ref = refs[5:10]
    acc_ref, squares_ref, sem, out_sem = refs[10:]
    copies = []
    for k in range(count):
        at = pl.ds(pl.multiple_of(index_ref[k] * FEAT, FEAT), FEAT)
        copies.append(
            start(
                [
                    (hiddens_hbm[k], hidden_ref.at[k]), (query_hbm.at[at], query_ref.at[k]),
                    (cond_hbm.at[:, at], cond_ref.at[k]), (cots_hbm[k], cot_ref.at[k]),
                    (out_hbm.at[:, at], out_weight_ref.at[k]),
                ], sem.at[k],
            )
        )
    for k in range(count):
        wait(copies[k])
        chunk = hidden_ref[k]
        squares = jnp.sum(jnp.square(chunk.astype(F32)), axis=-1, keepdims=True)
        parts = (
            dot(chunk, query_ref[k]),
            dot_nt(cot_ref[k], out_weight_ref[k]),
            dot_nt(chunk, cond_ref[k]),
        )
        for columns, part in zip((slice(0, 256), slice(256, 512), slice(512, 736)), parts):
            acc_ref[:, columns] = part if k == 0 else acc_ref[:, columns] + part
        squares_ref[...] = squares if k == 0 else squares_ref[...] + squares
    wait(start([(acc_ref, acc_hbm), (squares_ref, squares_hbm)], out_sem))


def project_last(count, index_ref, *refs):
    hiddens_hbm, cots_hbm, refs = refs[:count], refs[count : 2 * count], refs[2 * count :]
    acc_hbm, squares_hbm, query_hbm, cond_hbm, out_hbm, sent_hbm, inverse_hbm = refs[:7]
    hidden_ref, cot_ref, acc_ref, squares_ref, query_ref, cond_ref, out_weight_ref = refs[7:14]
    sent_ref, inverse_ref, sem, acc_sem, out_sem = refs[14:]
    before = start([(acc_hbm, acc_ref), (squares_hbm, squares_ref)], acc_sem)
    copies = []
    for k in range(count):
        at = pl.ds(pl.multiple_of(index_ref[k] * FEAT, FEAT), FEAT)
        copies.append(
            start(
                [
                    (hiddens_hbm[k], hidden_ref.at[k]), (query_hbm.at[at], query_ref.at[k]),
                    (cond_hbm.at[:, at], cond_ref.at[k]), (cots_hbm[k], cot_ref.at[k]),
                    (out_hbm.at[:, at], out_weight_ref.at[k]),
                ], sem.at[k],
            )
        )
    wait(before)
    for k in range(count):
        wait(copies[k])
        chunk = hidden_ref[k]
        squares_ref[...] += jnp.sum(jnp.square(chunk.astype(F32)), axis=-1, keepdims=True)
        if k < count - 1:
            acc_ref[:, 0:256] += dot(chunk, query_ref[k])
            acc_ref[:, 256:512] += dot_nt(cot_ref[k], out_weight_ref[k])
            acc_ref[:, 512:736] += dot_nt(chunk, cond_ref[k])
    inverse = lax.rsqrt(squares_ref[...] / D + epsilon)
    inverse_ref[...] = inverse
    outs = start([(inverse_ref, inverse_hbm)], out_sem.at[pl.ds(0, 1)])
    k = count - 1
    queries = (acc_ref[:, :256] + dot(chunk, query_ref[k])) * inverse
    sent_ref[:SEGS, :, 0:256] = queries.astype(BF).reshape(SEGS, SEG, -1)
    grads = acc_ref[:, 256:512] + dot_nt(cot_ref[k], out_weight_ref[k])
    sent_ref[:SEGS, :, 256:512] = grads.astype(BF).reshape(SEGS, SEG, -1)
    condition = (acc_ref[:, 512:736] + dot_nt(chunk, cond_ref[k])) * inverse
    sent_ref[:SEGS, :, 512:736] = condition.astype(BF).reshape(SEGS, SEG, -1)
    sent_ref[:, :, 736:] = jnp.zeros((NZ, SEG, 32), BF)
    sent_ref[SEGS, :, :736] = jnp.zeros((SEG, 736), BF)
    wait(start([(sent_ref, sent_hbm)], out_sem.at[pl.ds(1, 1)]) + outs)


def attention(
    fetched_hbm, enc_q_hbm, got_hbm, enc_out_hbm, weights_hbm, out_ref,
    fetched_ref, enc_q_ref, got_ref, enc_out_ref, kv_ref, key_ref, value_ref, mixed_ref, sem,
):
    small = start(
        [
            (got_hbm, got_ref), (enc_q_hbm, enc_q_ref),
            (fetched_hbm, fetched_ref), (enc_out_hbm, enc_out_ref),
        ], sem,
    )
    large = [
        pltpu.make_async_copy(
            weights_hbm.at[:, j, pl.ds(0, 112), :], kv_ref.at[j], sem.at[4 + j]
        )
        for j in range(2)
    ]
    for copy in large:
        copy.start()
    wait(small)
    cond_keys, cond_values = (
        jnp.concatenate([got_ref[z, :, 512:736] for z in range(n, n + 4)], axis=1)
        for n in (0, 4)
    )
    parts = [slice(h * HEAD, (h + 1) * HEAD) for h in range(EHEADS)]
    exponents = [
        jnp.exp(dot_nt(enc_q_ref[:, columns], cond_keys[:, columns]) * SCALE) for columns in parts
    ]
    weights = [(e / jnp.sum(e, axis=-1, keepdims=True)).astype(BF) for e in exponents]
    for columns, weight in zip(parts, weights):
        mixed_ref[:, columns] = dot(weight, cond_values[:, columns]).astype(BF)
    encoded = (fetched_ref[...].astype(F32) + dot(mixed_ref[...], enc_out_ref[...])).astype(BF)
    total = jnp.zeros((SEG, HEAD), F32)
    for j in range(2):
        large[j].wait()
        key_ref[j] = dot(encoded, kv_ref[j, 0:8].reshape(DE, HALF)).astype(BF)
        value_ref[j] = dot(encoded, kv_ref[j, 8:16].reshape(DE, HALF)).astype(BF)
        for group in (range(0, 4), range(4, 8)):
            queries = [got_ref[z, :, j * HEAD : (j + 1) * HEAD] for z in group]
            grads = [got_ref[z, :, (2 + j) * HEAD : (3 + j) * HEAD] for z in group]
            keys = [key_ref[j, :, z * HEAD : (z + 1) * HEAD] for z in group]
            values = [value_ref[j, :, z * HEAD : (z + 1) * HEAD] for z in group]
            exponents = [jnp.exp(dot_nt(q, k) * SCALE) for q, k in zip(queries, keys)]
            grad_probs = [dot_nt(g, v) for g, v in zip(grads, values)]
            probs = [e / jnp.sum(e, axis=-1, keepdims=True) for e in exponents]
            attended = [dot(p.astype(BF), v).astype(BF) for p, v in zip(probs, values)]
            deltas = [
                jnp.sum(g.astype(F32) * x.astype(F32), axis=-1, keepdims=True)
                for g, x in zip(grads, attended)
            ]
            grad_scores = [
                (p * (g - d) * SCALE).astype(BF) for p, g, d in zip(probs, grad_probs, deltas)
            ]
            for z, score, key, query in zip(group, grad_scores, keys, queries):
                grad_query = dot(score, key).astype(BF)
                out_ref[:, j * HALF + z * HEAD : j * HALF + (z + 1) * HEAD] = grad_query
                total = total + grad_query.astype(F32) * query.astype(F32)
    stat = jnp.sum(total, axis=-1, keepdims=True) / D
    high = stat.astype(BF)
    low = (stat - high.astype(F32)).astype(BF)
    lane = lax.broadcasted_iota(jnp.int32, (SEG, HEAD), 1)
    out_ref[:, 2 * HALF :] = jnp.where(
        lane == 0, high.astype(F32), jnp.where(lane == 1, low.astype(F32), 0.0)
    ).astype(BF)


def finish_rows(chunk_refs, hidden_ref, inverse_ref, weight_ref, source_ref, starts, out_refs, out_hbm, sem):
    rows = [c.shape[0] for c in chunk_refs]
    chunks = jnp.concatenate([c[...] for c in chunk_refs], axis=0)
    grads = sum(
        dot_nt(chunks[:, j * HALF : (j + 1) * HALF], weight_ref[j].reshape(FEAT, HALF))
        for j in range(2)
    )
    inside, copies = [], []
    for k, chunk_ref in enumerate(chunk_refs):
        source = source_ref[k]
        at = jnp.where(source < SEGS, source, 0) * SEG + starts[k]
        place = pl.ds(pl.multiple_of(at, 32), rows[k])
        grad = grads[sum(rows[:k]) : sum(rows[: k + 1])]
        tail = chunk_ref[:, 2 * HALF :].astype(F32)
        stat = tail[:, 0:1] + tail[:, 1:2]
        inverse = inverse_ref[place, :]
        out_refs[k][...] = (
            inverse * grad - hidden_ref[place, :].astype(F32) * (inverse * inverse * stat)
        ).astype(BF)
        inside.append(source < SEGS)
        copies.append(pltpu.make_async_copy(out_refs[k], out_hbm.at[place], sem.at[k]))
        pl.when(inside[k])(copies[k].start)
    for k, copy in enumerate(copies):
        pl.when(inside[k])(copy.wait)


def finish_first(
    source_ref, chunk_ref, hidden_hbm, inverse_hbm, weights_hbm,
    out_hbm, hidden_ref, inverse_ref, weight_ref, result_ref, sem, out_sem,
):
    loads = [(inverse_hbm, inverse_ref), (hidden_hbm, hidden_ref)]
    loads += [
        (weights_hbm.at[:, pl.ds(112 + 16 * j, 16), :], weight_ref.at[j]) for j in range(2)
    ]
    wait(start(loads, sem))
    finish_rows(
        [chunk_ref], hidden_ref, inverse_ref, weight_ref, source_ref, (0,), [result_ref],
        out_hbm, out_sem,
    )


def finish(starts, source_ref, *refs):
    count = len(starts)
    chunk_refs, refs = refs[:count], refs[count:]
    hidden_ref, inverse_ref, weight_ref, _, out_hbm = refs[:5]
    result_refs, sem = refs[5 : 5 + count], refs[5 + count]
    finish_rows(
        chunk_refs, hidden_ref, inverse_ref, weight_ref, source_ref, starts, result_refs,
        out_hbm, sem,
    )


def finish_call(chunks, starts, sources, held, previous):
    rows = [c.shape[0] for c in chunks]
    operands = [sources, *chunks, *held, previous]
    return pl.pallas_call(
        functools.partial(finish, starts),
        out_shape=jax.ShapeDtypeStruct((TOK, FEAT), BF),
        in_specs=[SMEM] + [VMEM] * (len(chunks) + 3) + [ANY],
        out_specs=ANY,
        scratch_shapes=[pltpu.VMEM((r, FEAT), BF) for r in rows]
        + [pltpu.SemaphoreType.DMA((len(chunks),))],
        input_output_aliases={len(operands) - 1: 0},
        compiler_params=SMALL,
        cost_estimate=cost(2 * sum(rows) * FEAT * 2048, 4_000_000),
        name="finish",
    )(*operands)


def shards(
    hidden,
    cotangent,
    query_weight,
    out_weight,
    condition_weight,
    key_value_weight,
    encoder_query,
    encoder_out,
    database,
    neighbours,
    owners,
):
    me = lax.axis_index(Z)
    mine = lax.axis_index("dp")

    owner = owners[:, 0]
    selector = owner[None, :] == jnp.arange(NDP, dtype=jnp.int32)[:, None]
    wanted = jnp.sum(selector.astype(jnp.int32)[:, :, None] * neighbours[None, :, :], axis=1)
    kv_part = lax.dynamic_slice(
        key_value_weight.reshape(2 * DE, 2 * HEAD),
        (mine // 2 * 112, mine % 2 * HEAD),
        (112, HEAD),
    )
    q_part = lax.dynamic_slice(
        query_weight.reshape(NZ, FEAT, 2 * HEAD), (0, mine * 16, 0), (NZ, 16, 2 * HEAD)
    )
    q_part = q_part.reshape(NZ, 16, 2, HEAD).transpose(0, 2, 1, 3).reshape(NZ, 32, HEAD)
    part = jnp.concatenate([jnp.broadcast_to(kv_part, (NZ, 112, HEAD)), q_part], axis=1)

    asked = exchange(wanted, "dp")
    part = exchange(part, Z)

    projections = (query_weight, condition_weight.T, out_weight)
    right = left = hidden
    grad_right = grad_left = cotangent
    index, chunks, grad_chunks = [me], [hidden], [cotangent]
    for step in range(1, 4):
        right, left = shift(right, 1), shift(left, -1)
        if step == 1:
            part, right, left = tie(part, right, left)
        grad_right, grad_left = shift(grad_right, 1), shift(grad_left, -1)
        if step == 1:
            asked, grad_right, grad_left = tie(asked, grad_right, grad_left)
        index += [(me - step) % NZ, (me + step) % NZ]
        chunks += [right, left]
        grad_chunks += [grad_right, grad_left]
    part = part.transpose(1, 0, 2).reshape(144, HALF)
    weights = lax.all_gather(part, "dp", axis=0, tiled=True).reshape(16, 2, 144, HALF)
    returned = exchange(database[asked].reshape(NDP, NEIGH * NLEN // NZ, DE), "dp")
    chosen = returned[jnp.concatenate([owner, owner[:1]])]
    early = 5
    acc, squares = pl.pallas_call(
        functools.partial(project, early),
        out_shape=(
            jax.ShapeDtypeStruct((TOK, 768), F32),
            jax.ShapeDtypeStruct((TOK, 1), F32),
        ),
        in_specs=[SMEM] + [ANY] * (2 * early + 3),
        out_specs=(ANY, ANY),
        scratch_shapes=[
            pltpu.VMEM((early, TOK, FEAT), BF),
            pltpu.VMEM((early, TOK, FEAT), BF),
            pltpu.VMEM((early, FEAT, 256), BF),
            pltpu.VMEM((early, 224, FEAT), BF),
            pltpu.VMEM((early, 256, FEAT), BF),
            pltpu.VMEM((TOK, 768), F32),
            pltpu.VMEM((TOK, 1), F32),
            pltpu.SemaphoreType.DMA((early, 5)),
            pltpu.SemaphoreType.DMA((2,)),
        ],
        compiler_params=ROOM,
        cost_estimate=cost(2 * early * TOK * FEAT * 736, 16_000_000),
        name="project",
    )(jnp.stack(index[:early]), *chunks[:early], *grad_chunks[:early], *projections)

    right, acc = tie(right, acc)
    chunks[5] = right
    fetched = exchange(chosen, Z).reshape(KEYS, DE)
    far = (shift(right, 1), shift(grad_left, -1))
    enc_q = pl.pallas_call(
        encoder_queries,
        out_shape=jax.ShapeDtypeStruct((KEYS, DE), BF),
        in_specs=[ANY, ANY],
        out_specs=ANY,
        scratch_shapes=[
            like(fetched), like(encoder_query), like(fetched), pltpu.SemaphoreType.DMA((3,))
        ],
        compiler_params=PARAMS,
        cost_estimate=cost(2 * KEYS * DE * DE, 3_000_000),
        name="encoder_queries",
    )(fetched, encoder_query)
    hiddens, cots = (*chunks[5:], far[0]), (*grad_chunks[5:], far[1])
    index = index[5:] + [(me + 4) % NZ]
    sent, inverse = pl.pallas_call(
        functools.partial(project_last, len(hiddens)),
        out_shape=(
            jax.ShapeDtypeStruct((NZ, SEG, 768), BF),
            jax.ShapeDtypeStruct((TOK, 1), F32),
        ),
        in_specs=[SMEM] + [ANY] * (2 * len(hiddens) + 5),
        out_specs=(ANY, ANY),
        scratch_shapes=[
            pltpu.VMEM((len(hiddens), TOK, FEAT), BF),
            pltpu.VMEM((len(hiddens), TOK, FEAT), BF),
            like(acc),
            like(squares),
            pltpu.VMEM((len(hiddens), FEAT, 256), BF),
            pltpu.VMEM((len(hiddens), 224, FEAT), BF),
            pltpu.VMEM((len(hiddens), 256, FEAT), BF),
            pltpu.VMEM((NZ, SEG, 768), BF),
            like(squares),
            pltpu.SemaphoreType.DMA((len(hiddens), 5)),
            pltpu.SemaphoreType.DMA((2,)),
            pltpu.SemaphoreType.DMA((2,)),
        ],
        compiler_params=ROOM,
        cost_estimate=cost(KNOB, 4_000_000),
        name="project_last",
    )(jnp.stack(index), *hiddens, *cots, acc, squares, *projections)
    got = exchange(sent, Z)
    operands = (fetched, enc_q, got, encoder_out)
    grad_query = pl.pallas_call(
        attention,
        out_shape=jax.ShapeDtypeStruct((SEG, 2 * HALF + HEAD), BF),
        in_specs=[ANY] * 5,
        out_specs=VMEM,
        scratch_shapes=[like(x) for x in operands]
        + [
            pltpu.VMEM((2, 16, 112, HALF), BF),
            pltpu.VMEM((2, KEYS, HALF), BF),
            pltpu.VMEM((2, KEYS, HALF), BF),
            pltpu.VMEM((KEYS, DE), BF),
            pltpu.SemaphoreType.DMA((6,)),
        ],
        compiler_params=PARAMS,
        cost_estimate=cost(4_000_000_000, 12_000_000),
        name="attention",
    )(*operands, weights)

    results = (
        jax.ShapeDtypeStruct((TOK, FEAT), BF),
        jax.ShapeDtypeStruct((TOK, FEAT), BF),
        jax.ShapeDtypeStruct((TOK, 1), F32),
        jax.ShapeDtypeStruct((2, NDP, 16, HALF), BF),
    )
    out, *held = pl.pallas_call(
        finish_first,
        out_shape=results,
        in_specs=[SMEM, VMEM, ANY, ANY, ANY],
        out_specs=(ANY, VMEM, VMEM, VMEM),
        scratch_shapes=[
            pltpu.VMEM((SEG, FEAT), BF),
            pltpu.SemaphoreType.DMA((4,)),
            pltpu.SemaphoreType.DMA((1,)),
        ],
        compiler_params=ROOM,
        cost_estimate=cost(2 * SEG * FEAT * 2048, 4_000_000),
        name="finish_first",
    )(jnp.stack([me]), grad_query, hidden, inverse, weights.reshape(NDP, 144, HALF))

    right = left = grad_query
    for step in range(1, 4):
        right, left = shift(right, 1), shift(left, -1)
        if step > 1:
            out = finish_call(*group, held, out)
        right, left, out = tie(right, left, out)
        group = [right, left], (0, 0), jnp.stack([(me - step) % NZ, (me + step) % NZ])
    far = [shift(right[: SEG // 2], 1), shift(left[SEG // 2 :], -1)]
    out = finish_call(*group, held, out)
    return finish_call(far, (0, SEG // 2), jnp.stack([(me + 4) % NZ] * 2), held, out)


def solution(mesh):
    return jax.shard_map(
        shards,
        mesh=mesh,
        in_specs=(
            P("dp", Z),
            P("dp", Z),
            P(None, Z),
            P(Z, None),
            P(None, Z),
            P(None, None, Z),
            P(),
            P(),
            P("dp", Z, None),
            P("dp", None),
            P("dp", None),
        ),
        out_specs=P("dp", Z),
        check_vma=False,
    )
```
